32 devices in a mesh: sect: 4 (over x, core), slab: 8 (over z, y).
Axes of the slice: x: 2, y: 2, z: 4, core: 2. Of those that a mesh axis runs over, the one named last changes fastest.
Arguments:
- density: float32 [64, 128, 128], P('slab', 'sect'), may hold values from 0.3 to 3
- velocity: float32 [3, 64, 128, 128], P(None, 'slab', 'sect'), may hold values from -4.8 to 4.8, as said below
- pressure: float32 [64, 128, 128], P('slab', 'sect'), may hold values from 0.3 to 3
- owners: int32 [128, 4, 1], P('sect'), may hold values from 0 to 7; in each aligned block of 128 rows (0 to 127, 128 to 255, ..., all dimensions but the last counted through in order) at most 32 rows name the same one
Outputs:
- new_state: float32 [5, 64, 128, 128], P(None, 'slab', 'sect')
- optical_depth: float32 [4, 8, 32, 64], P('sect', 'slab')
The draws below stay inside these ranges and needn't reach their ends.
Inputs may be any that keep to these rules, and one draw needn't show every extreme that they name: velocity components are real values within the range. `owners`: among the sightlines of one section (the aligned block of 128 rows) no index is named more than 32 times, a bound that some block reaches.
All inputs are finite; a program needn't handle non-finite values. Where the reference program divides by a largest or mean magnitude, that divisor is 1e-20 or more.
Results may differ from the reference program's by a relative error of at most 0.0001.
Values sent between devices are 32-bit elements; how exact they have to be, the bound alone decides.
No kernel may reach another device: no remote copies, remote signals or barrier semaphores. Data moves between devices by JAX's collectives and lax.ppermute only.
A program may use at most 128 MiB of HBM per device.

```python
import math
import jax
import jax.numpy as jnp
import numpy as np
from jax import lax

CY = 32
NZ = 128
STRIDE = 32
BAND = 512
NX = 64
NY = 128
LINES = 4
MOST = 32
N_SECT = 4
N_SLAB = 8


def draw_velocity(key, part):
    position = jnp.arange(NX, dtype=jnp.float32) / (NX - 1)
    scaling = 0.4 + 0.8 * position
    values = jnp.clip(jax.random.normal(key, (3, NX, NY, NZ), jnp.float32), -4.0, 4.0)
    return values * scaling[None, :, None, None]


def block_levels(key, extent, cuts, least, high):
    factor_of = 1.0
    for dim, blocks in cuts:
        draws = jax.random.uniform(jax.random.fold_in(jax.random.fold_in(key, 6), dim), (blocks,), jnp.float32, least / len(cuts), high / len(cuts))
        factor_of = factor_of * jnp.repeat(jnp.exp(draws), extent[dim] // blocks).reshape((-1,) + (1,) * (len(extent) - 1 - dim))
    return factor_of


def deal_out(key, own, number, rows, amount, top, reach, skew):
    order = jax.random.permutation(key, amount)
    packed, usual = shares(amount, rows * top, reach, skew, True), shares(amount, rows * top, reach, skew, False)
    places = jnp.arange(amount)

    def named(sizes, turn):
        used = int((sizes > 0).sum())
        fixed = max(1, used // 4)
        passed = fixed + (places - fixed + turn * (used - fixed)) % max(1, amount - fixed)
        return jnp.zeros((amount,), jnp.int32).at[order[jnp.where(places < fixed, places, passed)]].set(jnp.asarray(sizes, jnp.int32))

    sizes = jnp.where(number % 4 == 0, named(packed, number // 4), named(usual, number - number // 4 - 1))
    mixed = jax.random.permutation(jax.random.fold_in(own, 3), amount)
    source_of, sink = mixed[0:amount // 2 * 2:2], mixed[1:amount // 2 * 2:2]
    room = jnp.minimum(sizes[source_of] - 1, reach - sizes[sink]) // 2
    room = jnp.where((source_of == order[0]) | (sink == order[0]) | (sizes[sink] == 0), 0, jnp.maximum(room, 0))
    passed = jax.random.randint(jax.random.fold_in(own, 4), (amount // 2,), 0, 1 << 20) % (room + 1)
    sizes = sizes.at[source_of].add(-passed).at[sink].add(passed)
    members = jnp.searchsorted(jnp.cumsum(sizes), jnp.arange(rows * top), side="right").astype(jnp.int32)
    grid = members.reshape(top, rows).T
    grid = grid[jax.random.permutation(jax.random.fold_in(own, 1), rows)]
    turn = jax.random.randint(jax.random.fold_in(own, 2), (rows, 1), 0, top)
    return jnp.take_along_axis(grid, (jnp.arange(top)[None, :] + turn) % top, axis=1)


def shares(count, total, bound, skew, full):
    portions = [(1 << 20) // math.isqrt(standing ** skew) + 1 for standing in range(1, count + 1)]
    largest = bound if full else min(bound, max(-(-total // count), total * portions[0] // sum(portions)))
    least = 1 if total - largest >= count - 1 else 0
    holding, surplus = [largest] + [least] * (count - 1), total - largest - least * (count - 1)
    while surplus > 0:
        candidates = [i for i in range(1, count) if holding[i] < largest] or [i for i in range(1, count) if holding[i] < bound]
        mass, budget = sum([portions[i] for i in candidates]), surplus
        for i in candidates:
            more = min(bound - holding[i], max(1, budget * portions[i] // mass), surplus)
            holding[i] = holding[i] + more
            surplus = surplus - more
    return np.array(holding)


def setup_inputs(seed: int = 0) -> dict:
    key_of = jax.random.split(jax.random.key(seed), 5)
    density = jnp.clip(jnp.exp(math.log(3.0) - 2.3025851 * jax.random.uniform(key_of[0], (NX, NY, NZ), jnp.float32) ** block_levels(key_of[0], (NX, NY, NZ), ((0, 8), (1, 4)), -0.2, 0.2)), 0.3, 3.0)
    velocity = draw_velocity(jax.random.fold_in(key_of[4], 71), 0)
    pressure = jnp.clip(jnp.exp(math.log(3.0) - 2.3025851 * jax.random.uniform(key_of[2], (NX, NY, NZ), jnp.float32) ** block_levels(key_of[2], (NX, NY, NZ), ((0, 8), (1, 4)), -0.2, 0.2)), 0.3, 3.0)
    owners_keys = jax.random.split(jax.random.fold_in(key_of[3], 1), NY * LINES // (CY * LINES))
    owners_turns = jax.random.permutation(jax.random.fold_in(key_of[3], 3), NY * LINES // (CY * LINES))
    owners = jax.vmap(lambda own, number: deal_out(jax.random.fold_in(key_of[3], 2), own, number, CY * LINES, N_SLAB, 1, MOST, 2))(owners_keys, owners_turns).reshape((NY, LINES, 1))
    return dict(density=density, velocity=velocity, pressure=pressure, owners=owners)


GAMMA = 5.0 / 3.0
COURANT = 0.15
TURBULENT = 0.25
NORMALISE = 0.5641895835477563

def primitives(current):
    density = current[0]
    velocity = current[1:4] / density
    pressure = (GAMMA - 1.0) * (current[4] - 0.5 * lax.optimization_barrier(jnp.sum(current[1:4] * velocity, axis=0)))
    return (density, velocity, pressure)

def conserved(density, velocity, pressure):
    momentum = density[None] * velocity
    energy = pressure / (GAMMA - 1.0) + 0.5 * lax.optimization_barrier(jnp.sum(momentum * velocity, axis=0))
    return jnp.concatenate([density[None], momentum, energy[None]], axis=0)

def physical_flux(current, velocity, pressure, axis_dim):
    moving = velocity[axis_dim]
    pieces = [current[axis_dim + 1]]
    for component in range(3):
        summand = current[component + 1] * moving
        if component == axis_dim:
            summand = summand + pressure
        pieces.append(summand)
    pieces.append((current[4] + pressure) * moving)
    return jnp.stack(pieces, axis=0)

def face_flux(left_state, right_state, axis_dim):
    left_density, left_velocity, left_pressure = primitives(left_state)
    right_density, right_velocity, right_pressure = primitives(right_state)
    left_speed = jnp.abs(left_velocity[axis_dim]) + jnp.sqrt(GAMMA * left_pressure / left_density)
    right_speed = jnp.abs(right_velocity[axis_dim]) + jnp.sqrt(GAMMA * right_pressure / right_density)
    signal_speed = jnp.maximum(left_speed, right_speed)
    average = 0.5 * (physical_flux(left_state, left_velocity, left_pressure, axis_dim) + physical_flux(right_state, right_velocity, right_pressure, axis_dim))
    return average - 0.5 * signal_speed[None] * (right_state - left_state)

def line_inputs(current):
    density, velocity, pressure = primitives(current)
    broadening = TURBULENT + pressure / density
    return jnp.stack([density, broadening, velocity[0]], axis=0)

def line_params(fields):
    width = BAND / 64.0 * jnp.sqrt(fields[1])
    amplitude = NORMALISE * jnp.square(fields[0]) * jnp.power(fields[1], -0.7) / width
    return jnp.stack([amplitude, 1.0 / width, BAND / 8.0 * fields[2]], axis=0)

def line_depth(params):
    half_band = BAND // 2

    def add_offset(position, running):
        offset = (position - half_band).astype(jnp.float32)
        summand = params[0] * jnp.exp(-jnp.square((offset - params[2]) * params[1]))
        return running + jnp.roll(summand, position - half_band, axis=1)
    return lax.fori_loop(0, BAND, add_offset, jnp.zeros(params.shape[1:], jnp.float32))

def reference(density, velocity, pressure, owners):
    current = conserved(density, velocity, pressure)
    sound_speed = jnp.sqrt(GAMMA * pressure / density)
    fastest = jnp.max(jnp.abs(velocity) + sound_speed[None])
    time_step = COURANT / fastest
    change = jnp.zeros_like(current)
    for axis_dim in range(3):
        face_term = face_flux(current, jnp.roll(current, -1, axis=axis_dim + 1), axis_dim)
        change = change + (face_term - jnp.roll(face_term, 1, axis=axis_dim + 1))
    new_state = current - time_step * change
    fields = line_inputs(new_state[:, :, :, ::STRIDE])
    params = line_params(fields)
    columns = jnp.transpose(params, (0, 2, 3, 1)).reshape(3, NY * LINES, NX)
    skewers = line_depth(columns)
    owner_rows = owners.reshape(N_SECT, CY * LINES)
    choose = (owner_rows[:, :, None] == jnp.arange(N_SLAB, dtype=jnp.int32)[None, None, :]).astype(jnp.int32)
    ranking = lax.optimization_barrier(jnp.sum((jnp.cumsum(choose, axis=1) - choose) * choose, axis=2))
    target = owner_rows * MOST + ranking
    sections = jnp.arange(N_SECT, dtype=jnp.int32)[:, None]
    placed = jnp.zeros((N_SECT, N_SLAB * MOST, NX), jnp.float32)
    placed = placed.at[sections, target].set(skewers.reshape(N_SECT, CY * LINES, NX))
    return (new_state, placed.reshape(N_SECT, N_SLAB, MOST, NX))
```

```python
import functools
import math

import jax
import jax.numpy as jnp
from jax import lax
from jax.experimental import pallas as pl
from jax.experimental.pallas import tpu as pltpu
from jax.sharding import PartitionSpec as P

STRIDE = 32
BAND = 512

GAMMA = 5.0 / 3.0
COURANT = 0.15
TURBULENT = 0.25
NORMALISE = 0.5641895835477563

LANES = 128
ROWS = 8
FIELDS = 5

VMEM = pl.BlockSpec(memory_space=pltpu.VMEM)


def call(kernel, out_shapes, name, flops, scratch=()):
    return pl.pallas_call(
        kernel,
        out_shape=[jax.ShapeDtypeStruct(s, jnp.float32) for s in out_shapes],
        out_specs=[VMEM] * len(out_shapes),
        scratch_shapes=list(scratch),
        compiler_params=pltpu.CompilerParams(vmem_limit_bytes=24 * 1024 * 1024),
        cost_estimate=pl.CostEstimate(flops=flops, bytes_accessed=1 << 20, transcendentals=0),
        name=name,
    )


def shift(array, amount, axis):
    size = array.shape[axis]
    amount = amount % size
    return array if amount == 0 else pltpu.roll(array, amount, axis)


def derived(cell):
    r, u, v, w, p = cell
    m = (r * u, r * v, r * w)
    energy = p * (1.0 / (GAMMA - 1.0)) + 0.5 * (m[0] * u + m[1] * v + m[2] * w)
    sound = jnp.sqrt(GAMMA * p / r)
    return (r, *m, energy), sound


def flux_parts(cell, state, sound, d):
    moving = cell[1 + d]
    flux = [state[1 + d]]
    for k in range(3):
        term = state[1 + k] * moving
        flux.append(term + cell[4] if k == d else term)
    flux.append((state[4] + cell[4]) * moving)
    return (*state, *flux, jnp.abs(moving) + sound)


def face(left, right):
    speed = jnp.maximum(left[10], right[10])
    return [
        (left[5 + k] + right[5 + k]) - speed * (right[k] - left[k]) for k in range(FIELDS)
    ]


def fields_of(r_ref, v_ref, p_ref, index):
    total = r_ref.shape[0]
    first = index.start if isinstance(index, pl.Slice) else index
    out = [r_ref[index]]
    for k in range(3):
        if isinstance(index, pl.Slice):
            out.append(v_ref[pl.ds(k * total + first, index.size, index.stride)])
        else:
            out.append(v_ref[k * total + index])
    out.append(p_ref[index])
    return out


def edges_kernel(sizes, r_ref, v_ref, p_ref, x_first, x_last, y_first, y_last, top_ref):
    nx, ny, nz = sizes
    for out, x in ((x_first, 0), (x_last, nx - 1)):
        for f, value in enumerate(fields_of(r_ref, v_ref, p_ref, pl.ds(x * ny, ny))):
            out[f] = value
    for out, y in ((y_first, 0), (y_last, ny - 1)):
        for f, value in enumerate(fields_of(r_ref, v_ref, p_ref, pl.ds(y, nx, ny))):
            out[f] = value
    top = jnp.zeros((ROWS, nz), jnp.float32)
    for row in range(0, nx * ny, ROWS):
        r, u, v, w, p = fields_of(r_ref, v_ref, p_ref, pl.ds(row, ROWS))
        speed = jnp.maximum(jnp.maximum(jnp.abs(u), jnp.abs(v)), jnp.abs(w)) + jnp.sqrt(GAMMA * p / r)
        top = jnp.maximum(top, speed)
    y_first[FIELDS] = top
    y_last[FIELDS] = top
    top_ref[...] = top


def pack_kernel(sizes, geometry, n_far, r_ref, v_ref, p_ref, y_low, y_high, top_ref, owner_ref, *rest):
    nx, ny, nz = sizes
    n_owner, slots, group, width = geometry
    far, (out_ref, spread) = rest[:n_far], rest[n_far:]
    lines = nz // STRIDE
    columns = ny * lines
    step = STRIDE // ROWS
    per_owner = slots // group
    lane = lax.broadcasted_iota(jnp.int32, (nx, nz), 1)
    n_tiles = ny // ROWS
    tiles = []
    for t in range(n_tiles):
        cell = None
        for s in range(ROWS):
            rows = fields_of(r_ref, v_ref, p_ref, pl.ds(t * ROWS + s, nx, ny))
            rows = [shift(a, step * s, 1) for a in rows]
            if cell is None:
                cell = rows
            else:
                mine = (lane - step * s + 1) % STRIDE < 3
                cell = [jnp.where(mine, a, b) for a, b in zip(rows, cell)]
        tiles.append(cell)
    first = lane % STRIDE < step
    last = lane % STRIDE >= step * (ROWS - 1)
    span = step * (ROWS - 1)
    below = [shift(y_low[f], span, 1) for f in range(FIELDS)]
    above = [y_high[f] for f in range(FIELDS)]
    dense = None
    for t in range(n_tiles):
        cell = tiles[t]
        before = tiles[t - 1] if t > 0 else below
        after = tiles[t + 1] if t + 1 < n_tiles else above
        y_minus = [jnp.where(first, shift(b, -span, 1), shift(c, step, 1)) for b, c in zip(before, cell)]
        y_plus = [jnp.where(last, shift(a, span, 1), shift(c, -step, 1)) for a, c in zip(after, cell)]
        z_minus = [shift(c, 1, 1) for c in cell]
        z_plus = [shift(c, -1, 1) for c in cell]
        state, sound = derived(cell)
        total = None
        for d, minus, plus in ((1, y_minus, y_plus), (2, z_minus, z_plus)):
            here = flux_parts(cell, state, sound, d)
            low = flux_parts(minus, *derived(minus), d)
            high = flux_parts(plus, *derived(plus), d)
            change = [a - b for a, b in zip(face(here, high), face(low, here))]
            total = change if total is None else [a + b for a, b in zip(total, change)]
        values = [shift(a, t, 1) for a in [*cell, *total]]
        dense = values if dense is None else [jnp.where(lane % step == t, a, b) for a, b in zip(values, dense)]
    spread[...] = jnp.zeros_like(spread)
    for f, value in enumerate(dense):
        for h in range(group):
            spread[pl.ds(h * width + f * nx * group + h, nx, group), :] = value
    own = jnp.broadcast_to(owner_ref[...], (columns, columns))
    own_t = own.T

    def place(dim):
        at = lax.broadcasted_iota(jnp.int32, (columns, columns), dim)
        return ((at % step) * ROWS + (at // step) % ROWS) * lines + at // STRIDE

    ahead = (own == own_t) & (place(0) < place(1))
    rank = jnp.sum(jnp.where(ahead, 1.0, 0.0), axis=0, keepdims=True)
    target = owner_ref[...] * slots + rank
    row = lax.broadcasted_iota(jnp.int32, (n_owner * per_owner, columns), 0)
    chosen = []
    for h in range(group):
        slot = ((row // per_owner) * slots + h * per_owner + row % per_owner).astype(jnp.float32)
        chosen.append(jnp.where(slot == target, 1.0, 0.0))
    picked = lax.dot_general(
        jnp.concatenate(chosen, axis=1),
        jnp.concatenate([spread[pl.ds(h * width, width), :] for h in range(group)], axis=1),
        (((1,), (1,)), ((), ())),
        precision=lax.Precision.HIGHEST,
        preferred_element_type=jnp.float32,
    )
    top = jnp.maximum(jnp.maximum(top_ref[...], y_low[FIELDS]), y_high[FIELDS])
    for ref in far:
        top = jnp.maximum(top, ref[...])
    top = jnp.max(top, keepdims=True)
    out_lane = lax.broadcasted_iota(jnp.int32, picked.shape, 1)
    out_ref[...] = jnp.where(out_lane < 2 * FIELDS * nx * group, picked, top)


def change_kernel(sizes, r_ref, v_ref, p_ref, x_low, x_high, y_low, y_high, out_ref):
    nx, ny, nz = sizes
    row = lax.broadcasted_iota(jnp.int32, (ny, nz), 0)
    half = 0.5

    def layer(x):
        if x < 0:
            return [x_low[f] for f in range(FIELDS)]
        if x >= nx:
            return [x_high[f] for f in range(FIELDS)]
        return fields_of(r_ref, v_ref, p_ref, pl.ds(x * ny, ny))

    def prepared(x):
        cell = layer(x)
        state, sound = derived(cell)
        return cell, state, sound, flux_parts(cell, state, sound, 0)

    previous = prepared(-1)
    here = prepared(0)
    x_face = face(previous[3], here[3])
    for x in range(nx):
        following = prepared(x + 1)
        cell, state, sound, parts = here
        next_face = face(parts, following[3])
        total = [a - b for a, b in zip(next_face, x_face)]
        x_face = next_face
        low_cell = [y_low[f, pl.ds(x, 1), :] for f in range(FIELDS)]
        high_cell = [y_high[f, pl.ds(x, 1), :] for f in range(FIELDS)]
        low = flux_parts(low_cell, *derived(low_cell), 1)
        high = flux_parts(high_cell, *derived(high_cell), 1)
        parts = flux_parts(cell, state, sound, 1)
        plus = [jnp.where(row == ny - 1, h, shift(a, -1, 0)) for a, h in zip(parts, high)]
        after = face(parts, plus)
        edge = face(low, [a[0:1] for a in parts])
        before = [jnp.where(row == 0, e, shift(a, 1, 0)) for a, e in zip(after, edge)]
        total = [t + (a - b) for t, a, b in zip(total, after, before)]
        parts = flux_parts(cell, state, sound, 2)
        after = face(parts, [shift(a, -1, 1) for a in parts])
        total = [t + (a - shift(a, 1, 1)) for t, a in zip(total, after)]
        for f in range(FIELDS):
            out_ref[f, pl.ds(x * ny, ny), :] = half * total[f]
        here = following


def final_kernel(sizes, geometry, r_ref, v_ref, p_ref, change_ref, packed_ref, new_ref, depth_ref):
    nx, ny, nz = sizes
    n_owner, slots, group, width = geometry
    per_owner = slots // group
    part = nx * group
    length = nx * n_owner
    everything = packed_ref[...]
    lane = lax.broadcasted_iota(jnp.int32, everything.shape, 1)
    fastest = jnp.max(jnp.where(lane >= 2 * FIELDS * part, everything, 0.0), keepdims=True)
    step = COURANT / fastest
    for x in range(nx):
        state, _ = derived(fields_of(r_ref, v_ref, p_ref, pl.ds(x * ny, ny)))
        for f in range(FIELDS):
            new_ref[f, pl.ds(x * ny, ny), :] = state[f] - step * change_ref[f, pl.ds(x * ny, ny), :]
    line = []
    for f in range(2 * FIELDS):
        pieces = [
            packed_ref[pl.ds(q * per_owner, per_owner), pl.ds(f * part, part)] for q in range(n_owner)
        ]
        line.append(jnp.concatenate(pieces, axis=1))
    cell, change = line[:FIELDS], line[FIELDS:]
    taken = cell[0] > 0.0
    cell[0] = jnp.where(taken, cell[0], 1.0)
    state, sound = derived(cell)
    parts = flux_parts(cell, state, sound, 0)
    after = face(parts, [shift(a, -group, 1) for a in parts])
    change = [c + (a - shift(a, group, 1)) for c, a in zip(change, after)]
    new = [s - (0.5 * step) * c for s, c in zip(state, change)]
    density = new[0]
    pressure = (GAMMA - 1.0) * (new[4] - 0.5 * (new[1] * new[1] + new[2] * new[2] + new[3] * new[3]) / density)
    broadening = TURBULENT + pressure / density
    inverse = 1.0 / (BAND / 64.0 * jnp.sqrt(broadening))
    amplitude = NORMALISE * (density * density) * jnp.exp(-0.7 * jnp.log(broadening)) * inverse
    amplitude = jnp.where(taken, amplitude, 0.0)
    scaled = inverse * math.sqrt(math.log2(math.e))
    centre = (BAND / 8.0) * (new[1] / density)
    turns = BAND // length
    strides = [scaled * float(length * m) for m in range(turns)]

    def offset(count, running):
        e = (length - 1 - count).astype(jnp.float32) - float(BAND // 2)
        start = (e - centre) * scaled
        total = None
        for m in range(turns):
            t = start + strides[m] if m else start
            value = jnp.exp2(-(t * t))
            total = value if total is None else total + value
        return shift(running, group, 1) + amplitude * total

    running = lax.fori_loop(0, length, offset, jnp.zeros_like(amplitude), unroll=8)
    running = shift(running, -(BAND // 2) * group, 1)
    if group == 1:
        depth_ref[...] = running
    else:
        at = lax.broadcasted_iota(jnp.int32, (group * length, length), 0)
        cell_of = lax.broadcasted_iota(jnp.int32, (group * length, length), 1)
        for h in range(group):
            pick = jnp.where(at == cell_of * group + h, 1.0, 0.0)
            depth_ref[pl.ds(h * per_owner, per_owner), :] = jnp.dot(
                running, pick, precision=lax.Precision.HIGHEST, preferred_element_type=jnp.float32
            )


def around(value, axis, amount):
    count = lax.axis_size(axis)
    return lax.ppermute(value, axis, [(i, (i + amount) % count) for i in range(count)])


def body(density, velocity, pressure, owners):
    sizes = nx, ny, nz = density.shape
    n_sect, n_slab = lax.axis_size("sect"), lax.axis_size("slab")
    lines = nz // STRIDE
    columns = ny * lines
    slots = 2 * columns // n_slab
    length = nx * n_slab
    group = max(1, LANES // length)
    width = -(-(2 * FIELDS * nx * group + 1) // LANES) * LANES
    geometry = (n_slab, slots, group, width)
    gas = (
        density.reshape(nx * ny, nz),
        velocity.reshape(3 * nx * ny, nz),
        pressure.reshape(nx * ny, nz),
    )
    cells = nx * ny * nz
    x_edge, y_edge = (FIELDS, ny, nz), (FIELDS + 1, nx, nz)
    x_first, x_last, y_first, y_last, top = call(
        functools.partial(edges_kernel, sizes),
        [x_edge, x_edge, y_edge, y_edge, (ROWS, nz)],
        "edges",
        20 * cells,
    )(*gas)
    y_low = around(y_last, "sect", 1)
    y_high = around(y_first, "sect", -1)
    far = [around(top, "sect", d) for d in range(2, n_sect - 1)]
    x_low = around(x_last, "slab", 1)
    x_high = around(x_first, "slab", -1)
    order = jnp.transpose(owners.reshape(ny // ROWS, ROWS, lines), (2, 1, 0))
    owner_row = order.reshape(1, columns).astype(jnp.float32)
    (packed,) = call(
        functools.partial(pack_kernel, sizes, geometry, len(far)),
        [(n_slab * slots // group, width)],
        "pack",
        20 * cells,
        [pltpu.VMEM((group * width, columns), jnp.float32)],
    )(*gas, y_low, y_high, top, owner_row, *far)
    arrived = lax.all_to_all(packed, "slab", split_axis=0, concat_axis=0, tiled=True)
    (change,) = call(
        functools.partial(change_kernel, sizes),
        [(FIELDS, nx * ny, nz)],
        "change",
        300 * cells,
    )(*gas, x_low, x_high, y_low, y_high)
    new_state, depth = call(
        functools.partial(final_kernel, sizes, geometry),
        [(FIELDS, nx * ny, nz), (slots, length)],
        "final",
        100 * cells,
    )(*gas, change, arrived)
    return (new_state.reshape(FIELDS, nx, ny, nz), depth.reshape(1, 1, slots, length))


def solution(mesh):
    in_specs = (
        P("slab", "sect", None),
        P(None, "slab", "sect", None),
        P("slab", "sect", None),
        P("sect", None, None),
    )
    out_specs = (P(None, "slab", "sect", None), P("sect", "slab", None, None))
    return jax.shard_map(body, mesh=mesh, in_specs=in_specs, out_specs=out_specs, check_vma=False)
```

```python
import functools
import math

import jax
import jax.numpy as jnp
from jax import lax
from jax.experimental import pallas as pl
from jax.experimental.pallas import tpu as pltpu
from jax.sharding import PartitionSpec as P

STRIDE = 32
BAND = 512

GAMMA = 5.0 / 3.0
COURANT = 0.15
TURBULENT = 0.25
NORMALISE = 0.5641895835477563

LANES = 128
ROWS = 8
FIELDS = 5
UNROLL = 64

VMEM = pl.BlockSpec(memory_space=pltpu.VMEM)


HBM = pl.BlockSpec(memory_space=pltpu.HBM)


def call(kernel, out_shapes, name, flops, scratch=(), in_specs=None, out_specs=None):
    more = {} if in_specs is None else {"in_specs": in_specs}
    return pl.pallas_call(
        kernel,
        out_shape=[jax.ShapeDtypeStruct(s, jnp.float32) for s in out_shapes],
        out_specs=out_specs or [VMEM] * len(out_shapes),
        **more,
        scratch_shapes=list(scratch),
        compiler_params=pltpu.CompilerParams(vmem_limit_bytes=24 * 1024 * 1024),
        cost_estimate=pl.CostEstimate(flops=flops, bytes_accessed=1 << 20, transcendentals=0),
        name=name,
    )


def shift(array, amount, axis):
    size = array.shape[axis]
    amount = amount % size
    return array if amount == 0 else pltpu.roll(array, amount, axis)


def derived(cell):
    r, u, v, w, p = cell
    m = (r * u, r * v, r * w)
    energy = p * (1.0 / (GAMMA - 1.0)) + 0.5 * (m[0] * u + m[1] * v + m[2] * w)
    sound = jnp.sqrt(GAMMA * p / r)
    return (r, *m, energy), sound


def flux_parts(cell, state, sound, d):
    moving = cell[1 + d]
    flux = [state[1 + d]]
    for k in range(3):
        term = state[1 + k] * moving
        flux.append(term + cell[4] if k == d else term)
    flux.append((state[4] + cell[4]) * moving)
    return (*state, *flux, jnp.abs(moving) + sound)


def face(left, right):
    speed = jnp.maximum(left[10], right[10])
    return [
        (left[5 + k] + right[5 + k]) - speed * (right[k] - left[k]) for k in range(FIELDS)
    ]


def fields_of(r_ref, v_ref, p_ref, index):
    total = r_ref.shape[0]
    first = index.start if isinstance(index, pl.Slice) else index
    out = [r_ref[index]]
    for k in range(3):
        if isinstance(index, pl.Slice):
            out.append(v_ref[pl.ds(k * total + first, index.size, index.stride)])
        else:
            out.append(v_ref[k * total + index])
    out.append(p_ref[index])
    return out


def edges_kernel(sizes, r_hbm, v_hbm, p_hbm, x_first, x_last, y_first, y_last, top_ref, r_ref, v_ref, p_ref, sems):
    nx, ny, nz = sizes
    loads = [
        pltpu.make_async_copy(source, target, sems.at[i])
        for i, (source, target) in enumerate(((r_hbm, r_ref), (v_hbm, v_ref), (p_hbm, p_ref)))
    ]
    for load in loads:
        load.start()
    for load in loads:
        load.wait()
    for out, x in ((x_first, 0), (x_last, nx - 1)):
        for f, value in enumerate(fields_of(r_ref, v_ref, p_ref, pl.ds(x * ny, ny))):
            out[f] = value
    for out, y in ((y_first, 0), (y_last, ny - 1)):
        for f, value in enumerate(fields_of(r_ref, v_ref, p_ref, pl.ds(y, nx, ny))):
            out[f] = value
    top = jnp.zeros((ROWS, nz), jnp.float32)
    for row in range(0, nx * ny, ROWS):
        r, u, v, w, p = fields_of(r_ref, v_ref, p_ref, pl.ds(row, ROWS))
        speed = jnp.maximum(jnp.maximum(jnp.abs(u), jnp.abs(v)), jnp.abs(w)) + jnp.sqrt(GAMMA * p / r)
        top = jnp.maximum(top, speed)
    y_first[FIELDS] = top
    y_last[FIELDS] = top
    top_ref[...] = top


def pack_kernel(sizes, geometry, n_far, r_ref, v_ref, p_ref, y_low, y_high, top_ref, owner_ref, *rest):
    nx, ny, nz = sizes
    n_owner, slots, group, width = geometry
    far, (out_ref, spread) = rest[:n_far], rest[n_far:]
    lines = nz // STRIDE
    columns = ny * lines
    step = STRIDE // ROWS
    per_owner = slots // group
    lane = lax.broadcasted_iota(jnp.int32, (nx, nz), 1)
    n_tiles = ny // ROWS
    tiles = []
    for t in range(n_tiles):
        cell = None
        for s in range(ROWS):
            rows = fields_of(r_ref, v_ref, p_ref, pl.ds(t * ROWS + s, nx, ny))
            rows = [shift(a, step * s, 1) for a in rows]
            if cell is None:
                cell = rows
            else:
                mine = (lane - step * s + 1) % STRIDE < 3
                cell = [jnp.where(mine, a, b) for a, b in zip(rows, cell)]
        tiles.append(cell)
    first = lane % STRIDE < step
    last = lane % STRIDE >= step * (ROWS - 1)
    span = step * (ROWS - 1)
    below = [shift(y_low[f], span, 1) for f in range(FIELDS)]
    above = [y_high[f] for f in range(FIELDS)]
    dense = None
    for t in range(n_tiles):
        cell = tiles[t]
        before = tiles[t - 1] if t > 0 else below
        after = tiles[t + 1] if t + 1 < n_tiles else above
        y_minus = [jnp.where(first, shift(b, -span, 1), shift(c, step, 1)) for b, c in zip(before, cell)]
        y_plus = [jnp.where(last, shift(a, span, 1), shift(c, -step, 1)) for a, c in zip(after, cell)]
        z_minus = [shift(c, 1, 1) for c in cell]
        z_plus = [shift(c, -1, 1) for c in cell]
        state, sound = derived(cell)
        total = None
        for d, minus, plus in ((1, y_minus, y_plus), (2, z_minus, z_plus)):
            here = flux_parts(cell, state, sound, d)
            low = flux_parts(minus, *derived(minus), d)
            high = flux_parts(plus, *derived(plus), d)
            change = [a - b for a, b in zip(face(here, high), face(low, here))]
            total = change if total is None else [a + b for a, b in zip(total, change)]
        values = [shift(a, t, 1) for a in [*cell, *total]]
        dense = values if dense is None else [jnp.where(lane % step == t, a, b) for a, b in zip(values, dense)]
    spread[...] = jnp.zeros_like(spread)
    for f, value in enumerate(dense):
        for h in range(group):
            spread[pl.ds(h * width + f * nx * group + h, nx, group), :] = value
    own = jnp.broadcast_to(owner_ref[...], (columns, columns))
    own_t = own.T

    def place(dim):
        at = lax.broadcasted_iota(jnp.int32, (columns, columns), dim)
        return ((at % step) * ROWS + (at // step) % ROWS) * lines + at // STRIDE

    ahead = (own == own_t) & (place(0) < place(1))
    rank = jnp.sum(jnp.where(ahead, 1.0, 0.0), axis=0, keepdims=True)
    target = owner_ref[...] * slots + rank
    row = lax.broadcasted_iota(jnp.int32, (n_owner * per_owner, columns), 0)
    chosen = []
    for h in range(group):
        slot = ((row // per_owner) * slots + h * per_owner + row % per_owner).astype(jnp.float32)
        chosen.append(jnp.where(slot == target, 1.0, 0.0))
    picked = lax.dot_general(
        jnp.concatenate(chosen, axis=1),
        jnp.concatenate([spread[pl.ds(h * width, width), :] for h in range(group)], axis=1),
        (((1,), (1,)), ((), ())),
        precision=lax.Precision.HIGHEST,
        preferred_element_type=jnp.float32,
    )
    top = jnp.maximum(jnp.maximum(top_ref[...], y_low[FIELDS]), y_high[FIELDS])
    for ref in far:
        top = jnp.maximum(top, ref[...])
    top = jnp.max(top, keepdims=True)
    out_lane = lax.broadcasted_iota(jnp.int32, picked.shape, 1)
    out_ref[...] = jnp.where(out_lane < 2 * FIELDS * nx * group, picked, top)


def change_kernel(sizes, r_ref, v_ref, p_ref, x_low, x_high, y_low, y_high, out_ref):
    nx, ny, nz = sizes
    row = lax.broadcasted_iota(jnp.int32, (ny, nz), 0)
    half = 0.5

    def layer(x):
        if x < 0:
            return [x_low[f] for f in range(FIELDS)]
        if x >= nx:
            return [x_high[f] for f in range(FIELDS)]
        return fields_of(r_ref, v_ref, p_ref, pl.ds(x * ny, ny))

    def prepared(x):
        cell = layer(x)
        state, sound = derived(cell)
        return cell, state, sound, flux_parts(cell, state, sound, 0)

    previous = prepared(-1)
    here = prepared(0)
    x_face = face(previous[3], here[3])
    for x in range(nx):
        following = prepared(x + 1)
        cell, state, sound, parts = here
        next_face = face(parts, following[3])
        total = [a - b for a, b in zip(next_face, x_face)]
        x_face = next_face
        low_cell = [y_low[f, pl.ds(x, 1), :] for f in range(FIELDS)]
        high_cell = [y_high[f, pl.ds(x, 1), :] for f in range(FIELDS)]
        low = flux_parts(low_cell, *derived(low_cell), 1)
        high = flux_parts(high_cell, *derived(high_cell), 1)
        parts = flux_parts(cell, state, sound, 1)
        plus = [jnp.where(row == ny - 1, h, shift(a, -1, 0)) for a, h in zip(parts, high)]
        after = face(parts, plus)
        edge = face(low, [a[0:1] for a in parts])
        before = [jnp.where(row == 0, e, shift(a, 1, 0)) for a, e in zip(after, edge)]
        total = [t + (a - b) for t, a, b in zip(total, after, before)]
        parts = flux_parts(cell, state, sound, 2)
        after = face(parts, [shift(a, -1, 1) for a in parts])
        total = [t + (a - shift(a, 1, 1)) for t, a in zip(total, after)]
        for f in range(FIELDS):
            out_ref[f, pl.ds(x * ny, ny), :] = half * total[f]
        here = following


def final_kernel(sizes, geometry, r_ref, v_ref, p_ref, change_ref, packed_ref, new_hbm, depth_ref, new_ref, sem):
    nx, ny, nz = sizes
    n_owner, slots, group, width = geometry
    per_owner = slots // group
    part = nx * group
    length = nx * n_owner
    everything = packed_ref[...]
    lane = lax.broadcasted_iota(jnp.int32, everything.shape, 1)
    fastest = jnp.max(jnp.where(lane >= 2 * FIELDS * part, everything, 0.0), keepdims=True)
    step = COURANT / fastest
    for x in range(nx):
        state, _ = derived(fields_of(r_ref, v_ref, p_ref, pl.ds(x * ny, ny)))
        for f in range(FIELDS):
            new_ref[f, pl.ds(x * ny, ny), :] = state[f] - step * change_ref[f, pl.ds(x * ny, ny), :]
    writing = pltpu.make_async_copy(new_ref, new_hbm, sem)
    writing.start()
    line = []
    for f in range(2 * FIELDS):
        pieces = [
            packed_ref[pl.ds(q * per_owner, per_owner), pl.ds(f * part, part)] for q in range(n_owner)
        ]
        line.append(jnp.concatenate(pieces, axis=1))
    cell, change = line[:FIELDS], line[FIELDS:]
    taken = cell[0] > 0.0
    cell[0] = jnp.where(taken, cell[0], 1.0)
    state, sound = derived(cell)
    parts = flux_parts(cell, state, sound, 0)
    after = face(parts, [shift(a, -group, 1) for a in parts])
    change = [c + (a - shift(a, group, 1)) for c, a in zip(change, after)]
    new = [s - (0.5 * step) * c for s, c in zip(state, change)]
    density = new[0]
    pressure = (GAMMA - 1.0) * (new[4] - 0.5 * (new[1] * new[1] + new[2] * new[2] + new[3] * new[3]) / density)
    broadening = TURBULENT + pressure / density
    inverse = 1.0 / (BAND / 64.0 * jnp.sqrt(broadening))
    amplitude = NORMALISE * (density * density) * jnp.exp(-0.7 * jnp.log(broadening)) * inverse
    amplitude = jnp.where(taken, amplitude, 0.0)
    scaled = inverse * math.sqrt(math.log2(math.e))
    centre = (BAND / 8.0) * (new[1] / density)
    turns = BAND // length
    strides = [scaled * float(length * m) for m in range(turns)]

    block = min(length, UNROLL)

    def offsets(count, running):
        e = (length - block - block * count) * 1.0 - float(BAND // 2)
        for b in range(block):
            start = (e + float(b) - centre) * scaled
            total = None
            for m in range(turns):
                t = start + strides[m] if m else start
                value = jnp.exp2(-(t * t))
                total = value if total is None else total + value
            part = shift(amplitude * total, b * group, 1)
            block_sum = part if b == 0 else block_sum + part
        return block_sum if running is None else shift(running, block * group, 1) + block_sum

    if length == block:
        running = offsets(0, None)
    else:
        running = lax.fori_loop(
            0,
            length // block,
            lambda i, c: offsets(i.astype(jnp.float32), c),
            jnp.zeros_like(amplitude),
        )
    running = shift(running, -(BAND // 2) * group, 1)
    if group == 1:
        depth_ref[...] = running
    else:
        at = lax.broadcasted_iota(jnp.int32, (group * length, length), 0)
        cell_of = lax.broadcasted_iota(jnp.int32, (group * length, length), 1)
        for h in range(group):
            pick = jnp.where(at == cell_of * group + h, 1.0, 0.0)
            depth_ref[pl.ds(h * per_owner, per_owner), :] = jnp.dot(
                running, pick, precision=lax.Precision.HIGHEST, preferred_element_type=jnp.float32
            )
    writing.wait()


def around(value, axis, amount):
    count = lax.axis_size(axis)
    return lax.ppermute(value, axis, [(i, (i + amount) % count) for i in range(count)])


def body(density, velocity, pressure, owners):
    sizes = nx, ny, nz = density.shape
    n_sect, n_slab = lax.axis_size("sect"), lax.axis_size("slab")
    lines = nz // STRIDE
    columns = ny * lines
    slots = 2 * columns // n_slab
    length = nx * n_slab
    group = max(1, LANES // length)
    width = -(-(2 * FIELDS * nx * group + 1) // LANES) * LANES
    geometry = (n_slab, slots, group, width)
    gas = (
        density.reshape(nx * ny, nz),
        velocity.reshape(3 * nx * ny, nz),
        pressure.reshape(nx * ny, nz),
    )
    cells = nx * ny * nz
    x_edge, y_edge = (FIELDS, ny, nz), (FIELDS + 1, nx, nz)
    x_first, x_last, y_first, y_last, top, *gas = call(
        functools.partial(edges_kernel, sizes),
        [x_edge, x_edge, y_edge, y_edge, (ROWS, nz), *(a.shape for a in gas)],
        "edges",
        20 * cells,
        [pltpu.SemaphoreType.DMA((3,))],
        in_specs=[HBM] * 3,
    )(*(pltpu.with_memory_space_constraint(a, pltpu.HBM) for a in gas))
    y_low = around(y_last, "sect", 1)
    y_high = around(y_first, "sect", -1)
    far = [around(top, "sect", d) for d in range(2, n_sect - 1)]
    x_low = around(x_last, "slab", 1)
    x_high = around(x_first, "slab", -1)
    order = jnp.transpose(owners.reshape(ny // ROWS, ROWS, lines), (2, 1, 0))
    owner_row = order.reshape(1, columns).astype(jnp.float32)
    (packed,) = call(
        functools.partial(pack_kernel, sizes, geometry, len(far)),
        [(n_slab * slots // group, width)],
        "pack",
        20 * cells,
        [pltpu.VMEM((group * width, columns), jnp.float32)],
    )(*gas, y_low, y_high, top, owner_row, *far)
    arrived = lax.all_to_all(packed, "slab", split_axis=0, concat_axis=0, tiled=True)
    (change,) = call(
        functools.partial(change_kernel, sizes),
        [(FIELDS, nx * ny, nz)],
        "change",
        300_000 * cells,
    )(*gas, x_low, x_high, y_low, y_high)
    new_state, depth = call(
        functools.partial(final_kernel, sizes, geometry),
        [(FIELDS, nx * ny, nz), (slots, length)],
        "final",
        100 * cells,
        [pltpu.VMEM((FIELDS, nx * ny, nz), jnp.float32), pltpu.SemaphoreType.DMA],
        out_specs=[HBM, VMEM],
    )(*gas, change, arrived)
    return (new_state.reshape(FIELDS, nx, ny, nz), depth.reshape(1, 1, slots, length))


def solution(mesh):
    in_specs = (
        P("slab", "sect", None),
        P(None, "slab", "sect", None),
        P("slab", "sect", None),
        P("sect", None, None),
    )
    out_specs = (P(None, "slab", "sect", None), P("sect", "slab", None, None))
    return jax.shard_map(body, mesh=mesh, in_specs=in_specs, out_specs=out_specs, check_vma=False)
```

```python
import functools
import math

import jax
import jax.numpy as jnp
from jax import lax
from jax.experimental import pallas as pl
from jax.experimental.pallas import tpu as pltpu
from jax.sharding import PartitionSpec as P

STRIDE = 32
BAND = 512

GAMMA = 5.0 / 3.0
COURANT = 0.15
TURBULENT = 0.25
NORMALISE = 0.5641895835477563

LANES = 128
ROWS = 8
FIELDS = 5
UNROLL = 64
PACK_COST = 30_000

VMEM = pl.BlockSpec(memory_space=pltpu.VMEM)


HBM = pl.BlockSpec(memory_space=pltpu.HBM)


def call(kernel, out_shapes, name, flops, scratch=(), in_specs=None, out_specs=None):
    more = {} if in_specs is None else {"in_specs": in_specs}
    return pl.pallas_call(
        kernel,
        out_shape=[
            jax.ShapeDtypeStruct(*s) if isinstance(s[0], tuple) else jax.ShapeDtypeStruct(s, jnp.float32)
            for s in out_shapes
        ],
        out_specs=out_specs or [VMEM] * len(out_shapes),
        **more,
        scratch_shapes=list(scratch),
        compiler_params=pltpu.CompilerParams(vmem_limit_bytes=24 * 1024 * 1024),
        cost_estimate=pl.CostEstimate(flops=flops, bytes_accessed=1 << 20, transcendentals=0),
        name=name,
    )


def shift(array, amount, axis):
    size = array.shape[axis]
    amount = amount % size
    return array if amount == 0 else pltpu.roll(array, amount, axis)


def derived(cell):
    r, u, v, w, p = cell
    m = (r * u, r * v, r * w)
    energy = p * (1.0 / (GAMMA - 1.0)) + 0.5 * (m[0] * u + m[1] * v + m[2] * w)
    sound = jnp.sqrt(GAMMA * p / r)
    return (r, *m, energy), sound


def flux_parts(cell, state, sound, d):
    moving = cell[1 + d]
    flux = [state[1 + d]]
    for k in range(3):
        term = state[1 + k] * moving
        flux.append(term + cell[4] if k == d else term)
    flux.append((state[4] + cell[4]) * moving)
    return (*state, *flux, jnp.abs(moving) + sound)


def face(left, right):
    speed = jnp.maximum(left[10], right[10])
    return [
        (left[5 + k] + right[5 + k]) - speed * (right[k] - left[k]) for k in range(FIELDS)
    ]


def fields_of(r_ref, v_ref, p_ref, index):
    total = r_ref.shape[0]
    first = index.start if isinstance(index, pl.Slice) else index
    out = [r_ref[index]]
    for k in range(3):
        if isinstance(index, pl.Slice):
            out.append(v_ref[pl.ds(k * total + first, index.size, index.stride)])
        else:
            out.append(v_ref[k * total + index])
    out.append(p_ref[index])
    return out


def place_of(direct):
    me = lax.axis_index("slab")
    return (me // 2 if direct else 0), me % 2


def layer_of(r_ref, v_ref, p_ref, at, rows):
    total = r_ref.shape[0]
    velocity = [v_ref[pl.ds(pl.multiple_of(k * total + at, ROWS), rows)] for k in range(3)]
    return [r_ref[pl.ds(at, rows)], *velocity, p_ref[pl.ds(at, rows)]]


def is_odd(axis, shape):
    return jnp.full(shape, lax.axis_index(axis) % 2) == 1


def sides(near, far, axis):
    odd = is_odd(axis, near[0].shape)
    low = [jnp.where(odd, n, f) for n, f in zip(near, far)]
    high = [jnp.where(odd, f, n) for n, f in zip(near, far)]
    return low, high


def edges_kernel(
    sizes, r_hbm, v_hbm, p_hbm, o_hbm, x_near, x_far, y_near, y_far, top_ref, r_ref, v_ref, p_ref, o_ref, sems
):
    nx, ny, nz = sizes
    loads = [
        pltpu.make_async_copy(source, target, sems.at[i])
        for i, (source, target) in enumerate(((r_hbm, r_ref), (v_hbm, v_ref), (p_hbm, p_ref), (o_hbm, o_ref)))
    ]
    for load in loads:
        load.start()
    for load in loads:
        load.wait()
    odd = lax.axis_index("slab") % 2
    for out, end in ((x_near, 1 - odd), (x_far, odd)):
        at = pl.multiple_of(end * ((nx - 1) * ny), ROWS)
        for f, value in enumerate(layer_of(r_ref, v_ref, p_ref, at, ny)):
            out[f] = value
    first, last = (fields_of(r_ref, v_ref, p_ref, pl.ds(y, nx, ny)) for y in (0, ny - 1))
    far, near = sides(last, first, "sect")
    for f in range(FIELDS):
        y_near[f] = near[f]
        y_far[f] = far[f]
    top = jnp.zeros((ROWS, nz), jnp.float32)
    for row in range(0, nx * ny, ROWS):
        r, u, v, w, p = fields_of(r_ref, v_ref, p_ref, pl.ds(row, ROWS))
        speed = jnp.maximum(jnp.maximum(jnp.abs(u), jnp.abs(v)), jnp.abs(w)) + jnp.sqrt(GAMMA * p / r)
        top = jnp.maximum(top, speed)
    y_near[FIELDS] = top
    top_ref[...] = top


def join_kernel(y_far, top_ref, near_ref, out_ref):
    for f in range(FIELDS):
        out_ref[f] = y_far[f]
    out_ref[FIELDS] = jnp.maximum(top_ref[...], near_ref[FIELDS])


def pack_kernel(sizes, geometry, n_far, direct, r_ref, v_ref, p_ref, y_near, y_far, top_ref, owner_ref, *rest):
    nx, ny, nz = sizes
    n_owner, slots, group, width = geometry
    far, outs, spread = rest[:n_far], rest[n_far:-1], rest[-1]
    y_low, y_high = sides([y_near[f] for f in range(FIELDS)], [y_far[f] for f in range(FIELDS)], "sect")
    lines = nz // STRIDE
    columns = ny * lines
    step = STRIDE // ROWS
    per_owner = slots // group
    lane = lax.broadcasted_iota(jnp.int32, (nx, nz), 1)
    tiles = []
    for t in range(step):
        cell = None
        for s in range(ny // step):
            rows = fields_of(r_ref, v_ref, p_ref, pl.ds(step * s + t, nx, ny))
            rows = [shift(a, step * s, 1) for a in rows]
            if cell is None:
                cell = rows
            else:
                mine = (lane - step * s + 1) % STRIDE < 3
                cell = [jnp.where(mine, a, b) for a, b in zip(rows, cell)]
        tiles.append(cell)
    first = lane % STRIDE < step
    last = lane % STRIDE >= ny - step
    below = [jnp.where(first, y_low[f], shift(a, step, 1)) for f, a in enumerate(tiles[-1])]
    above = [jnp.where(last, shift(y_high[f], ny - step, 1), shift(a, -step, 1)) for f, a in enumerate(tiles[0])]
    full = [(cell, *derived(cell)) for cell in (below, *tiles, above)]
    y_parts = [flux_parts(*c, 1) for c in full]
    y_faces = [face(a, b) for a, b in zip(y_parts, y_parts[1:])]
    dense = None
    for t in range(step):
        cell, state, sound = full[t + 1]
        here = flux_parts(cell, state, sound, 2)
        after = face(here, [shift(a, -1, 1) for a in here])
        total = [
            (high - low) + (a - shift(a, 1, 1))
            for low, high, a in zip(y_faces[t], y_faces[t + 1], after)
        ]
        values = [shift(a, t, 1) for a in [*cell, *total]]
        dense = values if dense is None else [jnp.where(lane % step == t, a, b) for a, b in zip(values, dense)]
    spread[...] = jnp.zeros_like(spread)
    for f, value in enumerate(dense):
        for h in range(group):
            spread[pl.ds(h * width + f * nx * group + h, nx, group), :] = value
    owner = jnp.concatenate([owner_ref[k] for k in range(lines)], axis=1).astype(jnp.float32)
    own = jnp.broadcast_to(owner, (columns, columns))
    own_t = own.T

    def place(dim):
        at = lax.broadcasted_iota(jnp.int32, (columns, columns), dim)
        return (at % ny) * lines + at // ny

    ahead = (own == own_t) & (place(0) < place(1))
    rank = jnp.sum(jnp.where(ahead, 1.0, 0.0), axis=0, keepdims=True)
    target = owner * slots + rank
    row = lax.broadcasted_iota(jnp.int32, (n_owner * per_owner, columns), 0)
    block = row // per_owner
    z_me, y_me = place_of(direct)
    own_of = 2 * ((block // 2) ^ z_me) + ((block % 2) ^ y_me)
    chosen = []
    for h in range(group):
        slot = (own_of * slots + h * per_owner + row % per_owner).astype(jnp.float32)
        chosen.append(jnp.where(slot == target, 1.0, 0.0))
    chosen = jnp.concatenate(chosen, axis=1).astype(jnp.bfloat16)
    value = jnp.concatenate([spread[pl.ds(h * width, width), :] for h in range(group)], axis=1)
    picked = None
    for _ in range(3):
        piece = value.astype(jnp.bfloat16)
        value = value - piece.astype(jnp.float32)
        part = lax.dot_general(chosen, piece, (((1,), (1,)), ((), ())), preferred_element_type=jnp.float32)
        picked = part if picked is None else picked + part
    top = jnp.maximum(jnp.maximum(top_ref[...], y_near[FIELDS]), y_far[FIELDS])
    for ref in far:
        top = jnp.maximum(top, ref[...])
    top = jnp.max(top, keepdims=True)
    out_lane = lax.broadcasted_iota(jnp.int32, picked.shape, 1)
    picked = jnp.where(out_lane < 2 * FIELDS * nx * group, picked, top)
    parts = width // LANES
    each = n_owner // len(outs)
    for b in range(n_owner):
        for w in range(parts):
            outs[b // each][pl.ds(((b % each) * parts + w) * per_owner, per_owner), :] = picked[
                b * per_owner : (b + 1) * per_owner, w * LANES : (w + 1) * LANES
            ]


def merge_kernel(rows, firsts, *refs):
    for first, ref in zip(firsts, refs[:-1]):
        for d in range(ref.shape[0] // (2 * rows)):
            refs[-1][pl.ds((first + d) * rows, rows), :] = ref[pl.ds((2 * d + 1) * rows, rows), :]


def change_kernel(sizes, r_ref, v_ref, p_ref, x_near, x_far, y_near, y_far, out_ref):
    nx, ny, nz = sizes
    every = range(FIELDS)
    x_low, x_high = sides([x_near[f] for f in every], [x_far[f] for f in every], "slab")
    y_low, y_high = sides([y_near[f] for f in every], [y_far[f] for f in every], "sect")
    row = lax.broadcasted_iota(jnp.int32, (ny, nz), 0)
    half = 0.5

    def layer(x):
        if x < 0:
            return [x_low[f] for f in range(FIELDS)]
        if x >= nx:
            return [x_high[f] for f in range(FIELDS)]
        return fields_of(r_ref, v_ref, p_ref, pl.ds(x * ny, ny))

    def prepared(x):
        cell = layer(x)
        state, sound = derived(cell)
        return cell, state, sound, flux_parts(cell, state, sound, 0)

    previous = prepared(-1)
    here = prepared(0)
    x_face = face(previous[3], here[3])
    for x in range(nx):
        following = prepared(x + 1)
        cell, state, sound, parts = here
        next_face = face(parts, following[3])
        total = [a - b for a, b in zip(next_face, x_face)]
        x_face = next_face
        low_cell = [y_low[f][x : x + 1] for f in range(FIELDS)]
        high_cell = [y_high[f][x : x + 1] for f in range(FIELDS)]
        low = flux_parts(low_cell, *derived(low_cell), 1)
        high = flux_parts(high_cell, *derived(high_cell), 1)
        parts = flux_parts(cell, state, sound, 1)
        plus = [jnp.where(row == ny - 1, h, shift(a, -1, 0)) for a, h in zip(parts, high)]
        after = face(parts, plus)
        edge = face(low, [a[0:1] for a in parts])
        before = [jnp.where(row == 0, e, shift(a, 1, 0)) for a, e in zip(after, edge)]
        total = [t + (a - b) for t, a, b in zip(total, after, before)]
        parts = flux_parts(cell, state, sound, 2)
        after = face(parts, [shift(a, -1, 1) for a in parts])
        total = [t + (a - shift(a, 1, 1)) for t, a in zip(total, after)]
        for f in range(FIELDS):
            out_ref[f, pl.ds(x * ny, ny), :] = half * total[f]
        here = following


def final_kernel(sizes, geometry, firsts, direct, r_ref, v_ref, p_ref, change_ref, got_ref, *rest):
    blocks, (new_hbm, depth_ref, new_ref, packed_ref, sem) = rest[: len(firsts)], rest[len(firsts) :]
    nx, ny, nz = sizes
    n_owner, slots, group, width = geometry
    per_owner = slots // group
    part = nx * group
    length = nx * n_owner
    parts = width // LANES
    rows = parts * per_owner

    z_me, y_me = place_of(direct)

    def settle(source, at, d, odd):
        owner = 2 * (d ^ z_me) + (odd ^ y_me)
        for w in range(parts):
            to = owner * per_owner
            if per_owner % ROWS == 0:
                to = pl.multiple_of(to, ROWS)
            packed_ref[pl.ds(to, per_owner), pl.ds(w * LANES, LANES)] = source[
                pl.ds(at + w * per_owner, per_owner), :
            ]

    for first, ref in zip(firsts, blocks):
        for d in range(ref.shape[0] // (2 * rows)):
            settle(ref, 2 * d * rows, first + d, 0)
    for d in range(got_ref.shape[0] // rows):
        settle(got_ref, d * rows, d, 1)
    everything = packed_ref[...]
    lane = lax.broadcasted_iota(jnp.int32, everything.shape, 1)
    fastest = jnp.max(jnp.where(lane >= 2 * FIELDS * part, everything, 0.0), keepdims=True)
    step = COURANT / fastest
    for x in range(nx):
        state, _ = derived(fields_of(r_ref, v_ref, p_ref, pl.ds(x * ny, ny)))
        for f in range(FIELDS):
            new_ref[f, pl.ds(x * ny, ny), :] = state[f] - step * change_ref[f, pl.ds(x * ny, ny), :]
    writing = pltpu.make_async_copy(new_ref, new_hbm, sem)
    writing.start()
    line = []
    for f in range(2 * FIELDS):
        pieces = [
            packed_ref[pl.ds(q * per_owner, per_owner), pl.ds(f * part, part)] for q in range(n_owner)
        ]
        line.append(jnp.concatenate(pieces, axis=1))
    cell, change = line[:FIELDS], line[FIELDS:]
    taken = cell[0] > 0.0
    cell[0] = jnp.where(taken, cell[0], 1.0)
    state, sound = derived(cell)
    parts = flux_parts(cell, state, sound, 0)
    after = face(parts, [shift(a, -group, 1) for a in parts])
    change = [c + (a - shift(a, group, 1)) for c, a in zip(change, after)]
    new = [s - (0.5 * step) * c for s, c in zip(state, change)]
    density = new[0]
    pressure = (GAMMA - 1.0) * (new[4] - 0.5 * (new[1] * new[1] + new[2] * new[2] + new[3] * new[3]) / density)
    broadening = TURBULENT + pressure / density
    inverse = 1.0 / (BAND / 64.0 * jnp.sqrt(broadening))
    amplitude = NORMALISE * (density * density) * jnp.exp(-0.7 * jnp.log(broadening)) * inverse
    amplitude = jnp.where(taken, amplitude, 0.0)
    scaled = inverse * math.sqrt(math.log2(math.e))
    centre = (BAND / 8.0) * (new[1] / density)
    turns = BAND // length
    strides = [scaled * float(length * m) for m in range(turns)]

    block = min(length, UNROLL)

    def offsets(count, running):
        e = (length - block - block * count) * 1.0 - float(BAND // 2)
        for b in range(block):
            start = (e + float(b) - centre) * scaled
            total = None
            for m in range(turns):
                t = start + strides[m] if m else start
                value = jnp.exp2(-(t * t))
                total = value if total is None else total + value
            part = shift(amplitude * total, b * group, 1)
            block_sum = part if b == 0 else block_sum + part
        return block_sum if running is None else shift(running, block * group, 1) + block_sum

    if length == block:
        running = offsets(0, None)
    else:
        running = lax.fori_loop(
            0,
            length // block,
            lambda i, c: offsets(i.astype(jnp.float32), c),
            jnp.zeros_like(amplitude),
        )
    running = shift(running, -(BAND // 2) * group, 1)
    if group == 1:
        depth_ref[...] = running
    else:
        at = lax.broadcasted_iota(jnp.int32, (group * length, length), 0)
        cell_of = lax.broadcasted_iota(jnp.int32, (group * length, length), 1)
        for h in range(group):
            pick = jnp.where(at == cell_of * group + h, 1.0, 0.0)
            depth_ref[pl.ds(h * per_owner, per_owner), :] = jnp.dot(
                running, pick, precision=lax.Precision.HIGHEST, preferred_element_type=jnp.float32
            )
    writing.wait()


def around(value, axis, amount):
    count = lax.axis_size(axis)
    return lax.ppermute(value, axis, [(i, (i + amount) % count) for i in range(count)])


def to_partner(value, axis, bits):
    return lax.ppermute(value, axis, [(i, i ^ bits) for i in range(lax.axis_size(axis))])


def to_other(value, axis):
    count = lax.axis_size(axis)
    return lax.ppermute(value, axis, [(i, (i + 2 * (i % 2) - 1) % count) for i in range(count)])


def body(density, velocity, pressure, owners):
    sizes = nx, ny, nz = density.shape
    n_sect, n_slab = lax.axis_size("sect"), lax.axis_size("slab")
    lines = nz // STRIDE
    columns = ny * lines
    slots = 2 * columns // n_slab
    length = nx * n_slab
    group = max(1, LANES // length)
    width = -(-(2 * FIELDS * nx * group + 1) // LANES) * LANES
    geometry = (n_slab, slots, group, width)
    gas = (
        density.reshape(nx * ny, nz),
        velocity.reshape(3 * nx * ny, nz),
        pressure.reshape(nx * ny, nz),
    )
    cells = nx * ny * nz
    half = n_slab // 2
    direct = half <= 4
    x_edge, y_edge, row = (FIELDS, ny, nz), (FIELDS + 1, nx, nz), (ROWS, nz)
    owners = jnp.transpose(owners, (1, 2, 0))
    shapes = [(a.shape, a.dtype) for a in (*gas, owners)]
    x_near, x_far, y_near, y_far, top, *gas, owners = call(
        functools.partial(edges_kernel, sizes),
        [x_edge, x_edge, y_edge, (FIELDS, nx, nz), row, *shapes],
        "edges",
        20 * cells,
        [pltpu.SemaphoreType.DMA((4,))],
        in_specs=[HBM] * 4,
    )(*(pltpu.with_memory_space_constraint(a, pltpu.HBM) for a in (*gas, owners)))
    y_near = to_partner(y_near, "sect", 1)
    (y_far,) = call(join_kernel, [y_edge], "join", cells)(y_far, top, y_near)
    y_far = to_other(y_far, "sect")
    far = [around(top, "sect", d) for d in range(2, n_sect - 1)] if n_sect > 4 else []
    x_near = to_partner(x_near, "slab", 1)
    x_far = to_other(x_far, "slab")
    rows = width // LANES * slots // group
    firsts = range(half) if direct else range(1)
    packed = call(
        functools.partial(pack_kernel, sizes, geometry, len(far), direct),
        [(n_slab // len(firsts) * rows, LANES)] * len(firsts),
        "pack",
        PACK_COST * cells,
        [pltpu.VMEM((group * width, columns), jnp.float32)],
    )(*gas, y_near, y_far, top, owners, *far)
    if direct:
        arrived = [to_partner(m, "slab", 2 * d) if d else m for d, m in zip(firsts, packed)]
    else:
        alike = [[2 * i + odd for i in range(half)] for odd in range(2)]
        arrived = [
            lax.all_to_all(m, "slab", split_axis=0, concat_axis=0, axis_index_groups=alike, tiled=True) for m in packed
        ]
    (merged,) = call(
        functools.partial(merge_kernel, rows, firsts[::-1]),
        [(half * rows, LANES)],
        "merge",
        cells,
    )(*arrived[::-1])
    got = to_partner(merged, "slab", 1)
    (change,) = call(
        functools.partial(change_kernel, sizes),
        [(FIELDS, nx * ny, nz)],
        "change",
        300_000 * cells,
    )(*gas, x_near, x_far, y_near, y_far)
    new_state, depth = call(
        functools.partial(final_kernel, sizes, geometry, firsts, direct),
        [(FIELDS, nx * ny, nz), (slots, length)],
        "final",
        100 * cells,
        [
            pltpu.VMEM((FIELDS, nx * ny, nz), jnp.float32),
            pltpu.VMEM((n_slab * slots // group, width), jnp.float32),
            pltpu.SemaphoreType.DMA,
        ],
        out_specs=[HBM, VMEM],
    )(*gas, change, got, *arrived)
    return (new_state.reshape(FIELDS, nx, ny, nz), depth.reshape(1, 1, slots, length))


def solution(mesh):
    in_specs = (
        P("slab", "sect", None),
        P(None, "slab", "sect", None),
        P("slab", "sect", None),
        P("sect", None, None),
    )
    out_specs = (P(None, "slab", "sect", None), P("sect", "slab", None, None))
    return jax.shard_map(body, mesh=mesh, in_specs=in_specs, out_specs=out_specs, check_vma=False)
```

```python
import functools
import math
from typing import NamedTuple

import jax
import jax.numpy as jnp
from jax import lax
from jax.experimental import pallas as pl
from jax.experimental.pallas import tpu as pltpu
from jax.sharding import PartitionSpec as P

STRIDE = 32
BAND = 512

GAMMA = 5.0 / 3.0
COURANT = 0.15
TURBULENT = 0.25
NORMALISE = 0.5641895835477563

LANES = 128
ROWS = 8
FIELDS = 5
UNROLL = 64
PACK_COST = 30_000
PREPARE_COST = 300

VMEM = pl.BlockSpec(memory_space=pltpu.VMEM)


HBM = pl.BlockSpec(memory_space=pltpu.HBM)


class Message(NamedTuple):
    owners: int
    slots: int
    group: int
    rows: int
    part: int
    main: int
    extra: int
    fold: int
    extra_rows: int
    count: int


def shape_of_message(nx, owners, slots, group):
    rows, part = slots // group, nx * group
    main = min(2 * FIELDS, LANES // part)
    extra = 2 * FIELDS - main
    fold = min(rows, LANES // (extra * part)) if extra else 1
    extra_rows = rows // fold if extra else 0
    count = 2 * rows + 2 * extra_rows + ROWS
    return Message(owners, slots, group, rows, part, main, extra, fold, extra_rows, count)


def call(kernel, out_shapes, name, flops, scratch=(), in_specs=None, out_specs=None):
    more = {} if in_specs is None else {"in_specs": in_specs}
    return pl.pallas_call(
        kernel,
        out_shape=[
            jax.ShapeDtypeStruct(*s) if isinstance(s[0], tuple) else jax.ShapeDtypeStruct(s, jnp.float32)
            for s in out_shapes
        ],
        out_specs=out_specs or [VMEM] * len(out_shapes),
        **more,
        scratch_shapes=list(scratch),
        compiler_params=pltpu.CompilerParams(vmem_limit_bytes=24 * 1024 * 1024),
        cost_estimate=pl.CostEstimate(flops=flops, bytes_accessed=1 << 20, transcendentals=0),
        name=name,
    )


def shift(array, amount, axis):
    size = array.shape[axis]
    amount = amount % size
    return array if amount == 0 else pltpu.roll(array, amount, axis)


def derived(cell):
    r, u, v, w, p = cell
    m = (r * u, r * v, r * w)
    energy = p * (1.0 / (GAMMA - 1.0)) + 0.5 * (m[0] * u + m[1] * v + m[2] * w)
    sound = jnp.sqrt(GAMMA * p / r)
    return (r, *m, energy), sound


def flux_parts(cell, state, sound, d):
    moving = cell[1 + d]
    flux = [state[1 + d]]
    for k in range(3):
        term = state[1 + k] * moving
        flux.append(term + cell[4] if k == d else term)
    flux.append((state[4] + cell[4]) * moving)
    return (*state, *flux, jnp.abs(moving) + sound)


def face(left, right):
    speed = jnp.maximum(left[10], right[10])
    return [
        (left[5 + k] + right[5 + k]) - speed * (right[k] - left[k]) for k in range(FIELDS)
    ]


def fields_of(r_ref, v_ref, p_ref, index):
    total = r_ref.shape[0]
    first = index.start if isinstance(index, pl.Slice) else index
    out = [r_ref[index]]
    for k in range(3):
        if isinstance(index, pl.Slice):
            out.append(v_ref[pl.ds(k * total + first, index.size, index.stride)])
        else:
            out.append(v_ref[k * total + index])
    out.append(p_ref[index])
    return out


def place_of(direct):
    me = lax.axis_index("slab")
    return (me // 2 if direct else 0), me % 2


def layer_of(r_ref, v_ref, p_ref, at, rows):
    total = r_ref.shape[0]
    velocity = [v_ref[pl.ds(pl.multiple_of(k * total + at, ROWS), rows)] for k in range(3)]
    return [r_ref[pl.ds(at, rows)], *velocity, p_ref[pl.ds(at, rows)]]


def is_odd(axis, shape):
    return jnp.full(shape, lax.axis_index(axis) % 2) == 1


def sides(near, far, axis):
    odd = is_odd(axis, near[0].shape)
    low = [jnp.where(odd, n, f) for n, f in zip(near, far)]
    high = [jnp.where(odd, f, n) for n, f in zip(near, far)]
    return low, high


def edges_kernel(
    sizes, r_hbm, v_hbm, p_hbm, o_hbm, x_near, x_far, y_near, y_far, top_ref, r_ref, v_ref, p_ref, o_ref, sems
):
    nx, ny, nz = sizes
    pairs = [(r_hbm, r_ref), (p_hbm, p_ref), (o_hbm, o_ref)]
    for k in range(3):
        component = pl.ds(k * nx * ny, nx * ny)
        pairs.append((v_hbm.at[component], v_ref.at[component]))
    loads = [pltpu.make_async_copy(source, target, sems.at[i]) for i, (source, target) in enumerate(pairs)]
    for load in loads:
        load.start()
    for load in loads:
        load.wait()
    odd = lax.axis_index("slab") % 2
    for out, end in ((x_near, 1 - odd), (x_far, odd)):
        at = pl.multiple_of(end * ((nx - 1) * ny), ROWS)
        for f, value in enumerate(layer_of(r_ref, v_ref, p_ref, at, ny)):
            out[f] = value
    first, last = (fields_of(r_ref, v_ref, p_ref, pl.ds(y, nx, ny)) for y in (0, ny - 1))
    far, near = sides(last, first, "sect")
    for f in range(FIELDS):
        y_near[f] = near[f]
        y_far[f] = far[f]
    top = jnp.zeros((ROWS, nz), jnp.float32)
    for row in range(0, nx * ny, ROWS):
        r, u, v, w, p = fields_of(r_ref, v_ref, p_ref, pl.ds(row, ROWS))
        speed = jnp.maximum(jnp.maximum(jnp.abs(u), jnp.abs(v)), jnp.abs(w)) + jnp.sqrt(GAMMA * p / r)
        top = jnp.maximum(top, speed)
    y_near[FIELDS] = top
    top_ref[...] = top


def join_kernel(y_far, top_ref, near_ref, target_ref, out_ref, target_out):
    for f in range(FIELDS):
        out_ref[f] = y_far[f]
    out_ref[FIELDS] = jnp.maximum(top_ref[...], near_ref[FIELDS])
    target_out[...] = target_ref[...]


def spread_rows(msg):
    return LANES + msg.extra * msg.part


def prepare_kernel(sizes, msg, r_ref, v_ref, p_ref, owner_ref, cell_ref, change_ref, target_ref):
    nx, ny, nz = sizes
    lines = nz // STRIDE
    columns = ny * lines
    step = STRIDE // ROWS
    lane = lax.broadcasted_iota(jnp.int32, (nx, nz), 1)
    for t in range(step):
        cell = None
        for s in range(ny // step):
            rows = fields_of(r_ref, v_ref, p_ref, pl.ds(step * s + t, nx, ny))
            rows = [shift(a, step * s, 1) for a in rows]
            if cell is None:
                cell = rows
            else:
                mine = (lane - step * s + 1) % STRIDE < 3
                cell = [jnp.where(mine, a, b) for a, b in zip(rows, cell)]
        here = flux_parts(cell, *derived(cell), 2)
        after = face(here, [shift(a, -1, 1) for a in here])
        for f in range(FIELDS):
            cell_ref[t, f] = cell[f]
            change_ref[t, f] = after[f] - shift(after[f], 1, 1)
    owner = jnp.concatenate([owner_ref[k] for k in range(lines)], axis=1).astype(jnp.float32)
    own = jnp.broadcast_to(owner, (columns, columns))
    own_t = own.T

    def place(dim):
        at = lax.broadcasted_iota(jnp.int32, (columns, columns), dim)
        return (at % ny) * lines + at // ny

    ahead = (own == own_t) & (place(0) < place(1))
    rank = jnp.sum(jnp.where(ahead, 1.0, 0.0), axis=0, keepdims=True)
    target_ref[...] = jnp.broadcast_to(owner * msg.slots + rank, target_ref.shape)


def pack_kernel(sizes, msg, n_far, direct, cell_ref, change_ref, target_ref, y_near, y_far, top_ref, *rest):
    nx, ny, nz = sizes
    slots, group, width = msg.slots, msg.group, spread_rows(msg)
    far, outs, spread = rest[:n_far], rest[n_far:-1], rest[-1]
    y_low, y_high = sides([y_near[f] for f in range(FIELDS)], [y_far[f] for f in range(FIELDS)], "sect")
    columns = ny * (nz // STRIDE)
    step = STRIDE // ROWS
    lane = lax.broadcasted_iota(jnp.int32, (nx, nz), 1)
    target = target_ref[0:1]
    tiles = [[cell_ref[t, f] for f in range(FIELDS)] for t in range(step)]
    first = lane % STRIDE < step
    last = lane % STRIDE >= ny - step
    below = [jnp.where(first, y_low[f], shift(a, step, 1)) for f, a in enumerate(tiles[-1])]
    above = [jnp.where(last, shift(y_high[f], ny - step, 1), shift(a, -step, 1)) for f, a in enumerate(tiles[0])]
    parts = [flux_parts(cell, *derived(cell), 1) for cell in (below, *tiles, above)]
    faces = [face(a, b) for a, b in zip(parts, parts[1:])]
    dense = None
    for t in range(step):
        total = [(high - low) + change_ref[t, f] for f, (low, high) in enumerate(zip(faces[t], faces[t + 1]))]
        values = [shift(a, t, 1) for a in [*tiles[t], *total]]
        dense = values if dense is None else [jnp.where(lane % step == t, a, b) for a, b in zip(values, dense)]
    spread[...] = jnp.zeros_like(spread)
    for f, value in enumerate(dense):
        for h in range(group):
            spread[pl.ds(h * width + f * nx * group + h, nx, group), :] = value
    z_me, y_me = place_of(direct)

    def chosen(rows, first):
        row = lax.broadcasted_iota(jnp.int32, (msg.owners * rows, columns), 0)
        block = row // rows
        own_of = 2 * ((block // 2) ^ z_me) + ((block % 2) ^ y_me)
        out = []
        for h in range(group):
            slot = (own_of * slots + h * msg.rows + first + row % rows).astype(jnp.float32)
            out.append(jnp.where(slot == target, 1.0, 0.0))
        return jnp.concatenate(out, axis=1).astype(jnp.bfloat16)

    def pieces(first, count):
        value = jnp.concatenate([spread[pl.ds(h * width + first, count), :] for h in range(group)], axis=1)
        out = []
        for _ in range(3):
            out.append(value.astype(jnp.bfloat16))
            value = value - out[-1].astype(jnp.float32)
        return out

    def pick(selection, values):
        parts = [
            lax.dot_general(selection, v, (((1,), (1,)), ((), ())), preferred_element_type=jnp.float32) for v in values
        ]
        return (parts[0] + parts[1]) + parts[2]

    per = msg.count
    each = msg.owners // len(outs)
    picked = pick(chosen(msg.rows, 0), pieces(0, LANES))
    for b in range(msg.owners):
        at = (b % each) // 2 * per + b % 2 * msg.rows
        outs[b // each][pl.ds(at, msg.rows), :] = picked[b * msg.rows : (b + 1) * msg.rows]
    if msg.extra:
        values = pieces(LANES, msg.extra * msg.part)
        rows = msg.extra_rows
        picked = jnp.concatenate([pick(chosen(rows, a * rows), values) for a in range(msg.fold)], axis=1)
        for b in range(msg.owners):
            at = (b % each) // 2 * per + 2 * msg.rows + b % 2 * rows
            outs[b // each][pl.ds(at, rows), :] = picked[b * rows : (b + 1) * rows]
    top = jnp.maximum(jnp.maximum(top_ref[...], y_near[FIELDS]), y_far[FIELDS])
    for ref in far:
        top = jnp.maximum(top, ref[...])
    for out in outs:
        for d in range(each // 2):
            out[pl.ds((d + 1) * per - ROWS, ROWS), :] = top


def merge_kernel(msg, firsts, *refs):
    out = refs[-1]
    half, top = msg.owners // 2, None
    for first, ref in zip(firsts, refs[:-1]):
        for d in range(ref.shape[0] // msg.count):
            at, to = d * msg.count, first + d
            out[pl.ds(to * msg.rows, msg.rows), :] = ref[pl.ds(at + msg.rows, msg.rows), :]
            if msg.extra:
                rows = msg.extra_rows
                out[pl.ds(half * msg.rows + to * rows, rows), :] = ref[pl.ds(at + 2 * msg.rows + rows, rows), :]
            new = ref[pl.ds(at + msg.count - ROWS, ROWS), :]
            top = new if top is None else jnp.maximum(top, new)
    out[pl.ds(half * (msg.rows + msg.extra_rows), ROWS), :] = top


def change_kernel(sizes, r_ref, v_ref, p_ref, x_far, x_near, y_near, y_far, out_ref):
    nx, ny, nz = sizes
    every = range(FIELDS)
    x_low, x_high = sides([x_near[f] for f in every], [x_far[f] for f in every], "slab")
    y_low, y_high = sides([y_near[f] for f in every], [y_far[f] for f in every], "sect")
    row = lax.broadcasted_iota(jnp.int32, (ny, nz), 0)
    half = 0.5

    def layer(x):
        if x < 0:
            return [x_low[f] for f in range(FIELDS)]
        if x >= nx:
            return [x_high[f] for f in range(FIELDS)]
        return fields_of(r_ref, v_ref, p_ref, pl.ds(x * ny, ny))

    def prepared(x):
        cell = layer(x)
        state, sound = derived(cell)
        return cell, state, sound, flux_parts(cell, state, sound, 0)

    previous = prepared(-1)
    here = prepared(0)
    x_face = face(previous[3], here[3])
    for x in range(nx):
        following = prepared(x + 1)
        cell, state, sound, parts = here
        next_face = face(parts, following[3])
        total = [a - b for a, b in zip(next_face, x_face)]
        x_face = next_face
        low_cell = [y_low[f][x : x + 1] for f in range(FIELDS)]
        high_cell = [y_high[f][x : x + 1] for f in range(FIELDS)]
        low = flux_parts(low_cell, *derived(low_cell), 1)
        high = flux_parts(high_cell, *derived(high_cell), 1)
        parts = flux_parts(cell, state, sound, 1)
        plus = [jnp.where(row == ny - 1, h, shift(a, -1, 0)) for a, h in zip(parts, high)]
        after = face(parts, plus)
        edge = face(low, [a[0:1] for a in parts])
        before = [jnp.where(row == 0, e, shift(a, 1, 0)) for a, e in zip(after, edge)]
        total = [t + (a - b) for t, a, b in zip(total, after, before)]
        parts = flux_parts(cell, state, sound, 2)
        after = face(parts, [shift(a, -1, 1) for a in parts])
        total = [t + (a - shift(a, 1, 1)) for t, a in zip(total, after)]
        for f in range(FIELDS):
            out_ref[f, pl.ds(x * ny, ny), :] = half * total[f]
        here = following


def final_kernel(sizes, msg, firsts, direct, r_ref, v_ref, p_ref, change_ref, got_ref, *rest):
    blocks = rest[: len(firsts)]
    new_hbm, depth_hbm, new_ref, depth_ref, main_ref, extra_ref, sems = rest[len(firsts) :]
    nx, ny, nz = sizes
    n_owner, group, part = msg.owners, msg.group, msg.part
    half, length = n_owner // 2, nx * n_owner
    top = got_ref[pl.ds(half * (msg.rows + msg.extra_rows), ROWS), :]
    for ref in blocks:
        for d in range(ref.shape[0] // msg.count):
            top = jnp.maximum(top, ref[pl.ds((d + 1) * msg.count - ROWS, ROWS), :])
    step = COURANT / jnp.max(top, keepdims=True)
    writes = []
    for x in range(nx):
        rows = pl.ds(x * ny, ny)
        state, _ = derived(fields_of(r_ref, v_ref, p_ref, rows))
        for f in range(FIELDS):
            new_ref[f, rows, :] = state[f] - step * change_ref[f, rows, :]
        writes.append(pltpu.make_async_copy(new_ref.at[:, rows], new_hbm.at[:, rows], sems.at[x]))
        writes[-1].start()
    z_me, y_me = place_of(direct)

    def settle(source, at, extra_at, d, odd):
        owner = 2 * (d ^ z_me) + (odd ^ y_me)
        main_ref[owner] = source[pl.ds(at, msg.rows), :]
        if msg.extra:
            extra_ref[owner] = source[pl.ds(extra_at, msg.extra_rows), :]

    for first, ref in zip(firsts, blocks):
        for d in range(ref.shape[0] // msg.count):
            settle(ref, d * msg.count, d * msg.count + 2 * msg.rows, first + d, 0)
    for d in range(half):
        settle(got_ref, d * msg.rows, half * msg.rows + d * msg.extra_rows, d, 1)
    line = []
    for f in range(msg.main):
        line.append(jnp.concatenate([main_ref[q, :, pl.ds(f * part, part)] for q in range(n_owner)], axis=1))
    for f in range(msg.extra):
        folds = []
        for a in range(msg.fold):
            at = pl.ds((a * msg.extra + f) * part, part)
            folds.append(jnp.concatenate([extra_ref[q, :, at] for q in range(n_owner)], axis=1))
        line.append(jnp.concatenate(folds, axis=0))
    cell, change = line[:FIELDS], line[FIELDS:]
    taken = cell[0] > 0.0
    cell[0] = jnp.where(taken, cell[0], 1.0)
    state, sound = derived(cell)
    parts = flux_parts(cell, state, sound, 0)
    after = face(parts, [shift(a, -group, 1) for a in parts])
    change = [c + (a - shift(a, group, 1)) for c, a in zip(change, after)]
    new = [s - (0.5 * step) * c for s, c in zip(state, change)]
    density = new[0]
    pressure = (GAMMA - 1.0) * (new[4] - 0.5 * (new[1] * new[1] + new[2] * new[2] + new[3] * new[3]) / density)
    broadening = TURBULENT + pressure / density
    inverse = 1.0 / (BAND / 64.0 * jnp.sqrt(broadening))
    amplitude = NORMALISE * (density * density) * jnp.exp(-0.7 * jnp.log(broadening)) * inverse
    amplitude = jnp.where(taken, amplitude, 0.0)
    scaled = inverse * math.sqrt(math.log2(math.e))
    centre = (BAND / 8.0) * (new[1] / density)
    turns = BAND // length
    strides = [scaled * float(length * m) for m in range(turns)]

    block = min(length, UNROLL)

    def offsets(count, running):
        e = (length - block - block * count) * 1.0 - float(BAND // 2)
        for b in range(block):
            start = (e + float(b) - centre) * scaled
            total = None
            for m in range(turns):
                t = start + strides[m] if m else start
                value = jnp.exp2(-(t * t))
                total = value if total is None else total + value
            part = shift(amplitude * total, b * group, 1)
            block_sum = part if b == 0 else block_sum + part
        return block_sum if running is None else shift(running, block * group, 1) + block_sum

    if length == block:
        running = offsets(0, None)
    else:
        running = lax.fori_loop(
            0,
            length // block,
            lambda i, c: offsets(i.astype(jnp.float32), c),
            jnp.zeros_like(amplitude),
        )
    running = shift(running, -(BAND // 2) * group, 1)
    if group == 1:
        depth_ref[...] = running
    else:
        at = lax.broadcasted_iota(jnp.int32, (group * length, length), 0)
        cell_of = lax.broadcasted_iota(jnp.int32, (group * length, length), 1)
        for h in range(group):
            pick = jnp.where(at == cell_of * group + h, 1.0, 0.0)
            depth_ref[pl.ds(h * msg.rows, msg.rows), :] = jnp.dot(
                running, pick, precision=lax.Precision.HIGHEST, preferred_element_type=jnp.float32
            )
    writes.append(pltpu.make_async_copy(depth_ref, depth_hbm, sems.at[nx]))
    writes[-1].start()
    for write in writes:
        write.wait()


def around(value, axis, amount):
    count = lax.axis_size(axis)
    return lax.ppermute(value, axis, [(i, (i + amount) % count) for i in range(count)])


def to_partner(value, axis, bits):
    return lax.ppermute(value, axis, [(i, i ^ bits) for i in range(lax.axis_size(axis))])


def to_other(value, axis):
    count = lax.axis_size(axis)
    return lax.ppermute(value, axis, [(i, (i + 2 * (i % 2) - 1) % count) for i in range(count)])


def body(density, velocity, pressure, owners):
    sizes = nx, ny, nz = density.shape
    n_sect, n_slab = lax.axis_size("sect"), lax.axis_size("slab")
    lines = nz // STRIDE
    columns = ny * lines
    slots = 2 * columns // n_slab
    length = nx * n_slab
    group = max(1, LANES // length)
    geometry = shape_of_message(nx, n_slab, slots, group)
    gas = (
        density.reshape(nx * ny, nz),
        velocity.reshape(3 * nx * ny, nz),
        pressure.reshape(nx * ny, nz),
    )
    cells = nx * ny * nz
    half = n_slab // 2
    direct = half <= 4
    x_edge, y_edge, row = (FIELDS, ny, nz), (FIELDS + 1, nx, nz), (ROWS, nz)
    owners = jnp.transpose(owners, (1, 2, 0))
    shapes = [(a.shape, a.dtype) for a in (*gas, owners)]
    x_near, x_far, y_near, y_far, top, *gas, owners = call(
        functools.partial(edges_kernel, sizes),
        [x_edge, x_edge, y_edge, (FIELDS, nx, nz), row, *shapes],
        "edges",
        20 * cells,
        [pltpu.SemaphoreType.DMA((6,))],
        in_specs=[HBM] * 4,
    )(*(pltpu.with_memory_space_constraint(a, pltpu.HBM) for a in (*gas, owners)))
    tiles = (STRIDE // ROWS, FIELDS, nx, nz)
    cells_at, change_at, target = call(
        functools.partial(prepare_kernel, sizes, geometry),
        [tiles, tiles, (ROWS, columns)],
        "prepare",
        PREPARE_COST * cells,
    )(*gas, owners)
    y_near = to_partner(y_near, "sect", 1)
    y_far, target = call(join_kernel, [y_edge, (ROWS, columns)], "join", cells)(y_far, top, y_near, target)
    y_far = to_other(y_far, "sect")
    far = [around(top, "sect", d) for d in range(2, n_sect - 1)] if n_sect > 4 else []
    x_near = to_partner(x_near, "slab", 1)
    x_far = to_other(x_far, "slab")
    firsts = range(half) if direct else range(1)
    packed = call(
        functools.partial(pack_kernel, sizes, geometry, len(far), direct),
        [(half // len(firsts) * geometry.count, LANES)] * len(firsts),
        "pack",
        PACK_COST * cells,
        [pltpu.VMEM((group * spread_rows(geometry), columns), jnp.float32)],
    )(cells_at, change_at, target, y_near, y_far, top, *far)
    if direct:
        arrived = [to_partner(m, "slab", 2 * d) if d else m for d, m in zip(firsts, packed)]
    else:
        alike = [[2 * i + odd for i in range(half)] for odd in range(2)]
        arrived = [
            lax.all_to_all(m, "slab", split_axis=0, concat_axis=0, axis_index_groups=alike, tiled=True) for m in packed
        ]
    (merged,) = call(
        functools.partial(merge_kernel, geometry, firsts[::-1]),
        [(half * (geometry.rows + geometry.extra_rows) + ROWS, LANES)],
        "merge",
        cells,
    )(*arrived[::-1])
    got = to_partner(merged, "slab", 1)
    (change,) = call(
        functools.partial(change_kernel, sizes),
        [(FIELDS, nx * ny, nz)],
        "change",
        300_000 * cells,
    )(*gas, x_far, x_near, y_near, y_far)
    new_state, depth = call(
        functools.partial(final_kernel, sizes, geometry, firsts, direct),
        [(FIELDS, nx * ny, nz), (slots, length)],
        "final",
        100 * cells,
        [
            pltpu.VMEM((FIELDS, nx * ny, nz), jnp.float32),
            pltpu.VMEM((slots, length), jnp.float32),
            pltpu.VMEM((n_slab, geometry.rows, LANES), jnp.float32),
            pltpu.VMEM((n_slab, max(1, geometry.extra_rows), LANES), jnp.float32),
            pltpu.SemaphoreType.DMA((nx + 1,)),
        ],
        out_specs=[HBM, HBM],
    )(*gas, change, got, *arrived)
    return (new_state.reshape(FIELDS, nx, ny, nz), depth.reshape(1, 1, slots, length))


def solution(mesh):
    in_specs = (
        P("slab", "sect", None),
        P(None, "slab", "sect", None),
        P("slab", "sect", None),
        P("sect", None, None),
    )
    out_specs = (P(None, "slab", "sect", None), P("sect", "slab", None, None))
    return jax.shard_map(body, mesh=mesh, in_specs=in_specs, out_specs=out_specs, check_vma=False)
```

```python
import functools
import math
from typing import NamedTuple

import jax
import jax.numpy as jnp
from jax import lax
from jax.experimental import pallas as pl
from jax.experimental.pallas import tpu as pltpu
from jax.sharding import PartitionSpec as P

STRIDE = 32
BAND = 512

GAMMA = 5.0 / 3.0
COURANT = 0.15
TURBULENT = 0.25
NORMALISE = 0.5641895835477563

LANES = 128
ROWS = 8
FIELDS = 5
UNROLL = 64
PACK_COST = 30_000
PREPARE_COST = 300
MERGE_COST = 30_000

VMEM = pl.BlockSpec(memory_space=pltpu.VMEM)


HBM = pl.BlockSpec(memory_space=pltpu.HBM)


class Message(NamedTuple):
    owners: int
    slots: int
    group: int
    rows: int
    part: int
    main: int
    extra: int
    fold: int
    extra_rows: int
    count: int


def shape_of_message(nx, owners, slots, group):
    rows, part = slots // group, nx * group
    main = min(2 * FIELDS, LANES // part)
    extra = 2 * FIELDS - main
    fold = min(rows, LANES // (extra * part)) if extra else 1
    extra_rows = rows // fold if extra else 0
    count = 2 * rows + 2 * extra_rows + ROWS
    return Message(owners, slots, group, rows, part, main, extra, fold, extra_rows, count)


def call(kernel, out_shapes, name, flops, scratch=(), in_specs=None, out_specs=None):
    more = {} if in_specs is None else {"in_specs": in_specs}
    return pl.pallas_call(
        kernel,
        out_shape=[
            jax.ShapeDtypeStruct(*s) if isinstance(s[0], tuple) else jax.ShapeDtypeStruct(s, jnp.float32)
            for s in out_shapes
        ],
        out_specs=out_specs or [VMEM] * len(out_shapes),
        **more,
        scratch_shapes=list(scratch),
        compiler_params=pltpu.CompilerParams(vmem_limit_bytes=24 * 1024 * 1024),
        cost_estimate=pl.CostEstimate(flops=flops, bytes_accessed=1 << 20, transcendentals=0),
        name=name,
    )


def shift(array, amount, axis):
    size = array.shape[axis]
    amount = amount % size
    return array if amount == 0 else pltpu.roll(array, amount, axis)


def derived(cell):
    r, u, v, w, p = cell
    m = (r * u, r * v, r * w)
    energy = p * (1.0 / (GAMMA - 1.0)) + 0.5 * (m[0] * u + m[1] * v + m[2] * w)
    sound = jnp.sqrt(GAMMA * p / r)
    return (r, *m, energy), sound


def flux_parts(cell, state, sound, d):
    moving = cell[1 + d]
    flux = [state[1 + d]]
    for k in range(3):
        term = state[1 + k] * moving
        flux.append(term + cell[4] if k == d else term)
    flux.append((state[4] + cell[4]) * moving)
    return (*state, *flux, jnp.abs(moving) + sound)


def face(left, right):
    speed = jnp.maximum(left[10], right[10])
    return [
        (left[5 + k] + right[5 + k]) - speed * (right[k] - left[k]) for k in range(FIELDS)
    ]


def fields_of(r_ref, v_ref, p_ref, index):
    total = r_ref.shape[0]
    first = index.start if isinstance(index, pl.Slice) else index
    out = [r_ref[index]]
    for k in range(3):
        if isinstance(index, pl.Slice):
            out.append(v_ref[pl.ds(k * total + first, index.size, index.stride)])
        else:
            out.append(v_ref[k * total + index])
    out.append(p_ref[index])
    return out


def place_of(direct):
    me = lax.axis_index("slab")
    return (me // 2 if direct else 0), me % 2


def is_odd(axis, shape):
    return jnp.full(shape, lax.axis_index(axis) % 2) == 1


def sides(near, far, axis):
    odd = is_odd(axis, near[0].shape)
    low = [jnp.where(odd, n, f) for n, f in zip(near, far)]
    high = [jnp.where(odd, f, n) for n, f in zip(near, far)]
    return low, high


def edges_kernel(
    sizes, r_hbm, v_hbm, p_hbm, o_hbm, x_first, x_last, y_near, y_far, top_ref, r_ref, v_ref, p_ref, o_ref, sems
):
    nx, ny, nz = sizes
    pairs = [(r_hbm, r_ref), (v_hbm, v_ref), (p_hbm, p_ref), (o_hbm, o_ref)]
    loads = [pltpu.make_async_copy(source, target, sems.at[i]) for i, (source, target) in enumerate(pairs)]
    for load in loads:
        load.start()
    for load in loads:
        load.wait()
    for out, x in ((x_first, 0), (x_last, nx - 1)):
        for f, value in enumerate(fields_of(r_ref, v_ref, p_ref, pl.ds(x * ny, ny))):
            out[f] = value
    first, last = (fields_of(r_ref, v_ref, p_ref, pl.ds(y, nx, ny)) for y in (0, ny - 1))
    far, near = sides(last, first, "sect")
    for f in range(FIELDS):
        y_near[f] = near[f]
        y_far[f] = far[f]
    top = jnp.zeros((ROWS, nz), jnp.float32)
    for row in range(0, nx * ny, ROWS):
        r, u, v, w, p = fields_of(r_ref, v_ref, p_ref, pl.ds(row, ROWS))
        speed = jnp.maximum(jnp.maximum(jnp.abs(u), jnp.abs(v)), jnp.abs(w)) + jnp.sqrt(GAMMA * p / r)
        top = jnp.maximum(top, speed)
    y_near[FIELDS] = top
    top_ref[...] = top


def join_kernel(y_far, top_ref, near_ref, target_ref, out_ref, target_out):
    for f in range(FIELDS):
        out_ref[f] = y_far[f]
    out_ref[FIELDS] = jnp.maximum(top_ref[...], near_ref[FIELDS])
    target_out[...] = target_ref[...]


def spread_rows(msg):
    return LANES + msg.extra * msg.part


def prepare_kernel(sizes, msg, r_ref, v_ref, p_ref, owner_ref, cell_ref, change_ref, target_ref):
    nx, ny, nz = sizes
    lines = nz // STRIDE
    columns = ny * lines
    step = STRIDE // ROWS
    lane = lax.broadcasted_iota(jnp.int32, (nx, nz), 1)
    for t in range(step):
        cell = None
        for s in range(ny // step):
            rows = fields_of(r_ref, v_ref, p_ref, pl.ds(step * s + t, nx, ny))
            rows = [shift(a, step * s, 1) for a in rows]
            if cell is None:
                cell = rows
            else:
                mine = (lane - step * s + 1) % STRIDE < 3
                cell = [jnp.where(mine, a, b) for a, b in zip(rows, cell)]
        here = flux_parts(cell, *derived(cell), 2)
        after = face(here, [shift(a, -1, 1) for a in here])
        for f in range(FIELDS):
            cell_ref[t, f] = cell[f]
            change_ref[t, f] = after[f] - shift(after[f], 1, 1)
    owner = jnp.concatenate([owner_ref[k] for k in range(lines)], axis=1).astype(jnp.float32)
    own = jnp.broadcast_to(owner, (columns, columns))
    own_t = own.T

    def place(dim):
        at = lax.broadcasted_iota(jnp.int32, (columns, columns), dim)
        return (at % ny) * lines + at // ny

    ahead = (own == own_t) & (place(0) < place(1))
    rank = jnp.sum(jnp.where(ahead, 1.0, 0.0), axis=0, keepdims=True)
    target_ref[...] = jnp.broadcast_to(owner * msg.slots + rank, target_ref.shape)


def pack_kernel(sizes, msg, n_far, direct, cell_ref, change_ref, target_ref, y_near, y_far, top_ref, x_first, *rest):
    nx, ny, nz = sizes
    slots, group, width = msg.slots, msg.group, spread_rows(msg)
    far, x_out, outs, spread = rest[:n_far], rest[n_far], rest[n_far + 1 : -1], rest[-1]
    x_out[...] = x_first[...]
    y_low, y_high = sides([y_near[f] for f in range(FIELDS)], [y_far[f] for f in range(FIELDS)], "sect")
    columns = ny * (nz // STRIDE)
    step = STRIDE // ROWS
    lane = lax.broadcasted_iota(jnp.int32, (nx, nz), 1)
    target = target_ref[0:1]
    tiles = [[cell_ref[t, f] for f in range(FIELDS)] for t in range(step)]
    first = lane % STRIDE < step
    last = lane % STRIDE >= ny - step
    below = [jnp.where(first, y_low[f], shift(a, step, 1)) for f, a in enumerate(tiles[-1])]
    above = [jnp.where(last, shift(y_high[f], ny - step, 1), shift(a, -step, 1)) for f, a in enumerate(tiles[0])]
    parts = [flux_parts(cell, *derived(cell), 1) for cell in (below, *tiles, above)]
    faces = [face(a, b) for a, b in zip(parts, parts[1:])]
    dense = None
    for t in range(step):
        total = [(high - low) + change_ref[t, f] for f, (low, high) in enumerate(zip(faces[t], faces[t + 1]))]
        values = [shift(a, t, 1) for a in [*tiles[t], *total]]
        dense = values if dense is None else [jnp.where(lane % step == t, a, b) for a, b in zip(values, dense)]
    spread[...] = jnp.zeros_like(spread)
    for f, value in enumerate(dense):
        for h in range(group):
            spread[pl.ds(h * width + f * nx * group + h, nx, group), :] = value
    z_me, y_me = place_of(direct)

    def chosen(rows, first):
        row = lax.broadcasted_iota(jnp.int32, (msg.owners * rows, columns), 0)
        block = row // rows
        own_of = 2 * ((block // 2) ^ z_me) + ((block % 2) ^ y_me)
        out = []
        for h in range(group):
            slot = (own_of * slots + h * msg.rows + first + row % rows).astype(jnp.float32)
            out.append(jnp.where(slot == target, 1.0, 0.0))
        return jnp.concatenate(out, axis=1).astype(jnp.bfloat16)

    def pieces(first, count):
        value = jnp.concatenate([spread[pl.ds(h * width + first, count), :] for h in range(group)], axis=1)
        out = []
        for _ in range(3):
            out.append(value.astype(jnp.bfloat16))
            value = value - out[-1].astype(jnp.float32)
        return out

    def pick(selection, values):
        parts = [
            lax.dot_general(selection, v, (((1,), (1,)), ((), ())), preferred_element_type=jnp.float32) for v in values
        ]
        return (parts[0] + parts[1]) + parts[2]

    per = msg.count
    each = msg.owners // len(outs)
    picked = pick(chosen(msg.rows, 0), pieces(0, LANES))
    for b in range(msg.owners):
        at = (b % each) // 2 * per + b % 2 * msg.rows
        outs[b // each][pl.ds(at, msg.rows), :] = picked[b * msg.rows : (b + 1) * msg.rows]
    if msg.extra:
        values = pieces(LANES, msg.extra * msg.part)
        rows = msg.extra_rows
        picked = jnp.concatenate([pick(chosen(rows, a * rows), values) for a in range(msg.fold)], axis=1)
        for b in range(msg.owners):
            at = (b % each) // 2 * per + 2 * msg.rows + b % 2 * rows
            outs[b // each][pl.ds(at, rows), :] = picked[b * rows : (b + 1) * rows]
    top = jnp.maximum(jnp.maximum(top_ref[...], y_near[FIELDS]), y_far[FIELDS])
    for ref in far:
        top = jnp.maximum(top, ref[...])
    for out in outs:
        for d in range(each // 2):
            out[pl.ds((d + 1) * per - ROWS, ROWS), :] = top


def merge_kernel(msg, firsts, x_low, *refs):
    *refs, x_out, out = refs
    x_out[...] = x_low[...]
    half, top = msg.owners // 2, None
    for first, ref in zip(firsts, refs):
        for d in range(ref.shape[0] // msg.count):
            at, to = d * msg.count, first + d
            out[pl.ds(to * msg.rows, msg.rows), :] = ref[pl.ds(at + msg.rows, msg.rows), :]
            if msg.extra:
                rows = msg.extra_rows
                out[pl.ds(half * msg.rows + to * rows, rows), :] = ref[pl.ds(at + 2 * msg.rows + rows, rows), :]
            new = ref[pl.ds(at + msg.count - ROWS, ROWS), :]
            top = new if top is None else jnp.maximum(top, new)
    out[pl.ds(half * (msg.rows + msg.extra_rows), ROWS), :] = top


def change_kernel(sizes, r_ref, v_ref, p_ref, x_low, x_high, y_near, y_far, out_ref):
    nx, ny, nz = sizes
    every = range(FIELDS)
    y_low, y_high = sides([y_near[f] for f in every], [y_far[f] for f in every], "sect")
    row = lax.broadcasted_iota(jnp.int32, (ny, nz), 0)
    half = 0.5

    def layer(x):
        if x < 0:
            return [x_low[f] for f in range(FIELDS)]
        if x >= nx:
            return [x_high[f] for f in range(FIELDS)]
        return fields_of(r_ref, v_ref, p_ref, pl.ds(x * ny, ny))

    def prepared(x):
        cell = layer(x)
        state, sound = derived(cell)
        return cell, state, sound, flux_parts(cell, state, sound, 0)

    previous = prepared(-1)
    here = prepared(0)
    x_face = face(previous[3], here[3])
    for x in range(nx):
        following = prepared(x + 1)
        cell, state, sound, parts = here
        next_face = face(parts, following[3])
        total = [a - b for a, b in zip(next_face, x_face)]
        x_face = next_face
        low_cell = [y_low[f][x : x + 1] for f in range(FIELDS)]
        high_cell = [y_high[f][x : x + 1] for f in range(FIELDS)]
        low = flux_parts(low_cell, *derived(low_cell), 1)
        high = flux_parts(high_cell, *derived(high_cell), 1)
        parts = flux_parts(cell, state, sound, 1)
        plus = [jnp.where(row == ny - 1, h, shift(a, -1, 0)) for a, h in zip(parts, high)]
        after = face(parts, plus)
        edge = face(low, [a[0:1] for a in parts])
        before = [jnp.where(row == 0, e, shift(a, 1, 0)) for a, e in zip(after, edge)]
        total = [t + (a - b) for t, a, b in zip(total, after, before)]
        parts = flux_parts(cell, state, sound, 2)
        after = face(parts, [shift(a, -1, 1) for a in parts])
        total = [t + (a - shift(a, 1, 1)) for t, a in zip(total, after)]
        for f in range(FIELDS):
            out_ref[f, pl.ds(x * ny, ny), :] = half * total[f]
        here = following


def final_kernel(sizes, msg, firsts, direct, r_ref, v_ref, p_ref, change_ref, got_ref, *rest):
    blocks = rest[: len(firsts)]
    new_hbm, depth_hbm, new_ref, depth_ref, main_ref, extra_ref, sems = rest[len(firsts) :]
    nx, ny, nz = sizes
    n_owner, group, part = msg.owners, msg.group, msg.part
    half, length = n_owner // 2, nx * n_owner
    top = got_ref[pl.ds(half * (msg.rows + msg.extra_rows), ROWS), :]
    for ref in blocks:
        for d in range(ref.shape[0] // msg.count):
            top = jnp.maximum(top, ref[pl.ds((d + 1) * msg.count - ROWS, ROWS), :])
    step = COURANT / jnp.max(top, keepdims=True)
    writes = []
    for x in range(nx):
        rows = pl.ds(x * ny, ny)
        state, _ = derived(fields_of(r_ref, v_ref, p_ref, rows))
        for f in range(FIELDS):
            new_ref[f, rows, :] = state[f] - step * change_ref[f, rows, :]
        writes.append(pltpu.make_async_copy(new_ref.at[:, rows], new_hbm.at[:, rows], sems.at[x]))
        writes[-1].start()
    z_me, y_me = place_of(direct)

    def settle(source, at, extra_at, d, odd):
        owner = 2 * (d ^ z_me) + (odd ^ y_me)
        main_ref[owner] = source[pl.ds(at, msg.rows), :]
        if msg.extra:
            extra_ref[owner] = source[pl.ds(extra_at, msg.extra_rows), :]

    for first, ref in zip(firsts, blocks):
        for d in range(ref.shape[0] // msg.count):
            settle(ref, d * msg.count, d * msg.count + 2 * msg.rows, first + d, 0)
    for d in range(half):
        settle(got_ref, d * msg.rows, half * msg.rows + d * msg.extra_rows, d, 1)
    line = []
    for f in range(msg.main):
        line.append(jnp.concatenate([main_ref[q, :, pl.ds(f * part, part)] for q in range(n_owner)], axis=1))
    for f in range(msg.extra):
        folds = []
        for a in range(msg.fold):
            at = pl.ds((a * msg.extra + f) * part, part)
            folds.append(jnp.concatenate([extra_ref[q, :, at] for q in range(n_owner)], axis=1))
        line.append(jnp.concatenate(folds, axis=0))
    cell, change = line[:FIELDS], line[FIELDS:]
    taken = cell[0] > 0.0
    cell[0] = jnp.where(taken, cell[0], 1.0)
    state, sound = derived(cell)
    parts = flux_parts(cell, state, sound, 0)
    after = face(parts, [shift(a, -group, 1) for a in parts])
    change = [c + (a - shift(a, group, 1)) for c, a in zip(change, after)]
    new = [s - (0.5 * step) * c for s, c in zip(state, change)]
    density = new[0]
    pressure = (GAMMA - 1.0) * (new[4] - 0.5 * (new[1] * new[1] + new[2] * new[2] + new[3] * new[3]) / density)
    broadening = TURBULENT + pressure / density
    inverse = 1.0 / (BAND / 64.0 * jnp.sqrt(broadening))
    amplitude = NORMALISE * (density * density) * jnp.exp(-0.7 * jnp.log(broadening)) * inverse
    amplitude = jnp.where(taken, amplitude, 0.0)
    scaled = inverse * math.sqrt(math.log2(math.e))
    centre = (BAND / 8.0) * (new[1] / density)
    turns = BAND // length
    strides = [scaled * float(length * m) for m in range(turns)]

    block = min(length, UNROLL)

    def offsets(count, running):
        e = (length - block - block * count) * 1.0 - float(BAND // 2)
        for b in range(block):
            start = (e + float(b) - centre) * scaled
            total = None
            for m in range(turns):
                t = start + strides[m] if m else start
                value = jnp.exp2(-(t * t))
                total = value if total is None else total + value
            part = shift(amplitude * total, b * group, 1)
            block_sum = part if b == 0 else block_sum + part
        return block_sum if running is None else shift(running, block * group, 1) + block_sum

    if length == block:
        running = offsets(0, None)
    else:
        running = lax.fori_loop(
            0,
            length // block,
            lambda i, c: offsets(i.astype(jnp.float32), c),
            jnp.zeros_like(amplitude),
        )
    running = shift(running, -(BAND // 2) * group, 1)
    if group == 1:
        depth_ref[...] = running
    else:
        at = lax.broadcasted_iota(jnp.int32, (group * length, length), 0)
        cell_of = lax.broadcasted_iota(jnp.int32, (group * length, length), 1)
        for h in range(group):
            pick = jnp.where(at == cell_of * group + h, 1.0, 0.0)
            depth_ref[pl.ds(h * msg.rows, msg.rows), :] = jnp.dot(
                running, pick, precision=lax.Precision.HIGHEST, preferred_element_type=jnp.float32
            )
    writes.append(pltpu.make_async_copy(depth_ref, depth_hbm, sems.at[nx]))
    writes[-1].start()
    for write in writes:
        write.wait()


def around(value, axis, amount):
    count = lax.axis_size(axis)
    return lax.ppermute(value, axis, [(i, (i + amount) % count) for i in range(count)])


def to_partner(value, axis, bits):
    return lax.ppermute(value, axis, [(i, i ^ bits) for i in range(lax.axis_size(axis))])


def to_other(value, axis):
    count = lax.axis_size(axis)
    return lax.ppermute(value, axis, [(i, (i + 2 * (i % 2) - 1) % count) for i in range(count)])


def body(density, velocity, pressure, owners):
    sizes = nx, ny, nz = density.shape
    n_sect, n_slab = lax.axis_size("sect"), lax.axis_size("slab")
    lines = nz // STRIDE
    columns = ny * lines
    slots = 2 * columns // n_slab
    length = nx * n_slab
    group = max(1, LANES // length)
    geometry = shape_of_message(nx, n_slab, slots, group)
    gas = (
        density.reshape(nx * ny, nz),
        velocity.reshape(3 * nx * ny, nz),
        pressure.reshape(nx * ny, nz),
    )
    cells = nx * ny * nz
    half = n_slab // 2
    direct = half <= 4
    x_edge, y_edge, row = (FIELDS, ny, nz), (FIELDS + 1, nx, nz), (ROWS, nz)
    owners = jnp.transpose(owners, (1, 2, 0))
    shapes = [(a.shape, a.dtype) for a in (*gas, owners)]
    x_first, x_last, y_near, y_far, top, *gas, owners = call(
        functools.partial(edges_kernel, sizes),
        [x_edge, x_edge, y_edge, (FIELDS, nx, nz), row, *shapes],
        "edges",
        20 * cells,
        [pltpu.SemaphoreType.DMA((4,))],
        in_specs=[HBM] * 4,
    )(*(pltpu.with_memory_space_constraint(a, pltpu.HBM) for a in (*gas, owners)))
    tiles = (STRIDE // ROWS, FIELDS, nx, nz)
    cells_at, change_at, target = call(
        functools.partial(prepare_kernel, sizes, geometry),
        [tiles, tiles, (ROWS, columns)],
        "prepare",
        PREPARE_COST * cells,
    )(*gas, owners)
    y_near = to_partner(y_near, "sect", 1)
    y_far, target = call(join_kernel, [y_edge, (ROWS, columns)], "join", cells)(y_far, top, y_near, target)
    y_far = to_other(y_far, "sect")
    far = [around(top, "sect", d) for d in range(2, n_sect - 1)] if n_sect > 4 else []
    x_low = around(x_last, "slab", 1)
    firsts = range(half) if direct else range(1)
    x_first, *packed = call(
        functools.partial(pack_kernel, sizes, geometry, len(far), direct),
        [x_edge] + [(half // len(firsts) * geometry.count, LANES)] * len(firsts),
        "pack",
        PACK_COST * cells,
        [pltpu.VMEM((group * spread_rows(geometry), columns), jnp.float32)],
    )(cells_at, change_at, target, y_near, y_far, top, x_first, *far)
    if direct:
        arrived = [to_partner(m, "slab", 2 * d) if d else m for d, m in zip(firsts, packed)]
    else:
        alike = [[2 * i + odd for i in range(half)] for odd in range(2)]
        arrived = [
            lax.all_to_all(m, "slab", split_axis=0, concat_axis=0, axis_index_groups=alike, tiled=True) for m in packed
        ]
    x_low, merged = call(
        functools.partial(merge_kernel, geometry, [firsts[i] for i in [2, 3, 1, 0]] if direct else firsts),
        [x_edge, (half * (geometry.rows + geometry.extra_rows) + ROWS, LANES)],
        "merge",
        MERGE_COST * cells,
    )(x_low, *([arrived[i] for i in [2, 3, 1, 0]] if direct else arrived))
    got = to_partner(merged, "slab", 1)
    x_high = around(x_first, "slab", -1)
    (change,) = call(
        functools.partial(change_kernel, sizes),
        [(FIELDS, nx * ny, nz)],
        "change",
        300_000 * cells,
    )(*gas, x_low, x_high, y_near, y_far)
    new_state, depth = call(
        functools.partial(final_kernel, sizes, geometry, firsts, direct),
        [(FIELDS, nx * ny, nz), (slots, length)],
        "final",
        100 * cells,
        [
            pltpu.VMEM((FIELDS, nx * ny, nz), jnp.float32),
            pltpu.VMEM((slots, length), jnp.float32),
            pltpu.VMEM((n_slab, geometry.rows, LANES), jnp.float32),
            pltpu.VMEM((n_slab, max(1, geometry.extra_rows), LANES), jnp.float32),
            pltpu.SemaphoreType.DMA((nx + 1,)),
        ],
        out_specs=[HBM, HBM],
    )(*gas, change, got, *arrived)
    return (new_state.reshape(FIELDS, nx, ny, nz), depth.reshape(1, 1, slots, length))


def solution(mesh):
    in_specs = (
        P("slab", "sect", None),
        P(None, "slab", "sect", None),
        P("slab", "sect", None),
        P("sect", None, None),
    )
    out_specs = (P(None, "slab", "sect", None), P("sect", "slab", None, None))
    return jax.shard_map(body, mesh=mesh, in_specs=in_specs, out_specs=out_specs, check_vma=False)
```

```python
import functools
import math
from typing import NamedTuple

import jax
import jax.numpy as jnp
from jax import lax
from jax.experimental import pallas as pl
from jax.experimental.pallas import tpu as pltpu
from jax.sharding import PartitionSpec as P

STRIDE = 32
BAND = 512

GAMMA = 5.0 / 3.0
COURANT = 0.15
TURBULENT = 0.25
NORMALISE = 0.5641895835477563

LANES = 128
ROWS = 8
FIELDS = 5
UNROLL = 64
PACK_COST = 30_000
PREPARE_COST = 300
MERGE_COST = 30_000

VMEM = pl.BlockSpec(memory_space=pltpu.VMEM)


HBM = pl.BlockSpec(memory_space=pltpu.HBM)


class Message(NamedTuple):
    owners: int
    slots: int
    group: int
    rows: int
    part: int
    main: int
    extra: int
    fold: int
    extra_rows: int
    count: int


def shape_of_message(nx, owners, slots, group):
    rows, part = slots // group, nx * group
    main = min(2 * FIELDS, LANES // part)
    extra = 2 * FIELDS - main
    fold = min(rows, LANES // (extra * part)) if extra else 1
    extra_rows = rows // fold if extra else 0
    count = 2 * rows + 2 * extra_rows + ROWS
    return Message(owners, slots, group, rows, part, main, extra, fold, extra_rows, count)


def call(kernel, out_shapes, name, flops, scratch=(), in_specs=None, out_specs=None):
    more = {} if in_specs is None else {"in_specs": in_specs}
    return pl.pallas_call(
        kernel,
        out_shape=[
            jax.ShapeDtypeStruct(*s) if isinstance(s[0], tuple) else jax.ShapeDtypeStruct(s, jnp.float32)
            for s in out_shapes
        ],
        out_specs=out_specs or [VMEM] * len(out_shapes),
        **more,
        scratch_shapes=list(scratch),
        compiler_params=pltpu.CompilerParams(vmem_limit_bytes=24 * 1024 * 1024),
        cost_estimate=pl.CostEstimate(flops=flops, bytes_accessed=1 << 20, transcendentals=0),
        name=name,
    )


def shift(array, amount, axis):
    size = array.shape[axis]
    amount = amount % size
    return array if amount == 0 else pltpu.roll(array, amount, axis)


def derived(cell):
    r, u, v, w, p = cell
    m = (r * u, r * v, r * w)
    energy = p * (1.0 / (GAMMA - 1.0)) + 0.5 * (m[0] * u + m[1] * v + m[2] * w)
    sound = jnp.sqrt(GAMMA * p / r)
    return (r, *m, energy), sound


def flux_parts(cell, state, sound, d):
    moving = cell[1 + d]
    flux = [state[1 + d]]
    for k in range(3):
        term = state[1 + k] * moving
        flux.append(term + cell[4] if k == d else term)
    flux.append((state[4] + cell[4]) * moving)
    return (*state, *flux, jnp.abs(moving) + sound)


def face(left, right):
    speed = jnp.maximum(left[10], right[10])
    return [
        (left[5 + k] + right[5 + k]) - speed * (right[k] - left[k]) for k in range(FIELDS)
    ]


def fields_of(r_ref, v_ref, p_ref, index):
    total = r_ref.shape[0]
    first = index.start if isinstance(index, pl.Slice) else index
    out = [r_ref[index]]
    for k in range(3):
        if isinstance(index, pl.Slice):
            out.append(v_ref[pl.ds(k * total + first, index.size, index.stride)])
        else:
            out.append(v_ref[k * total + index])
    out.append(p_ref[index])
    return out


def place_of(direct):
    me = lax.axis_index("slab")
    return (me // 2 if direct else 0), me % 2


def is_odd(axis, shape):
    return jnp.full(shape, lax.axis_index(axis) % 2) == 1


def sides(near, far, axis):
    odd = is_odd(axis, near[0].shape)
    low = [jnp.where(odd, n, f) for n, f in zip(near, far)]
    high = [jnp.where(odd, f, n) for n, f in zip(near, far)]
    return low, high


def edges_kernel(
    sizes, r_hbm, v_hbm, p_hbm, o_hbm, x_first, x_last, y_near, y_far, top_ref, r_ref, v_ref, p_ref, o_ref, sems
):
    nx, ny, nz = sizes
    pairs = [(r_hbm, r_ref), (v_hbm, v_ref), (p_hbm, p_ref), (o_hbm, o_ref)]
    loads = [pltpu.make_async_copy(source, target, sems.at[i]) for i, (source, target) in enumerate(pairs)]
    for load in loads:
        load.start()
    for load in loads:
        load.wait()
    for out, x in ((x_first, 0), (x_last, nx - 1)):
        for f, value in enumerate(fields_of(r_ref, v_ref, p_ref, pl.ds(x * ny, ny))):
            out[f] = value
    first, last = (fields_of(r_ref, v_ref, p_ref, pl.ds(y, nx, ny)) for y in (0, ny - 1))
    far, near = sides(last, first, "sect")
    for f in range(FIELDS):
        y_near[f] = near[f]
        y_far[f] = far[f]
    top = jnp.zeros((ROWS, nz), jnp.float32)
    for row in range(0, nx * ny, ROWS):
        r, u, v, w, p = fields_of(r_ref, v_ref, p_ref, pl.ds(row, ROWS))
        speed = jnp.maximum(jnp.maximum(jnp.abs(u), jnp.abs(v)), jnp.abs(w)) + jnp.sqrt(GAMMA * p / r)
        top = jnp.maximum(top, speed)
    y_near[FIELDS] = top
    top_ref[...] = top


def join_kernel(y_far, top_ref, near_ref, target_ref, out_ref, target_out):
    for f in range(FIELDS):
        out_ref[f] = y_far[f]
    out_ref[FIELDS] = jnp.maximum(top_ref[...], near_ref[FIELDS])
    target_out[...] = target_ref[...]


def spread_rows(msg):
    return LANES + msg.extra * msg.part


def prepare_kernel(sizes, msg, r_ref, v_ref, p_ref, owner_ref, cell_ref, change_ref, target_ref):
    nx, ny, nz = sizes
    lines = nz // STRIDE
    columns = ny * lines
    step = STRIDE // ROWS
    lane = lax.broadcasted_iota(jnp.int32, (nx, nz), 1)
    for t in range(step):
        cell = None
        for s in range(ny // step):
            rows = fields_of(r_ref, v_ref, p_ref, pl.ds(step * s + t, nx, ny))
            rows = [shift(a, step * s, 1) for a in rows]
            if cell is None:
                cell = rows
            else:
                mine = (lane - step * s + 1) % STRIDE < 3
                cell = [jnp.where(mine, a, b) for a, b in zip(rows, cell)]
        here = flux_parts(cell, *derived(cell), 2)
        after = face(here, [shift(a, -1, 1) for a in here])
        for f in range(FIELDS):
            cell_ref[t, f] = cell[f]
            change_ref[t, f] = after[f] - shift(after[f], 1, 1)
    owner = jnp.concatenate([owner_ref[k] for k in range(lines)], axis=1).astype(jnp.float32)
    own = jnp.broadcast_to(owner, (columns, columns))
    own_t = own.T

    def place(dim):
        at = lax.broadcasted_iota(jnp.int32, (columns, columns), dim)
        return (at % ny) * lines + at // ny

    ahead = (own == own_t) & (place(0) < place(1))
    rank = jnp.sum(jnp.where(ahead, 1.0, 0.0), axis=0, keepdims=True)
    target_ref[...] = jnp.broadcast_to(owner * msg.slots + rank, target_ref.shape)


def pack_kernel(sizes, msg, n_far, direct, cell_ref, change_ref, target_ref, y_near, y_far, top_ref, x_first, *rest):
    nx, ny, nz = sizes
    slots, group, width = msg.slots, msg.group, spread_rows(msg)
    far, x_out, outs, spread = rest[:n_far], rest[n_far], rest[n_far + 1 : -1], rest[-1]
    x_out[...] = x_first[...]
    y_low, y_high = sides([y_near[f] for f in range(FIELDS)], [y_far[f] for f in range(FIELDS)], "sect")
    columns = ny * (nz // STRIDE)
    step = STRIDE // ROWS
    lane = lax.broadcasted_iota(jnp.int32, (nx, nz), 1)
    target = target_ref[0:1]
    tiles = [[cell_ref[t, f] for f in range(FIELDS)] for t in range(step)]
    first = lane % STRIDE < step
    last = lane % STRIDE >= ny - step
    below = [jnp.where(first, y_low[f], shift(a, step, 1)) for f, a in enumerate(tiles[-1])]
    above = [jnp.where(last, shift(y_high[f], ny - step, 1), shift(a, -step, 1)) for f, a in enumerate(tiles[0])]
    parts = [flux_parts(cell, *derived(cell), 1) for cell in (below, *tiles, above)]
    faces = [face(a, b) for a, b in zip(parts, parts[1:])]
    dense = None
    for t in range(step):
        total = [(high - low) + change_ref[t, f] for f, (low, high) in enumerate(zip(faces[t], faces[t + 1]))]
        values = [shift(a, t, 1) for a in [*tiles[t], *total]]
        dense = values if dense is None else [jnp.where(lane % step == t, a, b) for a, b in zip(values, dense)]
    spread[...] = jnp.zeros_like(spread)
    for f, value in enumerate(dense):
        for h in range(group):
            spread[pl.ds(h * width + f * nx * group + h, nx, group), :] = value
    z_me, y_me = place_of(direct)

    def chosen(rows, first):
        row = lax.broadcasted_iota(jnp.int32, (msg.owners * rows, columns), 0)
        block = row // rows
        own_of = 2 * ((block // 2) ^ z_me) + ((block % 2) ^ y_me)
        out = []
        for h in range(group):
            slot = (own_of * slots + (first + row % rows) * group + h).astype(jnp.float32)
            out.append(jnp.where(slot == target, 1.0, 0.0))
        return jnp.concatenate(out, axis=1).astype(jnp.bfloat16)

    def pieces(first, count):
        value = jnp.concatenate([spread[pl.ds(h * width + first, count), :] for h in range(group)], axis=1)
        out = []
        for _ in range(3):
            out.append(value.astype(jnp.bfloat16))
            value = value - out[-1].astype(jnp.float32)
        return jnp.concatenate(out, axis=1)

    def pick(selection, values):
        selection = jnp.concatenate([selection] * 3, axis=1)
        return lax.dot_general(selection, values, (((1,), (1,)), ((), ())), preferred_element_type=jnp.float32)

    per = msg.count
    each = msg.owners // len(outs)
    picked = pick(chosen(msg.rows, 0), pieces(0, LANES))
    for b in range(msg.owners):
        at = (b % each) // 2 * per + b % 2 * msg.rows
        outs[b // each][pl.ds(at, msg.rows), :] = picked[b * msg.rows : (b + 1) * msg.rows]
    if msg.extra:
        values = pieces(LANES, msg.extra * msg.part)
        rows = msg.extra_rows
        picked = jnp.concatenate([pick(chosen(rows, a * rows), values) for a in range(msg.fold)], axis=1)
        for b in range(msg.owners):
            at = (b % each) // 2 * per + 2 * msg.rows + b % 2 * rows
            outs[b // each][pl.ds(at, rows), :] = picked[b * rows : (b + 1) * rows]
    top = jnp.maximum(jnp.maximum(top_ref[...], y_near[FIELDS]), y_far[FIELDS])
    for ref in far:
        top = jnp.maximum(top, ref[...])
    for out in outs:
        for d in range(each // 2):
            out[pl.ds((d + 1) * per - ROWS, ROWS), :] = top


def merge_kernel(msg, firsts, x_low, *refs):
    *refs, x_out, out = refs
    x_out[...] = x_low[...]
    half, top = msg.owners // 2, None
    for first, ref in zip(firsts, refs):
        for d in range(ref.shape[0] // msg.count):
            at, to = d * msg.count, first + d
            out[pl.ds(to * msg.rows, msg.rows), :] = ref[pl.ds(at + msg.rows, msg.rows), :]
            if msg.extra:
                rows = msg.extra_rows
                out[pl.ds(half * msg.rows + to * rows, rows), :] = ref[pl.ds(at + 2 * msg.rows + rows, rows), :]
            new = ref[pl.ds(at + msg.count - ROWS, ROWS), :]
            top = new if top is None else jnp.maximum(top, new)
    out[pl.ds(half * (msg.rows + msg.extra_rows), ROWS), :] = top


def change_kernel(sizes, r_ref, v_ref, p_ref, x_low, x_high, y_near, y_far, out_ref):
    nx, ny, nz = sizes
    every = range(FIELDS)
    y_low, y_high = sides([y_near[f] for f in every], [y_far[f] for f in every], "sect")
    row = lax.broadcasted_iota(jnp.int32, (ny, nz), 0)
    half = 0.5

    def layer(x):
        if x < 0:
            return [x_low[f] for f in range(FIELDS)]
        if x >= nx:
            return [x_high[f] for f in range(FIELDS)]
        return fields_of(r_ref, v_ref, p_ref, pl.ds(x * ny, ny))

    def prepared(x):
        cell = layer(x)
        state, sound = derived(cell)
        return cell, state, sound, flux_parts(cell, state, sound, 0)

    previous = prepared(-1)
    here = prepared(0)
    x_face = face(previous[3], here[3])
    for x in range(nx):
        following = prepared(x + 1)
        cell, state, sound, parts = here
        next_face = face(parts, following[3])
        total = [a - b for a, b in zip(next_face, x_face)]
        x_face = next_face
        low_cell = [y_low[f][x : x + 1] for f in range(FIELDS)]
        high_cell = [y_high[f][x : x + 1] for f in range(FIELDS)]
        low = flux_parts(low_cell, *derived(low_cell), 1)
        high = flux_parts(high_cell, *derived(high_cell), 1)
        parts = flux_parts(cell, state, sound, 1)
        plus = [jnp.where(row == ny - 1, h, shift(a, -1, 0)) for a, h in zip(parts, high)]
        after = face(parts, plus)
        edge = face(low, [a[0:1] for a in parts])
        before = [jnp.where(row == 0, e, shift(a, 1, 0)) for a, e in zip(after, edge)]
        total = [t + (a - b) for t, a, b in zip(total, after, before)]
        parts = flux_parts(cell, state, sound, 2)
        after = face(parts, [shift(a, -1, 1) for a in parts])
        total = [t + (a - shift(a, 1, 1)) for t, a in zip(total, after)]
        for f in range(FIELDS):
            out_ref[f, pl.ds(x * ny, ny), :] = half * total[f]
        here = following


def final_kernel(sizes, msg, firsts, direct, r_ref, v_ref, p_ref, change_ref, got_ref, *rest):
    blocks = rest[: len(firsts)]
    new_hbm, depth_hbm, new_ref, depth_ref, main_ref, extra_ref, sems = rest[len(firsts) :]
    nx, ny, nz = sizes
    n_owner, group, part = msg.owners, msg.group, msg.part
    half, length = n_owner // 2, nx * n_owner
    top = got_ref[pl.ds(half * (msg.rows + msg.extra_rows), ROWS), :]
    for ref in blocks:
        for d in range(ref.shape[0] // msg.count):
            top = jnp.maximum(top, ref[pl.ds((d + 1) * msg.count - ROWS, ROWS), :])
    step = COURANT / jnp.max(top, keepdims=True)
    writes = []
    for x in range(nx):
        rows = pl.ds(x * ny, ny)
        state, _ = derived(fields_of(r_ref, v_ref, p_ref, rows))
        for f in range(FIELDS):
            new_ref[f, rows, :] = state[f] - step * change_ref[f, rows, :]
        writes.append(pltpu.make_async_copy(new_ref.at[:, rows], new_hbm.at[:, rows], sems.at[x]))
        writes[-1].start()
    z_me, y_me = place_of(direct)

    def settle(source, at, extra_at, d, odd):
        owner = 2 * (d ^ z_me) + (odd ^ y_me)
        main_ref[owner] = source[pl.ds(at, msg.rows), :]
        if msg.extra:
            extra_ref[owner] = source[pl.ds(extra_at, msg.extra_rows), :]

    for first, ref in zip(firsts, blocks):
        for d in range(ref.shape[0] // msg.count):
            settle(ref, d * msg.count, d * msg.count + 2 * msg.rows, first + d, 0)
    for d in range(half):
        settle(got_ref, d * msg.rows, half * msg.rows + d * msg.extra_rows, d, 1)
    line = []
    for f in range(msg.main):
        line.append(jnp.concatenate([main_ref[q, :, pl.ds(f * part, part)] for q in range(n_owner)], axis=1))
    for f in range(msg.extra):
        folds = []
        for a in range(msg.fold):
            at = pl.ds((a * msg.extra + f) * part, part)
            folds.append(jnp.concatenate([extra_ref[q, :, at] for q in range(n_owner)], axis=1))
        line.append(jnp.concatenate(folds, axis=0))
    cell, change = line[:FIELDS], line[FIELDS:]
    taken = cell[0] > 0.0
    cell[0] = jnp.where(taken, cell[0], 1.0)
    state, sound = derived(cell)
    parts = flux_parts(cell, state, sound, 0)
    after = face(parts, [shift(a, -group, 1) for a in parts])
    change = [c + (a - shift(a, group, 1)) for c, a in zip(change, after)]
    new = [s - (0.5 * step) * c for s, c in zip(state, change)]
    density = new[0]
    pressure = (GAMMA - 1.0) * (new[4] - 0.5 * (new[1] * new[1] + new[2] * new[2] + new[3] * new[3]) / density)
    broadening = TURBULENT + pressure / density
    inverse = 1.0 / (BAND / 64.0 * jnp.sqrt(broadening))
    amplitude = NORMALISE * (density * density) * jnp.exp(-0.7 * jnp.log(broadening)) * inverse
    amplitude = jnp.where(taken, amplitude, 0.0)
    scaled = inverse * math.sqrt(math.log2(math.e))
    centre = (BAND / 8.0) * (new[1] / density)
    turns = BAND // length
    block = min(length, UNROLL)

    def skewers(rows):
        scale, middle, size = scaled[:rows], centre[:rows], amplitude[:rows]
        strides = [scale * float(length * m) for m in range(turns)]

        def offsets(count, running):
            e = (length - block - block * count) * 1.0 - float(BAND // 2)
            for b in range(block):
                start = (e + float(b) - middle) * scale
                total = None
                for m in range(turns):
                    t = start + strides[m] if m else start
                    value = jnp.exp2(-(t * t))
                    total = value if total is None else total + value
                part = shift(size * total, b * group, 1)
                block_sum = part if b == 0 else block_sum + part
            return block_sum if running is None else shift(running, block * group, 1) + block_sum

        if length == block:
            running = offsets(0, None)
        else:
            running = lax.fori_loop(
                0,
                length // block,
                lambda i, c: offsets(i.astype(jnp.float32), c),
                jnp.zeros_like(size),
            )
        running = shift(running, -(BAND // 2) * group, 1)
        if group > 1:
            wide = jnp.broadcast_to(running[:, None, :], (rows, group, group * length))
            wide = wide.reshape(rows * group, group * length)
            at = lax.broadcasted_iota(jnp.int32, wide.shape, 1)
            of = lax.broadcasted_iota(jnp.int32, wide.shape, 0)
            wide = jnp.where(at % group == of % group, wide, 0.0)
            at = lax.broadcasted_iota(jnp.int32, (group * length, length), 0)
            of = lax.broadcasted_iota(jnp.int32, (group * length, length), 1)
            pick = jnp.where(at // group == of, 1.0, 0.0)
            running = jnp.dot(wide, pick, precision=lax.Precision.HIGHEST, preferred_element_type=jnp.float32)
        depth_ref[pl.ds(0, rows * group), :] = running

    if msg.rows > ROWS:
        more = jnp.max(jnp.where(taken[ROWS:], 1.0, 0.0)) > 0.0

        @pl.when(more)
        def _():
            skewers(msg.rows)

        @pl.when(jnp.logical_not(more))
        def _():
            depth_ref[...] = jnp.zeros_like(depth_ref)
            skewers(ROWS)

    else:
        skewers(msg.rows)
    writes.append(pltpu.make_async_copy(depth_ref, depth_hbm, sems.at[nx]))
    writes[-1].start()
    for write in writes:
        write.wait()


def around(value, axis, amount):
    count = lax.axis_size(axis)
    return lax.ppermute(value, axis, [(i, (i + amount) % count) for i in range(count)])


def to_partner(value, axis, bits):
    return lax.ppermute(value, axis, [(i, i ^ bits) for i in range(lax.axis_size(axis))])


def to_other(value, axis):
    count = lax.axis_size(axis)
    return lax.ppermute(value, axis, [(i, (i + 2 * (i % 2) - 1) % count) for i in range(count)])


def body(density, velocity, pressure, owners):
    sizes = nx, ny, nz = density.shape
    n_sect, n_slab = lax.axis_size("sect"), lax.axis_size("slab")
    lines = nz // STRIDE
    columns = ny * lines
    slots = 2 * columns // n_slab
    length = nx * n_slab
    group = max(1, LANES // length)
    geometry = shape_of_message(nx, n_slab, slots, group)
    gas = (
        density.reshape(nx * ny, nz),
        velocity.reshape(3 * nx * ny, nz),
        pressure.reshape(nx * ny, nz),
    )
    cells = nx * ny * nz
    half = n_slab // 2
    direct = half <= 4
    x_edge, y_edge, row = (FIELDS, ny, nz), (FIELDS + 1, nx, nz), (ROWS, nz)
    owners = jnp.transpose(owners, (1, 2, 0))
    shapes = [(a.shape, a.dtype) for a in (*gas, owners)]
    x_first, x_last, y_near, y_far, top, *gas, owners = call(
        functools.partial(edges_kernel, sizes),
        [x_edge, x_edge, y_edge, (FIELDS, nx, nz), row, *shapes],
        "edges",
        20 * cells,
        [pltpu.SemaphoreType.DMA((4,))],
        in_specs=[HBM] * 4,
    )(*(pltpu.with_memory_space_constraint(a, pltpu.HBM) for a in (*gas, owners)))
    tiles = (STRIDE // ROWS, FIELDS, nx, nz)
    cells_at, change_at, target = call(
        functools.partial(prepare_kernel, sizes, geometry),
        [tiles, tiles, (ROWS, columns)],
        "prepare",
        PREPARE_COST * cells,
    )(*gas, owners)
    y_near = to_partner(y_near, "sect", 1)
    y_far, target = call(join_kernel, [y_edge, (ROWS, columns)], "join", cells)(y_far, top, y_near, target)
    y_far = to_other(y_far, "sect")
    far = [around(top, "sect", d) for d in range(2, n_sect - 1)] if n_sect > 4 else []
    x_low = around(x_last, "slab", 1)
    firsts = range(half) if direct else range(1)
    x_first, *packed = call(
        functools.partial(pack_kernel, sizes, geometry, len(far), direct),
        [x_edge] + [(half // len(firsts) * geometry.count, LANES)] * len(firsts),
        "pack",
        PACK_COST * cells,
        [pltpu.VMEM((group * spread_rows(geometry), columns), jnp.float32)],
    )(cells_at, change_at, target, y_near, y_far, top, x_first, *far)
    if direct:
        arrived = [to_partner(m, "slab", 2 * d) if d else m for d, m in zip(firsts, packed)]
    else:
        alike = [[2 * i + odd for i in range(half)] for odd in range(2)]
        arrived = [
            lax.all_to_all(m, "slab", split_axis=0, concat_axis=0, axis_index_groups=alike, tiled=True) for m in packed
        ]
    x_low, merged = call(
        functools.partial(merge_kernel, geometry, [firsts[i] for i in [2, 3, 1, 0]] if direct else firsts),
        [x_edge, (half * (geometry.rows + geometry.extra_rows) + ROWS, LANES)],
        "merge",
        MERGE_COST * cells,
    )(x_low, *([arrived[i] for i in [2, 3, 1, 0]] if direct else arrived))
    got = to_partner(merged, "slab", 1)
    x_high = around(x_first, "slab", -1)
    (change,) = call(
        functools.partial(change_kernel, sizes),
        [(FIELDS, nx * ny, nz)],
        "change",
        300_000 * cells,
    )(*gas, x_low, x_high, y_near, y_far)
    new_state, depth = call(
        functools.partial(final_kernel, sizes, geometry, firsts, direct),
        [(FIELDS, nx * ny, nz), (slots, length)],
        "final",
        100 * cells,
        [
            pltpu.VMEM((FIELDS, nx * ny, nz), jnp.float32),
            pltpu.VMEM((slots, length), jnp.float32),
            pltpu.VMEM((n_slab, geometry.rows, LANES), jnp.float32),
            pltpu.VMEM((n_slab, max(1, geometry.extra_rows), LANES), jnp.float32),
            pltpu.SemaphoreType.DMA((nx + 1,)),
        ],
        out_specs=[HBM, HBM],
    )(*gas, change, got, *arrived)
    return (new_state.reshape(FIELDS, nx, ny, nz), depth.reshape(1, 1, slots, length))


def solution(mesh):
    in_specs = (
        P("slab", "sect", None),
        P(None, "slab", "sect", None),
        P("slab", "sect", None),
        P("sect", None, None),
    )
    out_specs = (P(None, "slab", "sect", None), P("sect", "slab", None, None))
    return jax.shard_map(body, mesh=mesh, in_specs=in_specs, out_specs=out_specs, check_vma=False)
```

```python
import functools
import math
from typing import NamedTuple

import jax
import jax.numpy as jnp
from jax import lax
from jax.experimental import pallas as pl
from jax.experimental.pallas import tpu as pltpu
from jax.sharding import PartitionSpec as P

STRIDE = 32
BAND = 512

GAMMA = 5.0 / 3.0
COURANT = 0.15
TURBULENT = 0.25
NORMALISE = 0.5641895835477563

LANES = 128
ROWS = 8
FIELDS = 5
UNROLL = 64
PACK_COST = 30_000
PREPARE_COST = 300
MERGE_COST = 30_000
HOLD_COST = 1

VMEM = pl.BlockSpec(memory_space=pltpu.VMEM)


HBM = pl.BlockSpec(memory_space=pltpu.HBM)


class Message(NamedTuple):
    owners: int
    slots: int
    group: int
    rows: int
    part: int
    main: int
    extra: int
    fold: int
    extra_rows: int
    count: int


def shape_of_message(nx, owners, slots, group):
    rows, part = slots // group, nx * group
    main = min(2 * FIELDS, LANES // part)
    extra = 2 * FIELDS - main
    fold = min(rows, LANES // (extra * part)) if extra else 1
    extra_rows = rows // fold if extra else 0
    count = 2 * rows + 2 * extra_rows + ROWS
    return Message(owners, slots, group, rows, part, main, extra, fold, extra_rows, count)


def call(kernel, out_shapes, name, flops, scratch=(), in_specs=None, out_specs=None):
    more = {} if in_specs is None else {"in_specs": in_specs}
    return pl.pallas_call(
        kernel,
        out_shape=[
            jax.ShapeDtypeStruct(*s) if isinstance(s[0], tuple) else jax.ShapeDtypeStruct(s, jnp.float32)
            for s in out_shapes
        ],
        out_specs=out_specs or [VMEM] * len(out_shapes),
        **more,
        scratch_shapes=list(scratch),
        compiler_params=pltpu.CompilerParams(vmem_limit_bytes=24 * 1024 * 1024),
        cost_estimate=pl.CostEstimate(flops=flops, bytes_accessed=1 << 20, transcendentals=0),
        name=name,
    )


def shift(array, amount, axis):
    size = array.shape[axis]
    amount = amount % size
    return array if amount == 0 else pltpu.roll(array, amount, axis)


def derived(cell):
    r, u, v, w, p = cell
    m = (r * u, r * v, r * w)
    energy = p * (1.0 / (GAMMA - 1.0)) + 0.5 * (m[0] * u + m[1] * v + m[2] * w)
    sound = jnp.sqrt(GAMMA * p / r)
    return (r, *m, energy), sound


def flux_parts(cell, state, sound, d):
    moving = cell[1 + d]
    flux = [state[1 + d]]
    for k in range(3):
        term = state[1 + k] * moving
        flux.append(term + cell[4] if k == d else term)
    flux.append((state[4] + cell[4]) * moving)
    return (*state, *flux, jnp.abs(moving) + sound)


def face(left, right):
    speed = jnp.maximum(left[10], right[10])
    return [
        (left[5 + k] + right[5 + k]) - speed * (right[k] - left[k]) for k in range(FIELDS)
    ]


def fields_of(r_ref, v_ref, p_ref, index):
    total = r_ref.shape[0]
    first = index.start if isinstance(index, pl.Slice) else index
    out = [r_ref[index]]
    for k in range(3):
        if isinstance(index, pl.Slice):
            out.append(v_ref[pl.ds(k * total + first, index.size, index.stride)])
        else:
            out.append(v_ref[k * total + index])
    out.append(p_ref[index])
    return out


def place_of(direct):
    me = lax.axis_index("slab")
    return (me // 2 if direct else 0), me % 2


def is_odd(axis, shape):
    return jnp.full(shape, lax.axis_index(axis) % 2) == 1


def sides(near, far, axis):
    odd = is_odd(axis, near[0].shape)
    low = [jnp.where(odd, n, f) for n, f in zip(near, far)]
    high = [jnp.where(odd, f, n) for n, f in zip(near, far)]
    return low, high


def edges_kernel(
    sizes, r_hbm, v_hbm, p_hbm, o_hbm, x_first, x_last, y_near, y_far, top_ref, r_ref, v_ref, p_ref, o_ref, sems
):
    nx, ny, nz = sizes
    pairs = [(r_hbm, r_ref), (v_hbm, v_ref), (p_hbm, p_ref), (o_hbm, o_ref)]
    loads = [pltpu.make_async_copy(source, target, sems.at[i]) for i, (source, target) in enumerate(pairs)]
    for load in loads:
        load.start()
    for load in loads:
        load.wait()
    for out, x in ((x_first, 0), (x_last, nx - 1)):
        for f, value in enumerate(fields_of(r_ref, v_ref, p_ref, pl.ds(x * ny, ny))):
            out[f] = value
    first, last = (fields_of(r_ref, v_ref, p_ref, pl.ds(y, nx, ny)) for y in (0, ny - 1))
    far, near = sides(last, first, "sect")
    for f in range(FIELDS):
        y_near[f] = near[f]
        y_far[f] = far[f]
    top = jnp.zeros((ROWS, nz), jnp.float32)
    for row in range(0, nx * ny, ROWS):
        r, u, v, w, p = fields_of(r_ref, v_ref, p_ref, pl.ds(row, ROWS))
        speed = jnp.maximum(jnp.maximum(jnp.abs(u), jnp.abs(v)), jnp.abs(w)) + jnp.sqrt(GAMMA * p / r)
        top = jnp.maximum(top, speed)
    y_near[FIELDS] = top
    top_ref[...] = top


def join_kernel(y_far, top_ref, near_ref, target_ref, out_ref, target_out):
    for f in range(FIELDS):
        out_ref[f] = y_far[f]
    out_ref[FIELDS] = jnp.maximum(top_ref[...], near_ref[FIELDS])
    target_out[...] = target_ref[...]


def spread_rows(msg):
    return LANES + msg.extra * msg.part


def prepare_kernel(sizes, msg, r_ref, v_ref, p_ref, owner_ref, cell_ref, change_ref, target_ref):
    nx, ny, nz = sizes
    lines = nz // STRIDE
    columns = ny * lines
    step = STRIDE // ROWS
    lane = lax.broadcasted_iota(jnp.int32, (nx, nz), 1)
    for t in range(step):
        cell = None
        for s in range(ny // step):
            rows = fields_of(r_ref, v_ref, p_ref, pl.ds(step * s + t, nx, ny))
            rows = [shift(a, step * s, 1) for a in rows]
            if cell is None:
                cell = rows
            else:
                mine = (lane - step * s + 1) % STRIDE < 3
                cell = [jnp.where(mine, a, b) for a, b in zip(rows, cell)]
        here = flux_parts(cell, *derived(cell), 2)
        after = face(here, [shift(a, -1, 1) for a in here])
        for f in range(FIELDS):
            cell_ref[t, f] = cell[f]
            change_ref[t, f] = after[f] - shift(after[f], 1, 1)
    owner = jnp.concatenate([owner_ref[k] for k in range(lines)], axis=1).astype(jnp.float32)
    own = jnp.broadcast_to(owner, (columns, columns))
    own_t = own.T

    def place(dim):
        at = lax.broadcasted_iota(jnp.int32, (columns, columns), dim)
        return (at % ny) * lines + at // ny

    ahead = (own == own_t) & (place(0) < place(1))
    rank = jnp.sum(jnp.where(ahead, 1.0, 0.0), axis=0, keepdims=True)
    target_ref[...] = jnp.broadcast_to(owner * msg.slots + rank, target_ref.shape)


def pack_kernel(sizes, msg, n_far, direct, cell_ref, change_ref, target_ref, y_near, y_far, top_ref, x_first, *rest):
    nx, ny, nz = sizes
    slots, group, width = msg.slots, msg.group, spread_rows(msg)
    far, x_out, outs, spread = rest[:n_far], rest[n_far], rest[n_far + 1 : -1], rest[-1]
    x_out[...] = x_first[...]
    y_low, y_high = sides([y_near[f] for f in range(FIELDS)], [y_far[f] for f in range(FIELDS)], "sect")
    columns = ny * (nz // STRIDE)
    step = STRIDE // ROWS
    lane = lax.broadcasted_iota(jnp.int32, (nx, nz), 1)
    target = target_ref[0:1]
    tiles = [[cell_ref[t, f] for f in range(FIELDS)] for t in range(step)]
    first = lane % STRIDE < step
    last = lane % STRIDE >= ny - step
    below = [jnp.where(first, y_low[f], shift(a, step, 1)) for f, a in enumerate(tiles[-1])]
    above = [jnp.where(last, shift(y_high[f], ny - step, 1), shift(a, -step, 1)) for f, a in enumerate(tiles[0])]
    parts = [flux_parts(cell, *derived(cell), 1) for cell in (below, *tiles, above)]
    faces = [face(a, b) for a, b in zip(parts, parts[1:])]
    dense = None
    for t in range(step):
        total = [(high - low) + change_ref[t, f] for f, (low, high) in enumerate(zip(faces[t], faces[t + 1]))]
        values = [shift(a, t, 1) for a in [*tiles[t], *total]]
        dense = values if dense is None else [jnp.where(lane % step == t, a, b) for a, b in zip(values, dense)]
    spread[...] = jnp.zeros_like(spread)
    for f, value in enumerate(dense):
        for h in range(group):
            spread[pl.ds(h * width + f * nx * group + h, nx, group), :] = value
    z_me, y_me = place_of(direct)

    def chosen(rows, first):
        row = lax.broadcasted_iota(jnp.int32, (msg.owners * rows, columns), 0)
        block = row // rows
        own_of = 2 * ((block // 2) ^ z_me) + ((block % 2) ^ y_me)
        out = []
        for h in range(group):
            slot = (own_of * slots + (first + row % rows) * group + h).astype(jnp.float32)
            out.append(jnp.where(slot == target, 1.0, 0.0))
        return jnp.concatenate(out, axis=1).astype(jnp.bfloat16)

    def pieces(first, count):
        value = jnp.concatenate([spread[pl.ds(h * width + first, count), :] for h in range(group)], axis=1)
        out = []
        for _ in range(3):
            out.append(value.astype(jnp.bfloat16))
            value = value - out[-1].astype(jnp.float32)
        return jnp.concatenate(out, axis=1)

    def pick(selection, values):
        selection = jnp.concatenate([selection] * 3, axis=1)
        return lax.dot_general(selection, values, (((1,), (1,)), ((), ())), preferred_element_type=jnp.float32)

    per = msg.count
    each = msg.owners // len(outs)
    picked = pick(chosen(msg.rows, 0), pieces(0, LANES))
    for b in range(msg.owners):
        at = (b % each) // 2 * per + b % 2 * msg.rows
        outs[b // each][pl.ds(at, msg.rows), :] = picked[b * msg.rows : (b + 1) * msg.rows]
    if msg.extra:
        values = pieces(LANES, msg.extra * msg.part)
        rows = msg.extra_rows
        picked = jnp.concatenate([pick(chosen(rows, a * rows), values) for a in range(msg.fold)], axis=1)
        for b in range(msg.owners):
            at = (b % each) // 2 * per + 2 * msg.rows + b % 2 * rows
            outs[b // each][pl.ds(at, rows), :] = picked[b * rows : (b + 1) * rows]
    top = jnp.maximum(jnp.maximum(top_ref[...], y_near[FIELDS]), y_far[FIELDS])
    for ref in far:
        top = jnp.maximum(top, ref[...])
    for out in outs:
        for d in range(each // 2):
            out[pl.ds((d + 1) * per - ROWS, ROWS), :] = top


def merge_kernel(msg, firsts, *refs):
    *refs, other_ref, own_ref = refs
    half, top = msg.owners // 2, None
    for first, ref in zip(firsts, refs):
        for d in range(ref.shape[0] // msg.count):
            at, to = d * msg.count, first + d
            for odd, out in ((0, own_ref), (1, other_ref)):
                out[pl.ds(to * msg.rows, msg.rows), :] = ref[pl.ds(at + odd * msg.rows, msg.rows), :]
                if msg.extra:
                    rows = msg.extra_rows
                    out[pl.ds(half * msg.rows + to * rows, rows), :] = ref[
                        pl.ds(at + 2 * msg.rows + odd * rows, rows), :
                    ]
            new = ref[pl.ds(at + msg.count - ROWS, ROWS), :]
            top = new if top is None else jnp.maximum(top, new)
    for out in (own_ref, other_ref):
        out[pl.ds(half * (msg.rows + msg.extra_rows), ROWS), :] = top


def hold_kernel(first_ref, second_ref, first_out, second_out):
    first_out[...] = first_ref[...]
    second_out[...] = second_ref[...]


def change_kernel(sizes, r_ref, v_ref, p_ref, x_low, x_high, y_near, y_far, out_ref):
    nx, ny, nz = sizes
    every = range(FIELDS)
    y_low, y_high = sides([y_near[f] for f in every], [y_far[f] for f in every], "sect")
    row = lax.broadcasted_iota(jnp.int32, (ny, nz), 0)
    half = 0.5

    def layer(x):
        if x < 0:
            return [x_low[f] for f in range(FIELDS)]
        if x >= nx:
            return [x_high[f] for f in range(FIELDS)]
        return fields_of(r_ref, v_ref, p_ref, pl.ds(x * ny, ny))

    def prepared(x):
        cell = layer(x)
        state, sound = derived(cell)
        return cell, state, sound, flux_parts(cell, state, sound, 0)

    previous = prepared(-1)
    here = prepared(0)
    x_face = face(previous[3], here[3])
    for x in range(nx):
        following = prepared(x + 1)
        cell, state, sound, parts = here
        next_face = face(parts, following[3])
        total = [a - b for a, b in zip(next_face, x_face)]
        x_face = next_face
        low_cell = [y_low[f][x : x + 1] for f in range(FIELDS)]
        high_cell = [y_high[f][x : x + 1] for f in range(FIELDS)]
        low = flux_parts(low_cell, *derived(low_cell), 1)
        high = flux_parts(high_cell, *derived(high_cell), 1)
        parts = flux_parts(cell, state, sound, 1)
        plus = [jnp.where(row == ny - 1, h, shift(a, -1, 0)) for a, h in zip(parts, high)]
        after = face(parts, plus)
        edge = face(low, [a[0:1] for a in parts])
        before = [jnp.where(row == 0, e, shift(a, 1, 0)) for a, e in zip(after, edge)]
        total = [t + (a - b) for t, a, b in zip(total, after, before)]
        parts = flux_parts(cell, state, sound, 2)
        after = face(parts, [shift(a, -1, 1) for a in parts])
        total = [t + (a - shift(a, 1, 1)) for t, a in zip(total, after)]
        for f in range(FIELDS):
            out_ref[f, pl.ds(x * ny, ny), :] = half * total[f]
        here = following


def final_kernel(sizes, msg, direct, r_ref, v_ref, p_ref, change_ref, other_ref, own_ref, kept_ref, *rest):
    new_hbm, depth_hbm, new_ref, depth_ref, main_ref, extra_ref, sems = rest
    nx, ny, nz = sizes
    n_owner, group, part = msg.owners, msg.group, msg.part
    half, length = n_owner // 2, nx * n_owner
    at = pl.ds(half * (msg.rows + msg.extra_rows), ROWS)
    top = jnp.maximum(other_ref[at, :], own_ref[at, :])
    step = COURANT / jnp.max(top, keepdims=True)
    writes = []
    for x in range(nx):
        rows = pl.ds(x * ny, ny)
        state, _ = derived(fields_of(r_ref, v_ref, p_ref, rows))
        for f in range(FIELDS):
            new_ref[f, rows, :] = state[f] - step * change_ref[f, rows, :]
        writes.append(pltpu.make_async_copy(new_ref.at[:, rows], new_hbm.at[:, rows], sems.at[x]))
        writes[-1].start()
    z_me, y_me = place_of(direct)

    def settle(source, at, extra_at, d, odd):
        owner = 2 * (d ^ z_me) + (odd ^ y_me)
        main_ref[owner] = source[pl.ds(at, msg.rows), :]
        if msg.extra:
            extra_ref[owner] = source[pl.ds(extra_at, msg.extra_rows), :]

    for d in range(half):
        extra_at = half * msg.rows + d * msg.extra_rows
        if direct and d == 0:
            settle(kept_ref, 0, 2 * msg.rows, 0, 0)
        else:
            settle(own_ref, d * msg.rows, extra_at, d, 0)
        settle(other_ref, d * msg.rows, extra_at, d, 1)
    line = []
    for f in range(msg.main):
        line.append(jnp.concatenate([main_ref[q, :, pl.ds(f * part, part)] for q in range(n_owner)], axis=1))
    for f in range(msg.extra):
        folds = []
        for a in range(msg.fold):
            at = pl.ds((a * msg.extra + f) * part, part)
            folds.append(jnp.concatenate([extra_ref[q, :, at] for q in range(n_owner)], axis=1))
        line.append(jnp.concatenate(folds, axis=0))
    cell, change = line[:FIELDS], line[FIELDS:]
    taken = cell[0] > 0.0
    cell[0] = jnp.where(taken, cell[0], 1.0)
    state, sound = derived(cell)
    parts = flux_parts(cell, state, sound, 0)
    after = face(parts, [shift(a, -group, 1) for a in parts])
    change = [c + (a - shift(a, group, 1)) for c, a in zip(change, after)]
    new = [s - (0.5 * step) * c for s, c in zip(state, change)]
    density = new[0]
    pressure = (GAMMA - 1.0) * (new[4] - 0.5 * (new[1] * new[1] + new[2] * new[2] + new[3] * new[3]) / density)
    broadening = TURBULENT + pressure / density
    inverse = 1.0 / (BAND / 64.0 * jnp.sqrt(broadening))
    amplitude = NORMALISE * (density * density) * jnp.exp(-0.7 * jnp.log(broadening)) * inverse
    amplitude = jnp.where(taken, amplitude, 0.0)
    scaled = inverse * math.sqrt(math.log2(math.e))
    centre = (BAND / 8.0) * (new[1] / density)
    turns = BAND // length
    block = min(length, UNROLL)

    def skewers(rows):
        scale, middle, size = scaled[:rows], centre[:rows], amplitude[:rows]
        strides = [scale * float(length * m) for m in range(turns)]

        def offsets(count, running):
            e = (length - block - block * count) * 1.0 - float(BAND // 2)
            for b in range(block):
                start = (e + float(b) - middle) * scale
                total = None
                for m in range(turns):
                    t = start + strides[m] if m else start
                    value = jnp.exp2(-(t * t))
                    total = value if total is None else total + value
                part = shift(size * total, b * group, 1)
                block_sum = part if b == 0 else block_sum + part
            return block_sum if running is None else shift(running, block * group, 1) + block_sum

        if length == block:
            running = offsets(0, None)
        else:
            running = lax.fori_loop(
                0,
                length // block,
                lambda i, c: offsets(i.astype(jnp.float32), c),
                jnp.zeros_like(size),
            )
        running = shift(running, -(BAND // 2) * group, 1)
        if group > 1:
            wide = jnp.broadcast_to(running[:, None, :], (rows, group, group * length))
            wide = wide.reshape(rows * group, group * length)
            at = lax.broadcasted_iota(jnp.int32, wide.shape, 1)
            of = lax.broadcasted_iota(jnp.int32, wide.shape, 0)
            wide = jnp.where(at % group == of % group, wide, 0.0)
            at = lax.broadcasted_iota(jnp.int32, (group * length, length), 0)
            of = lax.broadcasted_iota(jnp.int32, (group * length, length), 1)
            pick = jnp.where(at // group == of, 1.0, 0.0)
            running = jnp.dot(wide, pick, precision=lax.Precision.HIGHEST, preferred_element_type=jnp.float32)
        depth_ref[pl.ds(0, rows * group), :] = running

    if msg.rows > ROWS:
        more = jnp.max(jnp.where(taken[ROWS:], 1.0, 0.0)) > 0.0

        @pl.when(more)
        def _():
            skewers(msg.rows)

        @pl.when(jnp.logical_not(more))
        def _():
            depth_ref[...] = jnp.zeros_like(depth_ref)
            skewers(ROWS)

    else:
        skewers(msg.rows)
    writes.append(pltpu.make_async_copy(depth_ref, depth_hbm, sems.at[nx]))
    writes[-1].start()
    for write in writes:
        write.wait()


def around(value, axis, amount):
    count = lax.axis_size(axis)
    return lax.ppermute(value, axis, [(i, (i + amount) % count) for i in range(count)])


def to_partner(value, axis, bits):
    return lax.ppermute(value, axis, [(i, i ^ bits) for i in range(lax.axis_size(axis))])


def crossed(value, bits):
    count = lax.axis_size("slab")
    every = [(s, q) for s in range(lax.axis_size("sect")) for q in range(count)]
    pairs = [(s * count + q, (s ^ 1) * count + (q ^ bits)) for s, q in every]
    return lax.ppermute(value, ("sect", "slab"), pairs)


def to_other(value, axis):
    count = lax.axis_size(axis)
    return lax.ppermute(value, axis, [(i, (i + 2 * (i % 2) - 1) % count) for i in range(count)])


def body(density, velocity, pressure, owners):
    sizes = nx, ny, nz = density.shape
    n_sect, n_slab = lax.axis_size("sect"), lax.axis_size("slab")
    lines = nz // STRIDE
    columns = ny * lines
    slots = 2 * columns // n_slab
    length = nx * n_slab
    group = max(1, LANES // length)
    geometry = shape_of_message(nx, n_slab, slots, group)
    gas = (
        density.reshape(nx * ny, nz),
        velocity.reshape(3 * nx * ny, nz),
        pressure.reshape(nx * ny, nz),
    )
    cells = nx * ny * nz
    half = n_slab // 2
    direct = half <= 4
    x_edge, y_edge, row = (FIELDS, ny, nz), (FIELDS + 1, nx, nz), (ROWS, nz)
    owners = jnp.transpose(owners, (1, 2, 0))
    shapes = [(a.shape, a.dtype) for a in (*gas, owners)]
    x_first, x_last, y_near, y_far, top, *gas, owners = call(
        functools.partial(edges_kernel, sizes),
        [x_edge, x_edge, y_edge, (FIELDS, nx, nz), row, *shapes],
        "edges",
        20 * cells,
        [pltpu.SemaphoreType.DMA((4,))],
        in_specs=[HBM] * 4,
    )(*(pltpu.with_memory_space_constraint(a, pltpu.HBM) for a in (*gas, owners)))
    tiles = (STRIDE // ROWS, FIELDS, nx, nz)
    cells_at, change_at, target = call(
        functools.partial(prepare_kernel, sizes, geometry),
        [tiles, tiles, (ROWS, columns)],
        "prepare",
        PREPARE_COST * cells,
    )(*gas, owners)
    y_near = to_partner(y_near, "sect", 1)
    y_far, target = call(join_kernel, [y_edge, (ROWS, columns)], "join", cells)(y_far, top, y_near, target)
    y_far = to_other(y_far, "sect")
    far = [around(top, "sect", d) for d in range(2, n_sect - 1)] if n_sect > 4 else []
    x_low = around(x_last, "slab", 1)
    firsts = range(half) if direct else range(1)
    x_first, *packed = call(
        functools.partial(pack_kernel, sizes, geometry, len(far), direct),
        [x_edge] + [(half // len(firsts) * geometry.count, LANES)] * len(firsts),
        "pack",
        PACK_COST * cells,
        [pltpu.VMEM((group * spread_rows(geometry), columns), jnp.float32)],
    )(cells_at, change_at, target, y_near, y_far, top, x_first, *far)
    merge = functools.partial(
        call,
        out_shapes=[(half * (geometry.rows + geometry.extra_rows) + ROWS, LANES)] * 2,
        name="merge",
        flops=MERGE_COST * cells,
    )
    if direct:
        arrived = [crossed(m, 2 * d) for d, m in zip(firsts, packed)]
        turn = [2, 3, 1, 0] if half == 4 else list(firsts)
        other, own = merge(functools.partial(merge_kernel, geometry, turn))(*(arrived[d] for d in turn))
        other, own = crossed(other, 1), crossed(own, 0)
    else:
        alike = [[2 * i + odd for i in range(half)] for odd in range(2)]
        arrived = [
            lax.all_to_all(m, "slab", split_axis=0, concat_axis=0, axis_index_groups=alike, tiled=True) for m in packed
        ]
        other, own = merge(functools.partial(merge_kernel, geometry, firsts))(*arrived)
        other = to_partner(other, "slab", 1)
    x_low, x_first = call(hold_kernel, [x_edge] * 2, "hold", HOLD_COST * cells)(x_low, x_first)
    x_high = around(x_first, "slab", -1)
    (change,) = call(
        functools.partial(change_kernel, sizes),
        [(FIELDS, nx * ny, nz)],
        "change",
        300_000 * cells,
    )(*gas, x_low, x_high, y_near, y_far)
    new_state, depth = call(
        functools.partial(final_kernel, sizes, geometry, direct),
        [(FIELDS, nx * ny, nz), (slots, length)],
        "final",
        100 * cells,
        [
            pltpu.VMEM((FIELDS, nx * ny, nz), jnp.float32),
            pltpu.VMEM((slots, length), jnp.float32),
            pltpu.VMEM((n_slab, geometry.rows, LANES), jnp.float32),
            pltpu.VMEM((n_slab, max(1, geometry.extra_rows), LANES), jnp.float32),
            pltpu.SemaphoreType.DMA((nx + 1,)),
        ],
        out_specs=[HBM, HBM],
    )(*gas, change, other, own, packed[0])
    return (new_state.reshape(FIELDS, nx, ny, nz), depth.reshape(1, 1, slots, length))


def solution(mesh):
    in_specs = (
        P("slab", "sect", None),
        P(None, "slab", "sect", None),
        P("slab", "sect", None),
        P("sect", None, None),
    )
    out_specs = (P(None, "slab", "sect", None), P("sect", "slab", None, None))
    return jax.shard_map(body, mesh=mesh, in_specs=in_specs, out_specs=out_specs, check_vma=False)
```

```python
import functools
import math
from typing import NamedTuple

import jax
import jax.numpy as jnp
from jax import lax
from jax.experimental import pallas as pl
from jax.experimental.pallas import tpu as pltpu
from jax.sharding import PartitionSpec as P

STRIDE = 32
BAND = 512

GAMMA = 5.0 / 3.0
COURANT = 0.15
TURBULENT = 0.25
NORMALISE = 0.5641895835477563

LANES = 128
ROWS = 8
FIELDS = 5
UNROLL = 64
PACK_COST = 30_000
PREPARE_COST = 300
SELECT_COST = 300
PIECES = 3
MERGE_COST = 30_000
HOLD_COST = 1

VMEM = pl.BlockSpec(memory_space=pltpu.VMEM)


HBM = pl.BlockSpec(memory_space=pltpu.HBM)


class Message(NamedTuple):
    owners: int
    slots: int
    group: int
    rows: int
    part: int
    main: int
    extra: int
    fold: int
    extra_rows: int
    count: int


def shape_of_message(nx, owners, slots, group):
    rows, part = slots // group, nx * group
    main = min(2 * FIELDS, LANES // part)
    extra = 2 * FIELDS - main
    fold = min(rows, LANES // (extra * part)) if extra else 1
    extra_rows = rows // fold if extra else 0
    count = 2 * rows + 2 * extra_rows + ROWS
    return Message(owners, slots, group, rows, part, main, extra, fold, extra_rows, count)


def call(kernel, out_shapes, name, flops, scratch=(), in_specs=None, out_specs=None):
    more = {} if in_specs is None else {"in_specs": in_specs}
    return pl.pallas_call(
        kernel,
        out_shape=[
            jax.ShapeDtypeStruct(*s) if isinstance(s[0], tuple) else jax.ShapeDtypeStruct(s, jnp.float32)
            for s in out_shapes
        ],
        out_specs=out_specs or [VMEM] * len(out_shapes),
        **more,
        scratch_shapes=list(scratch),
        compiler_params=pltpu.CompilerParams(vmem_limit_bytes=24 * 1024 * 1024),
        cost_estimate=pl.CostEstimate(flops=flops, bytes_accessed=1 << 20, transcendentals=0),
        name=name,
    )


def shift(array, amount, axis):
    size = array.shape[axis]
    amount = amount % size
    return array if amount == 0 else pltpu.roll(array, amount, axis)


def derived(cell):
    r, u, v, w, p = cell
    m = (r * u, r * v, r * w)
    energy = p * (1.0 / (GAMMA - 1.0)) + 0.5 * (m[0] * u + m[1] * v + m[2] * w)
    sound = jnp.sqrt(GAMMA * p / r)
    return (r, *m, energy), sound


def flux_parts(cell, state, sound, d):
    moving = cell[1 + d]
    flux = [state[1 + d]]
    for k in range(3):
        term = state[1 + k] * moving
        flux.append(term + cell[4] if k == d else term)
    flux.append((state[4] + cell[4]) * moving)
    return (*state, *flux, jnp.abs(moving) + sound)


def face(left, right):
    speed = jnp.maximum(left[10], right[10])
    return [
        (left[5 + k] + right[5 + k]) - speed * (right[k] - left[k]) for k in range(FIELDS)
    ]


def fields_of(r_ref, v_ref, p_ref, index):
    total = r_ref.shape[0]
    first = index.start if isinstance(index, pl.Slice) else index
    out = [r_ref[index]]
    for k in range(3):
        if isinstance(index, pl.Slice):
            out.append(v_ref[pl.ds(k * total + first, index.size, index.stride)])
        else:
            out.append(v_ref[k * total + index])
    out.append(p_ref[index])
    return out


def place_of(direct):
    me = lax.axis_index("slab")
    return (me // 2 if direct else 0), me % 2


def is_odd(axis, shape):
    return jnp.full(shape, lax.axis_index(axis) % 2) == 1


def sides(near, far, axis):
    odd = is_odd(axis, near[0].shape)
    low = [jnp.where(odd, n, f) for n, f in zip(near, far)]
    high = [jnp.where(odd, f, n) for n, f in zip(near, far)]
    return low, high


def edges_kernel(
    sizes, r_hbm, v_hbm, p_hbm, o_hbm, x_first, x_last, y_near, y_far, top_ref, r_ref, v_ref, p_ref, o_ref, sems
):
    nx, ny, nz = sizes
    pairs = [(r_hbm, r_ref), (v_hbm, v_ref), (p_hbm, p_ref), (o_hbm, o_ref)]
    loads = [pltpu.make_async_copy(source, target, sems.at[i]) for i, (source, target) in enumerate(pairs)]
    for load in loads:
        load.start()
    for load in loads:
        load.wait()
    for out, x in ((x_first, 0), (x_last, nx - 1)):
        for f, value in enumerate(fields_of(r_ref, v_ref, p_ref, pl.ds(x * ny, ny))):
            out[f] = value
    first, last = (fields_of(r_ref, v_ref, p_ref, pl.ds(y, nx, ny)) for y in (0, ny - 1))
    far, near = sides(last, first, "sect")
    for f in range(FIELDS):
        y_near[f] = near[f]
        y_far[f] = far[f]
    top = jnp.zeros((ROWS, nz), jnp.float32)
    for row in range(0, nx * ny, ROWS):
        r, u, v, w, p = fields_of(r_ref, v_ref, p_ref, pl.ds(row, ROWS))
        speed = jnp.maximum(jnp.maximum(jnp.abs(u), jnp.abs(v)), jnp.abs(w)) + jnp.sqrt(GAMMA * p / r)
        top = jnp.maximum(top, speed)
    y_near[FIELDS] = top
    top_ref[...] = top


def join_kernel(y_far, top_ref, near_ref, edge_ref, out_ref, edge_out):
    for f in range(FIELDS):
        out_ref[f] = y_far[f]
    out_ref[FIELDS] = jnp.maximum(top_ref[...], near_ref[FIELDS])
    edge_out[...] = edge_ref[...]


def spread_rows(msg):
    return LANES + msg.extra * msg.part


def prepare_kernel(sizes, msg, r_ref, v_ref, p_ref, owner_ref, spread, edge_ref, target_ref):
    nx, ny, nz = sizes
    lines = nz // STRIDE
    columns = ny * lines
    step = STRIDE // ROWS
    lane = lax.broadcasted_iota(jnp.int32, (nx, nz), 1)
    first = lane % STRIDE < step
    last = lane % STRIDE >= ny - step
    tiles, changes, parts = [], [], []
    for t in range(step):
        cell = None
        for s in range(ny // step):
            rows = fields_of(r_ref, v_ref, p_ref, pl.ds(step * s + t, nx, ny))
            rows = [shift(a, step * s, 1) for a in rows]
            if cell is None:
                cell = rows
            else:
                mine = (lane - step * s + 1) % STRIDE < 3
                cell = [jnp.where(mine, a, b) for a, b in zip(rows, cell)]
        state, sound = derived(cell)
        here = flux_parts(cell, state, sound, 2)
        after = face(here, [shift(a, -1, 1) for a in here])
        tiles.append(cell)
        changes.append([a - shift(a, 1, 1) for a in after])
        parts.append(flux_parts(cell, state, sound, 1))
    inner = [face(a, b) for a, b in zip(parts, parts[1:])]
    around_face = face([shift(a, step, 1) for a in parts[-1]], parts[0])
    low = [jnp.where(first, 0.0, a) for a in around_face]
    high = [jnp.where(last, 0.0, shift(a, -step, 1)) for a in around_face]
    faces = [low, *inner, high]
    dense = None
    for t in range(step):
        total = [c + (b - a) for c, a, b in zip(changes[t], faces[t], faces[t + 1])]
        values = [shift(a, t, 1) for a in [*tiles[t], *total]]
        dense = values if dense is None else [jnp.where(lane % step == t, a, b) for a, b in zip(values, dense)]
    group, width = msg.group, spread_rows(msg)
    spread[...] = jnp.zeros_like(spread)
    for f, value in enumerate(dense):
        for h in range(group):
            spread[pl.ds(h * width + f * nx * group + h, nx, group), :] = value
    for i, (a, b) in enumerate(zip(parts[0], parts[-1])):
        edge_ref[0, i] = a
        edge_ref[1, i] = shift(b, step - ny, 1)
    owner = jnp.concatenate([owner_ref[k] for k in range(lines)], axis=1).astype(jnp.float32)
    own = jnp.broadcast_to(owner, (columns, columns))
    own_t = own.T

    def place(dim):
        at = lax.broadcasted_iota(jnp.int32, (columns, columns), dim)
        return (at % ny) * lines + at // ny

    ahead = (own == own_t) & (place(0) < place(1))
    rank = jnp.sum(jnp.where(ahead, 1.0, 0.0), axis=0, keepdims=True)
    target_ref[...] = jnp.broadcast_to(owner * msg.slots + rank, target_ref.shape)


def lane_of(side, piece, place, group):
    return (side * PIECES + piece) * group + place


def product(selection, values):
    return lax.dot_general(
        selection.astype(jnp.bfloat16), values, (((1,), (1,)), ((), ())), preferred_element_type=jnp.float32
    )


def folded(msg, picked):
    every = msg.owners * msg.extra_rows
    return jnp.concatenate([picked[a * every : (a + 1) * every] for a in range(msg.fold)], axis=1)


def select_kernel(sizes, msg, direct, spread, edge_ref, target_ref, edge_out, *outs):
    _, ny, nz = sizes
    group, width, columns = msg.group, spread_rows(msg), ny * (nz // STRIDE)
    edge_out[...] = edge_ref[...]
    target = target_ref[0:1]
    z_me, y_me = place_of(direct)
    at = lax.broadcasted_iota(jnp.int32, (1, columns), 1) % ny
    edges = jnp.full((1, columns), -1.0)
    for side, y in enumerate((0, ny - 1)):
        for p in range(PIECES):
            for h in range(group):
                some = jnp.where(at == y, target - float(h), -1.0)
                edges = jnp.maximum(edges, shift(some, lane_of(side, p, h, group) - y, 1))

    def slot_of(rows, first):
        row = lax.broadcasted_iota(jnp.int32, (msg.owners * rows, columns), 0)
        block = row // rows
        own_of = 2 * ((block // 2) ^ z_me) + ((block % 2) ^ y_me)
        return (own_of * msg.slots + (first + row % rows) * group).astype(jnp.float32)

    def pick(rows, folds, first, count):
        slot = jnp.concatenate([slot_of(rows, a * rows) for a in range(folds)], axis=0)
        every = [jnp.where(slot == target - float(h), 1.0, 0.0) for h in range(group)]
        every = jnp.concatenate(every, axis=1).astype(jnp.bfloat16)
        value = jnp.concatenate([spread[pl.ds(h * width + first, count), :] for h in range(group)], axis=1)
        out = []
        for _ in range(PIECES):
            out.append(value.astype(jnp.bfloat16))
            value = value - out[-1].astype(jnp.float32)
        picked = product(jnp.concatenate([every] * PIECES, axis=1), jnp.concatenate(out, axis=1))
        return picked, jnp.where(slot == edges, 1.0, 0.0)

    outs[0][...], outs[1][...] = pick(msg.rows, 1, 0, LANES)
    if msg.extra:
        picked, outs[3][...] = pick(msg.extra_rows, msg.fold, LANES, msg.extra * msg.part)
        outs[2][...] = folded(msg, picked)


def pack_kernel(sizes, msg, n_far, edge_ref, y_near, y_far, top_ref, x_first, main_ref, main_edges, *rest):
    nx, ny, nz = sizes
    group = msg.group
    (extra_ref, extra_edges), rest = (rest[:2], rest[2:]) if msg.extra else ((None, None), rest)
    far, x_out, outs, spread = rest[:n_far], rest[n_far], rest[n_far + 1 : -1], rest[-1]
    x_out[...] = x_first[...]
    on = lax.broadcasted_iota(jnp.int32, (nx, nz), 1) % STRIDE == 0
    spread[pl.ds(0, LANES), :] = jnp.zeros((LANES, spread.shape[1]), jnp.float32)
    rows = [[None] * group for _ in range(FIELDS)]
    cells = sides([y_near[f] for f in range(FIELDS)], [y_far[f] for f in range(FIELDS)], "sect")
    for side, cell in enumerate(cells):
        beyond = flux_parts(cell, *derived(cell), 1)
        edge = [edge_ref[side, i] for i in range(len(beyond))]
        faces = face(edge, beyond) if side else [-a for a in face(beyond, edge)]
        for f, value in enumerate(faces):
            value = jnp.where(on, value, 0.0)
            for p in range(PIECES):
                piece = value.astype(jnp.bfloat16).astype(jnp.float32)
                value = value - piece
                for h in range(group):
                    moved = shift(piece, lane_of(side, p, h, group), 1)
                    rows[f][h] = moved if rows[f][h] is None else rows[f][h] + moved
    for f in range(FIELDS):
        for h in range(group):
            spread[pl.ds((FIELDS + f) * nx * group + h, nx, group), :] = rows[f][h]
    top = jnp.maximum(jnp.maximum(top_ref[...], y_near[FIELDS]), y_far[FIELDS])
    for ref in far:
        top = jnp.maximum(top, ref[...])
    top = jnp.broadcast_to(jnp.max(top, keepdims=True), top.shape)
    per = msg.count
    each = msg.owners // len(outs)
    picked = main_ref[...] + product(main_edges[...], spread[pl.ds(0, LANES), :].astype(jnp.bfloat16))
    for b in range(msg.owners):
        at = (b % each) // 2 * per + b % 2 * msg.rows
        outs[b // each][pl.ds(at, msg.rows), :] = picked[b * msg.rows : (b + 1) * msg.rows]
    if msg.extra:
        rows = msg.extra_rows
        values = spread[pl.ds(LANES, msg.extra * msg.part), :].astype(jnp.bfloat16)
        picked = extra_ref[...] + folded(msg, product(extra_edges[...], values))
        for b in range(msg.owners):
            at = (b % each) // 2 * per + 2 * msg.rows + b % 2 * rows
            outs[b // each][pl.ds(at, rows), :] = picked[b * rows : (b + 1) * rows]
    for out in outs:
        for d in range(each // 2):
            out[pl.ds((d + 1) * per - ROWS, ROWS), :] = top


def merge_kernel(msg, firsts, *refs):
    *refs, other_ref, own_ref = refs
    half, top = msg.owners // 2, None
    for first, ref in zip(firsts, refs):
        for d in range(ref.shape[0] // msg.count):
            at, to = d * msg.count, first + d
            for odd, out in ((0, own_ref), (1, other_ref)):
                out[pl.ds(to * msg.rows, msg.rows), :] = ref[pl.ds(at + odd * msg.rows, msg.rows), :]
                if msg.extra:
                    rows = msg.extra_rows
                    out[pl.ds(half * msg.rows + to * rows, rows), :] = ref[
                        pl.ds(at + 2 * msg.rows + odd * rows, rows), :
                    ]
            new = ref[pl.ds(at + msg.count - ROWS, ROWS), :]
            top = new if top is None else jnp.maximum(top, new)
    for out in (own_ref, other_ref):
        out[pl.ds(half * (msg.rows + msg.extra_rows), ROWS), :] = top


def hold_kernel(first_ref, second_ref, first_out, second_out):
    first_out[...] = first_ref[...]
    second_out[...] = second_ref[...]


def change_kernel(sizes, r_ref, v_ref, p_ref, x_low, x_high, y_near, y_far, out_ref):
    nx, ny, nz = sizes
    every = range(FIELDS)
    y_low, y_high = sides([y_near[f] for f in every], [y_far[f] for f in every], "sect")
    row = lax.broadcasted_iota(jnp.int32, (ny, nz), 0)
    half = 0.5

    def layer(x):
        if x < 0:
            return [x_low[f] for f in range(FIELDS)]
        if x >= nx:
            return [x_high[f] for f in range(FIELDS)]
        return fields_of(r_ref, v_ref, p_ref, pl.ds(x * ny, ny))

    def prepared(x):
        cell = layer(x)
        state, sound = derived(cell)
        return cell, state, sound, flux_parts(cell, state, sound, 0)

    previous = prepared(-1)
    here = prepared(0)
    x_face = face(previous[3], here[3])
    for x in range(nx):
        following = prepared(x + 1)
        cell, state, sound, parts = here
        next_face = face(parts, following[3])
        total = [a - b for a, b in zip(next_face, x_face)]
        x_face = next_face
        low_cell = [y_low[f][x : x + 1] for f in range(FIELDS)]
        high_cell = [y_high[f][x : x + 1] for f in range(FIELDS)]
        low = flux_parts(low_cell, *derived(low_cell), 1)
        high = flux_parts(high_cell, *derived(high_cell), 1)
        parts = flux_parts(cell, state, sound, 1)
        plus = [jnp.where(row == ny - 1, h, shift(a, -1, 0)) for a, h in zip(parts, high)]
        after = face(parts, plus)
        edge = face(low, [a[0:1] for a in parts])
        before = [jnp.where(row == 0, e, shift(a, 1, 0)) for a, e in zip(after, edge)]
        total = [t + (a - b) for t, a, b in zip(total, after, before)]
        parts = flux_parts(cell, state, sound, 2)
        after = face(parts, [shift(a, -1, 1) for a in parts])
        total = [t + (a - shift(a, 1, 1)) for t, a in zip(total, after)]
        for f in range(FIELDS):
            out_ref[f, pl.ds(x * ny, ny), :] = half * total[f]
        here = following


def final_kernel(sizes, msg, direct, r_ref, v_ref, p_ref, change_ref, other_ref, own_ref, kept_ref, *rest):
    new_hbm, depth_hbm, new_ref, depth_ref, main_ref, extra_ref, sems = rest
    nx, ny, nz = sizes
    n_owner, group, part = msg.owners, msg.group, msg.part
    half, length = n_owner // 2, nx * n_owner
    at = pl.ds(half * (msg.rows + msg.extra_rows), ROWS)
    top = jnp.maximum(other_ref[at, :], own_ref[at, :])
    step = COURANT / top[0:1, 0:1]
    writes = []
    for x in range(nx):
        rows = pl.ds(x * ny, ny)
        state, _ = derived(fields_of(r_ref, v_ref, p_ref, rows))
        for f in range(FIELDS):
            new_ref[f, rows, :] = state[f] - step * change_ref[f, rows, :]
        writes.append(pltpu.make_async_copy(new_ref.at[:, rows], new_hbm.at[:, rows], sems.at[x]))
        writes[-1].start()
    z_me, y_me = place_of(direct)

    def settle(source, at, extra_at, d, odd):
        owner = 2 * (d ^ z_me) + (odd ^ y_me)
        main_ref[owner] = source[pl.ds(at, msg.rows), :]
        if msg.extra:
            extra_ref[owner] = source[pl.ds(extra_at, msg.extra_rows), :]

    for d in range(half):
        extra_at = half * msg.rows + d * msg.extra_rows
        if direct and d == 0:
            settle(kept_ref, 0, 2 * msg.rows, 0, 0)
        else:
            settle(own_ref, d * msg.rows, extra_at, d, 0)
        settle(other_ref, d * msg.rows, extra_at, d, 1)
    line = []
    for f in range(msg.main):
        line.append(jnp.concatenate([main_ref[q, :, pl.ds(f * part, part)] for q in range(n_owner)], axis=1))
    for f in range(msg.extra):
        folds = []
        for a in range(msg.fold):
            at = pl.ds((a * msg.extra + f) * part, part)
            folds.append(jnp.concatenate([extra_ref[q, :, at] for q in range(n_owner)], axis=1))
        line.append(jnp.concatenate(folds, axis=0))
    cell, change = line[:FIELDS], line[FIELDS:]
    taken = cell[0] > 0.0
    cell[0] = jnp.where(taken, cell[0], 1.0)
    state, sound = derived(cell)
    parts = flux_parts(cell, state, sound, 0)
    after = face(parts, [shift(a, -group, 1) for a in parts])
    change = [c + (a - shift(a, group, 1)) for c, a in zip(change, after)]
    new = [s - (0.5 * step) * c for s, c in zip(state, change)]
    density = new[0]
    pressure = (GAMMA - 1.0) * (new[4] - 0.5 * (new[1] * new[1] + new[2] * new[2] + new[3] * new[3]) / density)
    broadening = TURBULENT + pressure / density
    inverse = 1.0 / (BAND / 64.0 * jnp.sqrt(broadening))
    amplitude = NORMALISE * (density * density) * jnp.exp(-0.7 * jnp.log(broadening)) * inverse
    amplitude = jnp.where(taken, amplitude, 0.0)
    scaled = inverse * math.sqrt(math.log2(math.e))
    centre = (BAND / 8.0) * (new[1] / density)
    turns = BAND // length
    block = min(length, UNROLL)

    def skewers(rows):
        scale, middle, size = scaled[:rows], centre[:rows], amplitude[:rows]
        strides = [scale * float(length * m) for m in range(turns)]

        def offsets(count, running):
            e = (length - block - block * count) * 1.0 - float(BAND // 2)
            for b in range(block):
                start = (e + float(b) - middle) * scale
                total = None
                for m in range(turns):
                    t = start + strides[m] if m else start
                    value = jnp.exp2(-(t * t))
                    total = value if total is None else total + value
                part = shift(size * total, b * group, 1)
                block_sum = part if b == 0 else block_sum + part
            return block_sum if running is None else shift(running, block * group, 1) + block_sum

        if length == block:
            running = offsets(0, None)
        else:
            running = lax.fori_loop(
                0,
                length // block,
                lambda i, c: offsets(i.astype(jnp.float32), c),
                jnp.zeros_like(size),
            )
        running = shift(running, -(BAND // 2) * group, 1)
        if group > 1:
            wide = jnp.broadcast_to(running[:, None, :], (rows, group, group * length))
            wide = wide.reshape(rows * group, group * length)
            at = lax.broadcasted_iota(jnp.int32, wide.shape, 1)
            of = lax.broadcasted_iota(jnp.int32, wide.shape, 0)
            wide = jnp.where(at % group == of % group, wide, 0.0)
            at = lax.broadcasted_iota(jnp.int32, (group * length, length), 0)
            of = lax.broadcasted_iota(jnp.int32, (group * length, length), 1)
            pick = jnp.where(at // group == of, 1.0, 0.0)
            running = jnp.dot(wide, pick, precision=lax.Precision.HIGHEST, preferred_element_type=jnp.float32)
        depth_ref[pl.ds(0, rows * group), :] = running

    if msg.rows > ROWS:
        more = jnp.max(jnp.where(taken[ROWS:], 1.0, 0.0)) > 0.0

        @pl.when(more)
        def _():
            skewers(msg.rows)

        @pl.when(jnp.logical_not(more))
        def _():
            depth_ref[...] = jnp.zeros_like(depth_ref)
            skewers(ROWS)

    else:
        skewers(msg.rows)
    writes.append(pltpu.make_async_copy(depth_ref, depth_hbm, sems.at[nx]))
    writes[-1].start()
    for write in writes:
        write.wait()


def around(value, axis, amount):
    count = lax.axis_size(axis)
    return lax.ppermute(value, axis, [(i, (i + amount) % count) for i in range(count)])


def to_partner(value, axis, bits):
    return lax.ppermute(value, axis, [(i, i ^ bits) for i in range(lax.axis_size(axis))])


def crossed(value, bits):
    count = lax.axis_size("slab")
    every = [(s, q) for s in range(lax.axis_size("sect")) for q in range(count)]
    pairs = [(s * count + q, (s ^ 1) * count + (q ^ bits)) for s, q in every]
    return lax.ppermute(value, ("sect", "slab"), pairs)


def to_other(value, axis):
    count = lax.axis_size(axis)
    return lax.ppermute(value, axis, [(i, (i + 2 * (i % 2) - 1) % count) for i in range(count)])


def body(density, velocity, pressure, owners):
    sizes = nx, ny, nz = density.shape
    n_sect, n_slab = lax.axis_size("sect"), lax.axis_size("slab")
    lines = nz // STRIDE
    columns = ny * lines
    slots = 2 * columns // n_slab
    length = nx * n_slab
    group = max(1, LANES // length)
    geometry = shape_of_message(nx, n_slab, slots, group)
    gas = (
        density.reshape(nx * ny, nz),
        velocity.reshape(3 * nx * ny, nz),
        pressure.reshape(nx * ny, nz),
    )
    cells = nx * ny * nz
    half = n_slab // 2
    direct = half <= 4
    x_edge, y_edge, row = (FIELDS, ny, nz), (FIELDS + 1, nx, nz), (ROWS, nz)
    owners = jnp.transpose(owners, (1, 2, 0))
    shapes = [(a.shape, a.dtype) for a in (*gas, owners)]
    x_first, x_last, y_near, y_far, top, *gas, owners = call(
        functools.partial(edges_kernel, sizes),
        [x_edge, x_edge, y_edge, (FIELDS, nx, nz), row, *shapes],
        "edges",
        20 * cells,
        [pltpu.SemaphoreType.DMA((4,))],
        in_specs=[HBM] * 4,
    )(*(pltpu.with_memory_space_constraint(a, pltpu.HBM) for a in (*gas, owners)))
    parts = (2, 2 * FIELDS + 1, nx, nz)
    spread, edge, target = call(
        functools.partial(prepare_kernel, sizes, geometry),
        [(group * spread_rows(geometry), columns), parts, (ROWS, columns)],
        "prepare",
        PREPARE_COST * cells,
    )(*gas, owners)
    y_near = to_partner(y_near, "sect", 1)
    y_far, edge = call(join_kernel, [y_edge, parts], "join", cells)(y_far, top, y_near, edge)
    y_far = to_other(y_far, "sect")
    selected = [(n_slab * geometry.rows, LANES), (n_slab * geometry.rows, columns)]
    if geometry.extra:
        count = n_slab * geometry.extra_rows
        selected += [(count, LANES), (geometry.fold * count, columns)]
    edge, *selected = call(
        functools.partial(select_kernel, sizes, geometry, direct),
        [parts, *selected],
        "select",
        SELECT_COST * cells,
    )(spread, edge, target)
    far = [around(top, "sect", d) for d in range(2, n_sect - 1)] if n_sect > 4 else []
    x_low = around(x_last, "slab", 1)
    firsts = range(half) if direct else range(1)
    x_first, *packed = call(
        functools.partial(pack_kernel, sizes, geometry, len(far)),
        [x_edge] + [(half // len(firsts) * geometry.count, LANES)] * len(firsts),
        "pack",
        PACK_COST * cells,
        [pltpu.VMEM((spread_rows(geometry), columns), jnp.float32)],
    )(edge, y_near, y_far, top, x_first, *selected, *far)
    merge = functools.partial(
        call,
        out_shapes=[(half * (geometry.rows + geometry.extra_rows) + ROWS, LANES)] * 2,
        name="merge",
        flops=MERGE_COST * cells,
    )
    if direct:
        arrived = [crossed(m, 2 * d) for d, m in zip(firsts, packed)]
        turn = [2, 3, 1, 0] if half == 4 else list(firsts)
        other, own = merge(functools.partial(merge_kernel, geometry, turn))(*(arrived[d] for d in turn))
        other, own = crossed(other, 1), crossed(own, 0)
    else:
        alike = [[2 * i + odd for i in range(half)] for odd in range(2)]
        arrived = [
            lax.all_to_all(m, "slab", split_axis=0, concat_axis=0, axis_index_groups=alike, tiled=True) for m in packed
        ]
        other, own = merge(functools.partial(merge_kernel, geometry, firsts))(*arrived)
        other = to_partner(other, "slab", 1)
    x_low, x_first = call(hold_kernel, [x_edge] * 2, "hold", HOLD_COST * cells)(x_low, x_first)
    x_high = around(x_first, "slab", -1)
    (change,) = call(
        functools.partial(change_kernel, sizes),
        [(FIELDS, nx * ny, nz)],
        "change",
        300_000 * cells,
    )(*gas, x_low, x_high, y_near, y_far)
    new_state, depth = call(
        functools.partial(final_kernel, sizes, geometry, direct),
        [(FIELDS, nx * ny, nz), (slots, length)],
        "final",
        100 * cells,
        [
            pltpu.VMEM((FIELDS, nx * ny, nz), jnp.float32),
            pltpu.VMEM((slots, length), jnp.float32),
            pltpu.VMEM((n_slab, geometry.rows, LANES), jnp.float32),
            pltpu.VMEM((n_slab, max(1, geometry.extra_rows), LANES), jnp.float32),
            pltpu.SemaphoreType.DMA((nx + 1,)),
        ],
        out_specs=[HBM, HBM],
    )(*gas, change, other, own, packed[0])
    return (new_state.reshape(FIELDS, nx, ny, nz), depth.reshape(1, 1, slots, length))


def solution(mesh):
    in_specs = (
        P("slab", "sect", None),
        P(None, "slab", "sect", None),
        P("slab", "sect", None),
        P("sect", None, None),
    )
    out_specs = (P(None, "slab", "sect", None), P("sect", "slab", None, None))
    return jax.shard_map(body, mesh=mesh, in_specs=in_specs, out_specs=out_specs, check_vma=False)
```

```python
import functools
import math
from typing import NamedTuple

import jax
import jax.numpy as jnp
from jax import lax
from jax.experimental import pallas as pl
from jax.experimental.pallas import tpu as pltpu
from jax.sharding import PartitionSpec as P

STRIDE = 32
BAND = 512

GAMMA = 5.0 / 3.0
COURANT = 0.15
TURBULENT = 0.25
NORMALISE = 0.5641895835477563

LANES = 128
ROWS = 8
FIELDS = 5
UNROLL = 64
PACK_COST = 30_000
PREPARE_COST = 300
SELECT_COST = 300
PIECES = 3
MERGE_COST = 30_000
HOLD_COST = 1

VMEM = pl.BlockSpec(memory_space=pltpu.VMEM)


HBM = pl.BlockSpec(memory_space=pltpu.HBM)


class Message(NamedTuple):
    owners: int
    slots: int
    group: int
    rows: int
    part: int
    main: int
    extra: int
    fold: int
    extra_rows: int
    count: int


def shape_of_message(nx, owners, slots, group):
    rows, part = slots // group, nx * group
    main = min(2 * FIELDS, LANES // part)
    extra = 2 * FIELDS - main
    fold = min(rows, LANES // (extra * part)) if extra else 1
    extra_rows = rows // fold if extra else 0
    count = 2 * rows + 2 * extra_rows + ROWS
    return Message(owners, slots, group, rows, part, main, extra, fold, extra_rows, count)


def call(kernel, out_shapes, name, flops, scratch=(), in_specs=None, out_specs=None):
    more = {} if in_specs is None else {"in_specs": in_specs}
    return pl.pallas_call(
        kernel,
        out_shape=[
            jax.ShapeDtypeStruct(*s) if isinstance(s[0], tuple) else jax.ShapeDtypeStruct(s, jnp.float32)
            for s in out_shapes
        ],
        out_specs=out_specs or [VMEM] * len(out_shapes),
        **more,
        scratch_shapes=list(scratch),
        compiler_params=pltpu.CompilerParams(vmem_limit_bytes=24 * 1024 * 1024),
        cost_estimate=pl.CostEstimate(flops=flops, bytes_accessed=1 << 20, transcendentals=0),
        name=name,
    )


def shift(array, amount, axis):
    size = array.shape[axis]
    amount = amount % size
    return array if amount == 0 else pltpu.roll(array, amount, axis)


def derived(cell):
    r, u, v, w, p = cell
    m = (r * u, r * v, r * w)
    energy = p * (1.0 / (GAMMA - 1.0)) + 0.5 * (m[0] * u + m[1] * v + m[2] * w)
    sound = jnp.sqrt(GAMMA * p / r)
    return (r, *m, energy), sound


def flux_parts(cell, state, sound, d):
    moving = cell[1 + d]
    flux = [state[1 + d]]
    for k in range(3):
        term = state[1 + k] * moving
        flux.append(term + cell[4] if k == d else term)
    flux.append((state[4] + cell[4]) * moving)
    return (*state, *flux, jnp.abs(moving) + sound)


def face(left, right):
    speed = jnp.maximum(left[10], right[10])
    return [
        (left[5 + k] + right[5 + k]) - speed * (right[k] - left[k]) for k in range(FIELDS)
    ]


def fields_of(r_ref, v_ref, p_ref, index):
    total = r_ref.shape[0]
    first = index.start if isinstance(index, pl.Slice) else index
    out = [r_ref[index]]
    for k in range(3):
        if isinstance(index, pl.Slice):
            out.append(v_ref[pl.ds(k * total + first, index.size, index.stride)])
        else:
            out.append(v_ref[k * total + index])
    out.append(p_ref[index])
    return out


def place_of(direct):
    me = lax.axis_index("slab")
    return (me // 2 if direct else 0), me % 2


def is_odd(axis, shape):
    return jnp.full(shape, lax.axis_index(axis) % 2) == 1


def sides(near, far, axis):
    odd = is_odd(axis, near[0].shape)
    low = [jnp.where(odd, n, f) for n, f in zip(near, far)]
    high = [jnp.where(odd, f, n) for n, f in zip(near, far)]
    return low, high


def edges_kernel(
    sizes, r_hbm, v_hbm, p_hbm, o_hbm, x_first, x_last, y_near, y_far, top_ref, r_ref, v_ref, p_ref, o_ref, sems
):
    nx, ny, nz = sizes
    pairs = [(r_hbm, r_ref), (v_hbm, v_ref), (p_hbm, p_ref), (o_hbm, o_ref)]
    loads = [pltpu.make_async_copy(source, target, sems.at[i]) for i, (source, target) in enumerate(pairs)]
    for load in loads:
        load.start()
    for load in loads:
        load.wait()
    for out, x in ((x_first, 0), (x_last, nx - 1)):
        for f, value in enumerate(fields_of(r_ref, v_ref, p_ref, pl.ds(x * ny, ny))):
            out[f] = value
    first, last = (fields_of(r_ref, v_ref, p_ref, pl.ds(y, nx, ny)) for y in (0, ny - 1))
    far, near = sides(last, first, "sect")
    for f in range(FIELDS):
        y_near[f] = near[f]
        y_far[f] = far[f]
    top = jnp.zeros((ROWS, nz), jnp.float32)
    for row in range(0, nx * ny, ROWS):
        r, u, v, w, p = fields_of(r_ref, v_ref, p_ref, pl.ds(row, ROWS))
        speed = jnp.maximum(jnp.maximum(jnp.abs(u), jnp.abs(v)), jnp.abs(w)) + jnp.sqrt(GAMMA * p / r)
        top = jnp.maximum(top, speed)
    y_near[FIELDS] = top
    top_ref[...] = top


def join_kernel(y_far, top_ref, near_ref, edge_ref, out_ref, edge_out):
    for f in range(FIELDS):
        out_ref[f] = y_far[f]
    out_ref[FIELDS] = jnp.maximum(top_ref[...], near_ref[FIELDS])
    edge_out[...] = edge_ref[...]


def spread_rows(msg):
    return LANES + msg.extra * msg.part


def prepare_kernel(sizes, msg, r_ref, v_ref, p_ref, owner_ref, spread, edge_ref, target_ref):
    nx, ny, nz = sizes
    lines = nz // STRIDE
    columns = ny * lines
    step = STRIDE // ROWS
    lane = lax.broadcasted_iota(jnp.int32, (nx, nz), 1)
    first = lane % STRIDE < step
    last = lane % STRIDE >= ny - step
    tiles, changes, parts = [], [], []
    for t in range(step):
        cell = None
        for s in range(ny // step):
            rows = fields_of(r_ref, v_ref, p_ref, pl.ds(step * s + t, nx, ny))
            rows = [shift(a, step * s, 1) for a in rows]
            if cell is None:
                cell = rows
            else:
                mine = (lane - step * s + 1) % STRIDE < 3
                cell = [jnp.where(mine, a, b) for a, b in zip(rows, cell)]
        state, sound = derived(cell)
        here = flux_parts(cell, state, sound, 2)
        after = face(here, [shift(a, -1, 1) for a in here])
        tiles.append(cell)
        changes.append([a - shift(a, 1, 1) for a in after])
        parts.append(flux_parts(cell, state, sound, 1))
    inner = [face(a, b) for a, b in zip(parts, parts[1:])]
    around_face = face([shift(a, step, 1) for a in parts[-1]], parts[0])
    low = [jnp.where(first, 0.0, a) for a in around_face]
    high = [jnp.where(last, 0.0, shift(a, -step, 1)) for a in around_face]
    faces = [low, *inner, high]
    dense = None
    for t in range(step):
        total = [c + (b - a) for c, a, b in zip(changes[t], faces[t], faces[t + 1])]
        values = [shift(a, t, 1) for a in [*tiles[t], *total]]
        dense = values if dense is None else [jnp.where(lane % step == t, a, b) for a, b in zip(values, dense)]
    group, width = msg.group, spread_rows(msg)
    spread[...] = jnp.zeros_like(spread)
    for f, value in enumerate(dense):
        for h in range(group):
            spread[pl.ds(h * width + f * nx * group + h, nx, group), :] = value
    for i, (a, b) in enumerate(zip(parts[0], parts[-1])):
        edge_ref[0, i] = a
        edge_ref[1, i] = shift(b, step - ny, 1)
    owner = jnp.concatenate([owner_ref[k] for k in range(lines)], axis=1).astype(jnp.float32)
    own = jnp.broadcast_to(owner, (columns, columns))
    own_t = own.T

    def place(dim):
        at = lax.broadcasted_iota(jnp.int32, (columns, columns), dim)
        return (at % ny) * lines + at // ny

    ahead = (own == own_t) & (place(0) < place(1))
    rank = jnp.sum(jnp.where(ahead, 1.0, 0.0), axis=0, keepdims=True)
    target_ref[...] = jnp.broadcast_to(owner * msg.slots + rank, target_ref.shape)


def lane_of(side, piece, place, group):
    return (side * PIECES + piece) * group + place


def product(selection, values):
    return lax.dot_general(
        selection.astype(jnp.bfloat16), values, (((1,), (1,)), ((), ())), preferred_element_type=jnp.float32
    )


def folded(msg, picked):
    every = msg.owners * msg.extra_rows
    return jnp.concatenate([picked[a * every : (a + 1) * every] for a in range(msg.fold)], axis=1)


def select_kernel(sizes, msg, direct, spread, edge_ref, target_ref, edge_out, *outs):
    _, ny, nz = sizes
    group, width, columns = msg.group, spread_rows(msg), ny * (nz // STRIDE)
    edge_out[...] = edge_ref[...]
    target = target_ref[0:1]
    z_me, y_me = place_of(direct)
    at = lax.broadcasted_iota(jnp.int32, (1, columns), 1) % ny
    edges = jnp.full((1, columns), -1.0)
    for side, y in enumerate((0, ny - 1)):
        for p in range(PIECES):
            for h in range(group):
                some = jnp.where(at == y, target - float(h), -1.0)
                edges = jnp.maximum(edges, shift(some, lane_of(side, p, h, group) - y, 1))

    def slot_of(rows, first):
        row = lax.broadcasted_iota(jnp.int32, (msg.owners * rows, columns), 0)
        block = row // rows
        own_of = 2 * ((block // 2) ^ z_me) + ((block % 2) ^ y_me)
        return (own_of * msg.slots + (first + row % rows) * group).astype(jnp.float32)

    def pick(rows, folds, first, count):
        slot = jnp.concatenate([slot_of(rows, a * rows) for a in range(folds)], axis=0)
        every = [jnp.where(slot == target - float(h), 1.0, 0.0) for h in range(group)]
        every = jnp.concatenate(every, axis=1).astype(jnp.bfloat16)
        value = jnp.concatenate([spread[pl.ds(h * width + first, count), :] for h in range(group)], axis=1)
        out = []
        for _ in range(PIECES):
            out.append(value.astype(jnp.bfloat16))
            value = value - out[-1].astype(jnp.float32)
        picked = product(jnp.concatenate([every] * PIECES, axis=1), jnp.concatenate(out, axis=1))
        return picked, jnp.where(slot == edges, 1.0, 0.0)

    outs[0][...], outs[1][...] = pick(msg.rows, 1, 0, LANES)
    if msg.extra:
        picked, outs[3][...] = pick(msg.extra_rows, msg.fold, LANES, msg.extra * msg.part)
        outs[2][...] = folded(msg, picked)


def pack_kernel(sizes, msg, n_far, edge_ref, y_near, y_far, top_ref, x_first, main_ref, main_edges, *rest):
    nx, ny, nz = sizes
    group = msg.group
    (extra_ref, extra_edges), rest = (rest[:2], rest[2:]) if msg.extra else ((None, None), rest)
    far, x_out, outs, spread = rest[:n_far], rest[n_far], rest[n_far + 1 : -1], rest[-1]
    x_out[...] = x_first[...]
    on = lax.broadcasted_iota(jnp.int32, (nx, nz), 1) % STRIDE == 0
    spread[pl.ds(0, LANES), :] = jnp.zeros((LANES, spread.shape[1]), jnp.float32)
    rows = [[None] * group for _ in range(FIELDS)]
    cells = sides([y_near[f] for f in range(FIELDS)], [y_far[f] for f in range(FIELDS)], "sect")
    for side, cell in enumerate(cells):
        beyond = flux_parts(cell, *derived(cell), 1)
        edge = [edge_ref[side, i] for i in range(len(beyond))]
        faces = face(edge, beyond) if side else [-a for a in face(beyond, edge)]
        for f, value in enumerate(faces):
            value = jnp.where(on, value, 0.0)
            for p in range(PIECES):
                piece = value.astype(jnp.bfloat16).astype(jnp.float32)
                value = value - piece
                for h in range(group):
                    moved = shift(piece, lane_of(side, p, h, group), 1)
                    rows[f][h] = moved if rows[f][h] is None else rows[f][h] + moved
    for f in range(FIELDS):
        for h in range(group):
            spread[pl.ds((FIELDS + f) * nx * group + h, nx, group), :] = rows[f][h]
    top = jnp.maximum(jnp.maximum(top_ref[...], y_near[FIELDS]), y_far[FIELDS])
    for ref in far:
        top = jnp.maximum(top, ref[...])
    top = jnp.broadcast_to(jnp.max(top, keepdims=True), top.shape)
    per = msg.count
    each = msg.owners // len(outs)
    picked = main_ref[...] + product(main_edges[...], spread[pl.ds(0, LANES), :].astype(jnp.bfloat16))
    for b in range(msg.owners):
        at = (b % each) // 2 * per + b % 2 * msg.rows
        outs[b // each][pl.ds(at, msg.rows), :] = picked[b * msg.rows : (b + 1) * msg.rows]
    if msg.extra:
        rows = msg.extra_rows
        values = spread[pl.ds(LANES, msg.extra * msg.part), :].astype(jnp.bfloat16)
        picked = extra_ref[...] + folded(msg, product(extra_edges[...], values))
        for b in range(msg.owners):
            at = (b % each) // 2 * per + 2 * msg.rows + b % 2 * rows
            outs[b // each][pl.ds(at, rows), :] = picked[b * rows : (b + 1) * rows]
    for out in outs:
        for d in range(each // 2):
            out[pl.ds((d + 1) * per - ROWS, ROWS), :] = top


def merge_kernel(msg, firsts, *refs):
    *refs, other_ref, own_ref = refs
    half, top = msg.owners // 2, None
    for first, ref in zip(firsts, refs):
        for d in range(ref.shape[0] // msg.count):
            at, to = d * msg.count, first + d
            for odd, out in ((0, own_ref), (1, other_ref)):
                out[pl.ds(to * msg.rows, msg.rows), :] = ref[pl.ds(at + odd * msg.rows, msg.rows), :]
                if msg.extra:
                    rows = msg.extra_rows
                    out[pl.ds(half * msg.rows + to * rows, rows), :] = ref[
                        pl.ds(at + 2 * msg.rows + odd * rows, rows), :
                    ]
            new = ref[pl.ds(at + msg.count - ROWS, ROWS), :]
            top = new if top is None else jnp.maximum(top, new)
    for out in (own_ref, other_ref):
        out[pl.ds(half * (msg.rows + msg.extra_rows), ROWS), :] = top


def hold_kernel(first_ref, second_ref, first_out, second_out):
    first_out[...] = first_ref[...]
    second_out[...] = second_ref[...]


def change_kernel(sizes, r_ref, v_ref, p_ref, x_low, x_high, y_near, y_far, out_ref, state_ref):
    nx, ny, nz = sizes
    every = range(FIELDS)
    y_low, y_high = sides([y_near[f] for f in every], [y_far[f] for f in every], "sect")
    row = lax.broadcasted_iota(jnp.int32, (ny, nz), 0)
    half = 0.5

    def layer(x):
        if x < 0:
            return [x_low[f] for f in range(FIELDS)]
        if x >= nx:
            return [x_high[f] for f in range(FIELDS)]
        return fields_of(r_ref, v_ref, p_ref, pl.ds(x * ny, ny))

    def prepared(x):
        cell = layer(x)
        state, sound = derived(cell)
        return cell, state, sound, flux_parts(cell, state, sound, 0)

    previous = prepared(-1)
    here = prepared(0)
    x_face = face(previous[3], here[3])
    for x in range(nx):
        following = prepared(x + 1)
        cell, state, sound, parts = here
        next_face = face(parts, following[3])
        total = [a - b for a, b in zip(next_face, x_face)]
        x_face = next_face
        low_cell = [y_low[f][x : x + 1] for f in range(FIELDS)]
        high_cell = [y_high[f][x : x + 1] for f in range(FIELDS)]
        low = flux_parts(low_cell, *derived(low_cell), 1)
        high = flux_parts(high_cell, *derived(high_cell), 1)
        parts = flux_parts(cell, state, sound, 1)
        plus = [jnp.where(row == ny - 1, h, shift(a, -1, 0)) for a, h in zip(parts, high)]
        after = face(parts, plus)
        edge = face(low, [a[0:1] for a in parts])
        before = [jnp.where(row == 0, e, shift(a, 1, 0)) for a, e in zip(after, edge)]
        total = [t + (a - b) for t, a, b in zip(total, after, before)]
        parts = flux_parts(cell, state, sound, 2)
        after = face(parts, [shift(a, -1, 1) for a in parts])
        total = [t + (a - shift(a, 1, 1)) for t, a in zip(total, after)]
        for f in range(FIELDS):
            out_ref[f, pl.ds(x * ny, ny), :] = half * total[f]
            state_ref[f, pl.ds(x * ny, ny), :] = state[f]
        here = following


def final_kernel(sizes, msg, direct, state_ref, change_ref, other_ref, own_ref, kept_ref, *rest):
    new_hbm, depth_hbm, new_ref, depth_ref, main_ref, extra_ref, sems = rest
    nx, ny, nz = sizes
    n_owner, group, part = msg.owners, msg.group, msg.part
    half, length = n_owner // 2, nx * n_owner
    at = pl.ds(half * (msg.rows + msg.extra_rows), ROWS)
    top = jnp.maximum(other_ref[at, :], own_ref[at, :])
    step = COURANT / top[0:1, 0:1]
    writes = []
    for x in range(nx):
        rows = pl.ds(x * ny, ny)
        for f in range(FIELDS):
            new_ref[f, rows, :] = state_ref[f, rows, :] - step * change_ref[f, rows, :]
        writes.append(pltpu.make_async_copy(new_ref.at[:, rows], new_hbm.at[:, rows], sems.at[x]))
        writes[-1].start()
    z_me, y_me = place_of(direct)

    def settle(source, at, extra_at, d, odd):
        owner = 2 * (d ^ z_me) + (odd ^ y_me)
        main_ref[owner] = source[pl.ds(at, msg.rows), :]
        if msg.extra:
            extra_ref[owner] = source[pl.ds(extra_at, msg.extra_rows), :]

    for d in range(half):
        extra_at = half * msg.rows + d * msg.extra_rows
        if direct and d == 0:
            settle(kept_ref, 0, 2 * msg.rows, 0, 0)
        else:
            settle(own_ref, d * msg.rows, extra_at, d, 0)
        settle(other_ref, d * msg.rows, extra_at, d, 1)
    line = []
    for f in range(msg.main):
        line.append(jnp.concatenate([main_ref[q, :, pl.ds(f * part, part)] for q in range(n_owner)], axis=1))
    for f in range(msg.extra):
        folds = []
        for a in range(msg.fold):
            at = pl.ds((a * msg.extra + f) * part, part)
            folds.append(jnp.concatenate([extra_ref[q, :, at] for q in range(n_owner)], axis=1))
        line.append(jnp.concatenate(folds, axis=0))
    cell, change = line[:FIELDS], line[FIELDS:]
    taken = cell[0] > 0.0
    cell[0] = jnp.where(taken, cell[0], 1.0)
    state, sound = derived(cell)
    parts = flux_parts(cell, state, sound, 0)
    after = face(parts, [shift(a, -group, 1) for a in parts])
    change = [c + (a - shift(a, group, 1)) for c, a in zip(change, after)]
    new = [s - (0.5 * step) * c for s, c in zip(state, change)]
    density = new[0]
    pressure = (GAMMA - 1.0) * (new[4] - 0.5 * (new[1] * new[1] + new[2] * new[2] + new[3] * new[3]) / density)
    broadening = TURBULENT + pressure / density
    inverse = 1.0 / (BAND / 64.0 * jnp.sqrt(broadening))
    amplitude = NORMALISE * (density * density) * jnp.exp(-0.7 * jnp.log(broadening)) * inverse
    amplitude = jnp.where(taken, amplitude, 0.0)
    scaled = inverse * math.sqrt(math.log2(math.e))
    centre = (BAND / 8.0) * (new[1] / density)
    turns = BAND // length
    block = min(length, UNROLL)

    def skewers(rows):
        scale, middle, size = scaled[:rows], centre[:rows], amplitude[:rows]
        strides = [scale * float(length * m) for m in range(turns)]

        def offsets(count, running):
            e = (length - block - block * count) * 1.0 - float(BAND // 2)
            for b in range(block):
                start = (e + float(b) - middle) * scale
                total = None
                for m in range(turns):
                    t = start + strides[m] if m else start
                    value = jnp.exp2(-(t * t))
                    total = value if total is None else total + value
                part = shift(size * total, b * group, 1)
                block_sum = part if b == 0 else block_sum + part
            return block_sum if running is None else shift(running, block * group, 1) + block_sum

        if length == block:
            running = offsets(0, None)
        else:
            running = lax.fori_loop(
                0,
                length // block,
                lambda i, c: offsets(i.astype(jnp.float32), c),
                jnp.zeros_like(size),
            )
        running = shift(running, -(BAND // 2) * group, 1)
        if group > 1:
            wide = jnp.broadcast_to(running[:, None, :], (rows, group, group * length))
            wide = wide.reshape(rows * group, group * length)
            at = lax.broadcasted_iota(jnp.int32, wide.shape, 1)
            of = lax.broadcasted_iota(jnp.int32, wide.shape, 0)
            wide = jnp.where(at % group == of % group, wide, 0.0)
            at = lax.broadcasted_iota(jnp.int32, (group * length, length), 0)
            of = lax.broadcasted_iota(jnp.int32, (group * length, length), 1)
            pick = jnp.where(at // group == of, 1.0, 0.0)
            pieces = []
            for _ in range(PIECES):
                pieces.append(wide.astype(jnp.bfloat16))
                wide = wide - pieces[-1].astype(jnp.float32)
            pick = jnp.concatenate([pick.astype(jnp.bfloat16)] * PIECES, axis=0)
            running = jnp.dot(jnp.concatenate(pieces, axis=1), pick, preferred_element_type=jnp.float32)
        depth_ref[pl.ds(0, rows * group), :] = running

    if msg.rows > ROWS:
        some = kept_ref if direct else own_ref
        more = jnp.max(some[pl.ds(ROWS, msg.rows - ROWS), pl.ds(0, part)]) > 0.0

        @pl.when(more)
        def _():
            skewers(msg.rows)

        @pl.when(jnp.logical_not(more))
        def _():
            depth_ref[...] = jnp.zeros_like(depth_ref)
            skewers(ROWS)

    else:
        skewers(msg.rows)
    writes.append(pltpu.make_async_copy(depth_ref, depth_hbm, sems.at[nx]))
    writes[-1].start()
    for write in writes:
        write.wait()


def around(value, axis, amount):
    count = lax.axis_size(axis)
    return lax.ppermute(value, axis, [(i, (i + amount) % count) for i in range(count)])


def to_partner(value, axis, bits):
    return lax.ppermute(value, axis, [(i, i ^ bits) for i in range(lax.axis_size(axis))])


def crossed(value, bits):
    count = lax.axis_size("slab")
    every = [(s, q) for s in range(lax.axis_size("sect")) for q in range(count)]
    pairs = [(s * count + q, (s ^ 1) * count + (q ^ bits)) for s, q in every]
    return lax.ppermute(value, ("sect", "slab"), pairs)


def to_other(value, axis):
    count = lax.axis_size(axis)
    return lax.ppermute(value, axis, [(i, (i + 2 * (i % 2) - 1) % count) for i in range(count)])


def body(density, velocity, pressure, owners):
    sizes = nx, ny, nz = density.shape
    n_sect, n_slab = lax.axis_size("sect"), lax.axis_size("slab")
    lines = nz // STRIDE
    columns = ny * lines
    slots = 2 * columns // n_slab
    length = nx * n_slab
    group = max(1, LANES // length)
    geometry = shape_of_message(nx, n_slab, slots, group)
    gas = (
        density.reshape(nx * ny, nz),
        velocity.reshape(3 * nx * ny, nz),
        pressure.reshape(nx * ny, nz),
    )
    cells = nx * ny * nz
    half = n_slab // 2
    direct = half <= 4
    x_edge, y_edge, row = (FIELDS, ny, nz), (FIELDS + 1, nx, nz), (ROWS, nz)
    owners = jnp.transpose(owners, (1, 2, 0))
    shapes = [(a.shape, a.dtype) for a in (*gas, owners)]
    x_first, x_last, y_near, y_far, top, *gas, owners = call(
        functools.partial(edges_kernel, sizes),
        [x_edge, x_edge, y_edge, (FIELDS, nx, nz), row, *shapes],
        "edges",
        20 * cells,
        [pltpu.SemaphoreType.DMA((4,))],
        in_specs=[HBM] * 4,
    )(*(pltpu.with_memory_space_constraint(a, pltpu.HBM) for a in (*gas, owners)))
    parts = (2, 2 * FIELDS + 1, nx, nz)
    spread, edge, target = call(
        functools.partial(prepare_kernel, sizes, geometry),
        [(group * spread_rows(geometry), columns), parts, (ROWS, columns)],
        "prepare",
        PREPARE_COST * cells,
    )(*gas, owners)
    y_near = to_partner(y_near, "sect", 1)
    y_far, edge = call(join_kernel, [y_edge, parts], "join", cells)(y_far, top, y_near, edge)
    y_far = to_other(y_far, "sect")
    selected = [(n_slab * geometry.rows, LANES), (n_slab * geometry.rows, columns)]
    if geometry.extra:
        count = n_slab * geometry.extra_rows
        selected += [(count, LANES), (geometry.fold * count, columns)]
    edge, *selected = call(
        functools.partial(select_kernel, sizes, geometry, direct),
        [parts, *selected],
        "select",
        SELECT_COST * cells,
    )(spread, edge, target)
    far = [around(top, "sect", d) for d in range(2, n_sect - 1)] if n_sect > 4 else []
    x_low = around(x_last, "slab", 1)
    firsts = range(half) if direct else range(1)
    x_first, *packed = call(
        functools.partial(pack_kernel, sizes, geometry, len(far)),
        [x_edge] + [(half // len(firsts) * geometry.count, LANES)] * len(firsts),
        "pack",
        PACK_COST * cells,
        [pltpu.VMEM((spread_rows(geometry), columns), jnp.float32)],
    )(edge, y_near, y_far, top, x_first, *selected, *far)
    merge = functools.partial(
        call,
        out_shapes=[(half * (geometry.rows + geometry.extra_rows) + ROWS, LANES)] * 2,
        name="merge",
        flops=MERGE_COST * cells,
    )
    if direct:
        arrived = [crossed(m, 2 * d) for d, m in zip(firsts, packed)]
        turn = [2, 3, 1, 0] if half == 4 else list(firsts)
        other, own = merge(functools.partial(merge_kernel, geometry, turn))(*(arrived[d] for d in turn))
        other, own = crossed(other, 1), crossed(own, 0)
    else:
        alike = [[2 * i + odd for i in range(half)] for odd in range(2)]
        arrived = [
            lax.all_to_all(m, "slab", split_axis=0, concat_axis=0, axis_index_groups=alike, tiled=True) for m in packed
        ]
        other, own = merge(functools.partial(merge_kernel, geometry, firsts))(*arrived)
        other = to_partner(other, "slab", 1)
    x_low, x_first = call(hold_kernel, [x_edge] * 2, "hold", HOLD_COST * cells)(x_low, x_first)
    x_high = around(x_first, "slab", -1)
    change, state = call(
        functools.partial(change_kernel, sizes),
        [(FIELDS, nx * ny, nz)] * 2,
        "change",
        300_000 * cells,
    )(*gas, x_low, x_high, y_near, y_far)
    new_state, depth = call(
        functools.partial(final_kernel, sizes, geometry, direct),
        [(FIELDS, nx * ny, nz), (slots, length)],
        "final",
        100 * cells,
        [
            pltpu.VMEM((FIELDS, nx * ny, nz), jnp.float32),
            pltpu.VMEM((slots, length), jnp.float32),
            pltpu.VMEM((n_slab, geometry.rows, LANES), jnp.float32),
            pltpu.VMEM((n_slab, max(1, geometry.extra_rows), LANES), jnp.float32),
            pltpu.SemaphoreType.DMA((nx + 1,)),
        ],
        out_specs=[HBM, HBM],
    )(state, change, other, own, packed[0])
    return (new_state.reshape(FIELDS, nx, ny, nz), depth.reshape(1, 1, slots, length))


def solution(mesh):
    in_specs = (
        P("slab", "sect", None),
        P(None, "slab", "sect", None),
        P("slab", "sect", None),
        P("sect", None, None),
    )
    out_specs = (P(None, "slab", "sect", None), P("sect", "slab", None, None))
    return jax.shard_map(body, mesh=mesh, in_specs=in_specs, out_specs=out_specs, check_vma=False)
```

```python
import functools
import math
from typing import NamedTuple

import jax
import jax.numpy as jnp
from jax import lax
from jax.experimental import pallas as pl
from jax.experimental.pallas import tpu as pltpu
from jax.sharding import PartitionSpec as P

STRIDE = 32
BAND = 512

GAMMA = 5.0 / 3.0
COURANT = 0.15
TURBULENT = 0.25
NORMALISE = 0.5641895835477563

LANES = 128
ROWS = 8
FIELDS = 5
UNROLL = 64
PACK_COST = 30_000
PREPARE_COST = 300
SELECT_COST = 300
PIECES = 3
MERGE_COST = 30_000
HOLD_COST = 1

VMEM = pl.BlockSpec(memory_space=pltpu.VMEM)


HBM = pl.BlockSpec(memory_space=pltpu.HBM)


class Message(NamedTuple):
    owners: int
    slots: int
    group: int
    rows: int
    part: int
    main: int
    extra: int
    fold: int
    extra_rows: int
    count: int


def shape_of_message(nx, owners, slots, group):
    rows, part = slots // group, nx * group
    main = min(2 * FIELDS, LANES // part)
    extra = 2 * FIELDS - main
    fold = min(rows, LANES // (extra * part)) if extra else 1
    extra_rows = rows // fold if extra else 0
    count = 2 * rows + 2 * extra_rows + ROWS
    return Message(owners, slots, group, rows, part, main, extra, fold, extra_rows, count)


def call(kernel, out_shapes, name, flops, scratch=(), in_specs=None, out_specs=None):
    more = {} if in_specs is None else {"in_specs": in_specs}
    return pl.pallas_call(
        kernel,
        out_shape=[
            jax.ShapeDtypeStruct(*s) if isinstance(s[0], tuple) else jax.ShapeDtypeStruct(s, jnp.float32)
            for s in out_shapes
        ],
        out_specs=out_specs or [VMEM] * len(out_shapes),
        **more,
        scratch_shapes=list(scratch),
        compiler_params=pltpu.CompilerParams(vmem_limit_bytes=24 * 1024 * 1024),
        cost_estimate=pl.CostEstimate(flops=flops, bytes_accessed=1 << 20, transcendentals=0),
        name=name,
    )


def shift(array, amount, axis):
    size = array.shape[axis]
    amount = amount % size
    return array if amount == 0 else pltpu.roll(array, amount, axis)


def derived(cell):
    r, u, v, w, p = cell
    m = (r * u, r * v, r * w)
    energy = p * (1.0 / (GAMMA - 1.0)) + 0.5 * (m[0] * u + m[1] * v + m[2] * w)
    sound = jnp.sqrt(GAMMA * p / r)
    return (r, *m, energy), sound


def flux_parts(cell, state, sound, d):
    moving = cell[1 + d]
    flux = [state[1 + d]]
    for k in range(3):
        term = state[1 + k] * moving
        flux.append(term + cell[4] if k == d else term)
    flux.append((state[4] + cell[4]) * moving)
    return (*state, *flux, jnp.abs(moving) + sound)


def face(left, right):
    speed = jnp.maximum(left[10], right[10])
    return [
        (left[5 + k] + right[5 + k]) - speed * (right[k] - left[k]) for k in range(FIELDS)
    ]


def fields_of(r_ref, v_ref, p_ref, index):
    total = r_ref.shape[0]
    first = index.start if isinstance(index, pl.Slice) else index
    out = [r_ref[index]]
    for k in range(3):
        if isinstance(index, pl.Slice):
            out.append(v_ref[pl.ds(k * total + first, index.size, index.stride)])
        else:
            out.append(v_ref[k * total + index])
    out.append(p_ref[index])
    return out


def place_of(direct):
    me = lax.axis_index("slab")
    return (me // 2 if direct else 0), me % 2


def is_odd(axis, shape):
    return jnp.full(shape, lax.axis_index(axis) % 2) == 1


def sides(near, far, axis):
    odd = is_odd(axis, near[0].shape)
    low = [jnp.where(odd, n, f) for n, f in zip(near, far)]
    high = [jnp.where(odd, f, n) for n, f in zip(near, far)]
    return low, high


def edges_kernel(
    sizes, r_hbm, v_hbm, p_hbm, o_hbm, x_first, x_last, y_near, y_far, top_ref, r_ref, v_ref, p_ref, o_ref, sems
):
    nx, ny, nz = sizes
    pairs = [(r_hbm, r_ref), (v_hbm, v_ref), (p_hbm, p_ref), (o_hbm, o_ref)]
    loads = [pltpu.make_async_copy(source, target, sems.at[i]) for i, (source, target) in enumerate(pairs)]
    for load in loads:
        load.start()
    for load in loads:
        load.wait()
    for out, x in ((x_first, 0), (x_last, nx - 1)):
        for f, value in enumerate(fields_of(r_ref, v_ref, p_ref, pl.ds(x * ny, ny))):
            out[f] = value
    first, last = (fields_of(r_ref, v_ref, p_ref, pl.ds(y, nx, ny)) for y in (0, ny - 1))
    far, near = sides(last, first, "sect")
    for f in range(FIELDS):
        y_near[f] = near[f]
        y_far[f] = far[f]
    top = jnp.zeros((ROWS, nz), jnp.float32)
    for row in range(0, nx * ny, ROWS):
        r, u, v, w, p = fields_of(r_ref, v_ref, p_ref, pl.ds(row, ROWS))
        speed = jnp.maximum(jnp.maximum(jnp.abs(u), jnp.abs(v)), jnp.abs(w)) + jnp.sqrt(GAMMA * p / r)
        top = jnp.maximum(top, speed)
    y_near[FIELDS] = top
    top_ref[...] = top


def join_kernel(y_far, top_ref, near_ref, edge_ref, out_ref, edge_out):
    for f in range(FIELDS):
        out_ref[f] = y_far[f]
    out_ref[FIELDS] = jnp.maximum(top_ref[...], near_ref[FIELDS])
    edge_out[...] = edge_ref[...]


def spread_rows(msg):
    return LANES + msg.extra * msg.part


def prepare_kernel(sizes, msg, r_ref, v_ref, p_ref, owner_ref, spread, edge_ref, target_ref):
    nx, ny, nz = sizes
    lines = nz // STRIDE
    columns = ny * lines
    step = STRIDE // ROWS
    lane = lax.broadcasted_iota(jnp.int32, (nx, nz), 1)
    first = lane % STRIDE < step
    last = lane % STRIDE >= ny - step
    tiles, changes, parts = [], [], []
    for t in range(step):
        cell = None
        for s in range(ny // step):
            rows = fields_of(r_ref, v_ref, p_ref, pl.ds(step * s + t, nx, ny))
            rows = [shift(a, step * s, 1) for a in rows]
            if cell is None:
                cell = rows
            else:
                mine = (lane - step * s + 1) % STRIDE < 3
                cell = [jnp.where(mine, a, b) for a, b in zip(rows, cell)]
        state, sound = derived(cell)
        here = flux_parts(cell, state, sound, 2)
        after = face(here, [shift(a, -1, 1) for a in here])
        tiles.append(cell)
        changes.append([a - shift(a, 1, 1) for a in after])
        parts.append(flux_parts(cell, state, sound, 1))
    inner = [face(a, b) for a, b in zip(parts, parts[1:])]
    around_face = face([shift(a, step, 1) for a in parts[-1]], parts[0])
    low = [jnp.where(first, 0.0, a) for a in around_face]
    high = [jnp.where(last, 0.0, shift(a, -step, 1)) for a in around_face]
    faces = [low, *inner, high]
    dense = None
    for t in range(step):
        total = [c + (b - a) for c, a, b in zip(changes[t], faces[t], faces[t + 1])]
        values = [shift(a, t, 1) for a in [*tiles[t], *total]]
        dense = values if dense is None else [jnp.where(lane % step == t, a, b) for a, b in zip(values, dense)]
    group, width = msg.group, spread_rows(msg)
    spread[...] = jnp.zeros_like(spread)
    for f, value in enumerate(dense):
        for h in range(group):
            spread[pl.ds(h * width + f * nx * group + h, nx, group), :] = value
    for i, (a, b) in enumerate(zip(parts[0], parts[-1])):
        edge_ref[0, i] = a
        edge_ref[1, i] = shift(b, step - ny, 1)
    owner = jnp.concatenate([owner_ref[k] for k in range(lines)], axis=1).astype(jnp.float32)
    own = jnp.broadcast_to(owner, (columns, columns))
    own_t = own.T

    def place(dim):
        at = lax.broadcasted_iota(jnp.int32, (columns, columns), dim)
        return (at % ny) * lines + at // ny

    ahead = (own == own_t) & (place(0) < place(1))
    rank = jnp.sum(jnp.where(ahead, 1.0, 0.0), axis=0, keepdims=True)
    target_ref[...] = jnp.broadcast_to(owner * msg.slots + rank, target_ref.shape)


def lane_of(side, piece, place, group):
    return (side * PIECES + piece) * group + place


def product(selection, values):
    return lax.dot_general(
        selection.astype(jnp.bfloat16), values, (((1,), (1,)), ((), ())), preferred_element_type=jnp.float32
    )


def folded(msg, picked):
    every = msg.owners * msg.extra_rows
    return jnp.concatenate([picked[a * every : (a + 1) * every] for a in range(msg.fold)], axis=1)


def select_kernel(sizes, msg, direct, spread, edge_ref, target_ref, edge_out, *outs):
    _, ny, nz = sizes
    group, width, columns = msg.group, spread_rows(msg), ny * (nz // STRIDE)
    edge_out[...] = edge_ref[...]
    target = target_ref[0:1]
    z_me, y_me = place_of(direct)
    at = lax.broadcasted_iota(jnp.int32, (1, columns), 1) % ny
    edges = jnp.full((1, columns), -1.0)
    for side, y in enumerate((0, ny - 1)):
        for p in range(PIECES):
            for h in range(group):
                some = jnp.where(at == y, target - float(h), -1.0)
                edges = jnp.maximum(edges, shift(some, lane_of(side, p, h, group) - y, 1))

    def slot_of(rows, first):
        row = lax.broadcasted_iota(jnp.int32, (msg.owners * rows, columns), 0)
        block = row // rows
        own_of = 2 * ((block // 2) ^ z_me) + ((block % 2) ^ y_me)
        return (own_of * msg.slots + (first + row % rows) * group).astype(jnp.float32)

    def pick(rows, folds, first, count):
        slot = jnp.concatenate([slot_of(rows, a * rows) for a in range(folds)], axis=0)
        every = [jnp.where(slot == target - float(h), 1.0, 0.0) for h in range(group)]
        every = jnp.concatenate(every, axis=1).astype(jnp.bfloat16)
        value = jnp.concatenate([spread[pl.ds(h * width + first, count), :] for h in range(group)], axis=1)
        out = []
        for _ in range(PIECES):
            out.append(value.astype(jnp.bfloat16))
            value = value - out[-1].astype(jnp.float32)
        picked = product(jnp.concatenate([every] * PIECES, axis=1), jnp.concatenate(out, axis=1))
        return picked, jnp.where(slot == edges, 1.0, 0.0)

    outs[0][...], outs[1][...] = pick(msg.rows, 1, 0, LANES)
    if msg.extra:
        picked, outs[3][...] = pick(msg.extra_rows, msg.fold, LANES, msg.extra * msg.part)
        outs[2][...] = folded(msg, picked)


def pack_kernel(sizes, msg, n_far, edge_ref, y_near, y_far, top_ref, x_first, main_ref, main_edges, *rest):
    nx, ny, nz = sizes
    group = msg.group
    (extra_ref, extra_edges), rest = (rest[:2], rest[2:]) if msg.extra else ((None, None), rest)
    far, x_out, outs, spread = rest[:n_far], rest[n_far], rest[n_far + 1 : -1], rest[-1]
    x_out[...] = x_first[...]
    on = lax.broadcasted_iota(jnp.int32, (nx, nz), 1) % STRIDE == 0
    spread[pl.ds(0, LANES), :] = jnp.zeros((LANES, spread.shape[1]), jnp.float32)
    rows = [[None] * group for _ in range(FIELDS)]
    cells = sides([y_near[f] for f in range(FIELDS)], [y_far[f] for f in range(FIELDS)], "sect")
    for side, cell in enumerate(cells):
        beyond = flux_parts(cell, *derived(cell), 1)
        edge = [edge_ref[side, i] for i in range(len(beyond))]
        faces = face(edge, beyond) if side else [-a for a in face(beyond, edge)]
        for f, value in enumerate(faces):
            value = jnp.where(on, value, 0.0)
            for p in range(PIECES):
                piece = value.astype(jnp.bfloat16).astype(jnp.float32)
                value = value - piece
                for h in range(group):
                    moved = shift(piece, lane_of(side, p, h, group), 1)
                    rows[f][h] = moved if rows[f][h] is None else rows[f][h] + moved
    for f in range(FIELDS):
        for h in range(group):
            spread[pl.ds((FIELDS + f) * nx * group + h, nx, group), :] = rows[f][h]
    top = jnp.maximum(jnp.maximum(top_ref[...], y_near[FIELDS]), y_far[FIELDS])
    for ref in far:
        top = jnp.maximum(top, ref[...])
    top = jnp.broadcast_to(jnp.max(top, keepdims=True), top.shape)
    per = msg.count
    each = msg.owners // len(outs)
    picked = main_ref[...] + product(main_edges[...], spread[pl.ds(0, LANES), :].astype(jnp.bfloat16))
    for b in range(msg.owners):
        at = (b % each) // 2 * per + b % 2 * msg.rows
        outs[b // each][pl.ds(at, msg.rows), :] = picked[b * msg.rows : (b + 1) * msg.rows]
    if msg.extra:
        rows = msg.extra_rows
        values = spread[pl.ds(LANES, msg.extra * msg.part), :].astype(jnp.bfloat16)
        picked = extra_ref[...] + folded(msg, product(extra_edges[...], values))
        for b in range(msg.owners):
            at = (b % each) // 2 * per + 2 * msg.rows + b % 2 * rows
            outs[b // each][pl.ds(at, rows), :] = picked[b * rows : (b + 1) * rows]
    for out in outs:
        for d in range(each // 2):
            out[pl.ds((d + 1) * per - ROWS, ROWS), :] = top


def merge_kernel(msg, firsts, *refs):
    *refs, other_ref, own_ref = refs
    half, top = msg.owners // 2, None
    for first, ref in zip(firsts, refs):
        for d in range(ref.shape[0] // msg.count):
            at, to = d * msg.count, first + d
            for odd, out in ((0, own_ref), (1, other_ref)):
                out[pl.ds(to * msg.rows, msg.rows), :] = ref[pl.ds(at + odd * msg.rows, msg.rows), :]
                if msg.extra:
                    rows = msg.extra_rows
                    out[pl.ds(half * msg.rows + to * rows, rows), :] = ref[
                        pl.ds(at + 2 * msg.rows + odd * rows, rows), :
                    ]
            new = ref[pl.ds(at + msg.count - ROWS, ROWS), :]
            top = new if top is None else jnp.maximum(top, new)
    for out in (own_ref, other_ref):
        out[pl.ds(half * (msg.rows + msg.extra_rows), ROWS), :] = top


def hold_kernel(*refs):
    half = len(refs) // 2
    for ref, out in zip(refs[:half], refs[half:]):
        out[...] = ref[...]


def change_kernel(sizes, r_ref, v_ref, p_ref, x_low, x_high, y_near, y_far, out_ref, state_ref):
    nx, ny, nz = sizes
    every = range(FIELDS)
    y_low, y_high = sides([y_near[f] for f in every], [y_far[f] for f in every], "sect")
    row = lax.broadcasted_iota(jnp.int32, (ny, nz), 0)
    half = 0.5

    def layer(x):
        if x < 0:
            return [x_low[f] for f in range(FIELDS)]
        if x >= nx:
            return [x_high[f] for f in range(FIELDS)]
        return fields_of(r_ref, v_ref, p_ref, pl.ds(x * ny, ny))

    def prepared(x):
        cell = layer(x)
        state, sound = derived(cell)
        return cell, state, sound, flux_parts(cell, state, sound, 0)

    previous = prepared(-1)
    here = prepared(0)
    x_face = face(previous[3], here[3])
    for x in range(nx):
        following = prepared(x + 1)
        cell, state, sound, parts = here
        next_face = face(parts, following[3])
        total = [a - b for a, b in zip(next_face, x_face)]
        x_face = next_face
        low_cell = [y_low[f][x : x + 1] for f in range(FIELDS)]
        high_cell = [y_high[f][x : x + 1] for f in range(FIELDS)]
        low = flux_parts(low_cell, *derived(low_cell), 1)
        high = flux_parts(high_cell, *derived(high_cell), 1)
        parts = flux_parts(cell, state, sound, 1)
        plus = [jnp.where(row == ny - 1, h, shift(a, -1, 0)) for a, h in zip(parts, high)]
        after = face(parts, plus)
        edge = face(low, [a[0:1] for a in parts])
        before = [jnp.where(row == 0, e, shift(a, 1, 0)) for a, e in zip(after, edge)]
        total = [t + (a - b) for t, a, b in zip(total, after, before)]
        parts = flux_parts(cell, state, sound, 2)
        after = face(parts, [shift(a, -1, 1) for a in parts])
        total = [t + (a - shift(a, 1, 1)) for t, a in zip(total, after)]
        for f in range(FIELDS):
            out_ref[f, pl.ds(x * ny, ny), :] = half * total[f]
            state_ref[f, pl.ds(x * ny, ny), :] = state[f]
        here = following


def final_kernel(sizes, msg, direct, state_ref, change_ref, other_ref, own_ref, kept_ref, *rest):
    new_hbm, depth_hbm, new_ref, depth_ref, main_ref, extra_ref, sems = rest
    nx, ny, nz = sizes
    n_owner, group, part = msg.owners, msg.group, msg.part
    half, length = n_owner // 2, nx * n_owner
    at = pl.ds(half * (msg.rows + msg.extra_rows), ROWS)
    top = jnp.maximum(other_ref[at, :], own_ref[at, :])
    step = COURANT / top[0:1, 0:1]
    writes = []
    for x in range(nx):
        rows = pl.ds(x * ny, ny)
        for f in range(FIELDS):
            new_ref[f, rows, :] = state_ref[f, rows, :] - step * change_ref[f, rows, :]
        writes.append(pltpu.make_async_copy(new_ref.at[:, rows], new_hbm.at[:, rows], sems.at[x]))
        writes[-1].start()
    z_me, y_me = place_of(direct)

    def settle(source, at, extra_at, d, odd):
        owner = 2 * (d ^ z_me) + (odd ^ y_me)
        main_ref[owner] = source[pl.ds(at, msg.rows), :]
        if msg.extra:
            extra_ref[owner] = source[pl.ds(extra_at, msg.extra_rows), :]

    for d in range(half):
        extra_at = half * msg.rows + d * msg.extra_rows
        if direct and d == 0:
            settle(kept_ref, 0, 2 * msg.rows, 0, 0)
        else:
            settle(own_ref, d * msg.rows, extra_at, d, 0)
        settle(other_ref, d * msg.rows, extra_at, d, 1)
    line = []
    for f in range(msg.main):
        line.append(jnp.concatenate([main_ref[q, :, pl.ds(f * part, part)] for q in range(n_owner)], axis=1))
    for f in range(msg.extra):
        folds = []
        for a in range(msg.fold):
            at = pl.ds((a * msg.extra + f) * part, part)
            folds.append(jnp.concatenate([extra_ref[q, :, at] for q in range(n_owner)], axis=1))
        line.append(jnp.concatenate(folds, axis=0))
    cell, change = line[:FIELDS], line[FIELDS:]
    taken = cell[0] > 0.0
    cell[0] = jnp.where(taken, cell[0], 1.0)
    state, sound = derived(cell)
    parts = flux_parts(cell, state, sound, 0)
    after = face(parts, [shift(a, -group, 1) for a in parts])
    change = [c + (a - shift(a, group, 1)) for c, a in zip(change, after)]
    new = [s - (0.5 * step) * c for s, c in zip(state, change)]
    density = new[0]
    pressure = (GAMMA - 1.0) * (new[4] - 0.5 * (new[1] * new[1] + new[2] * new[2] + new[3] * new[3]) / density)
    broadening = TURBULENT + pressure / density
    inverse = 1.0 / (BAND / 64.0 * jnp.sqrt(broadening))
    amplitude = NORMALISE * (density * density) * jnp.exp(-0.7 * jnp.log(broadening)) * inverse
    amplitude = jnp.where(taken, amplitude, 0.0)
    scaled = inverse * math.sqrt(math.log2(math.e))
    centre = (BAND / 8.0) * (new[1] / density)
    turns = BAND // length
    block = min(length, UNROLL)

    def skewers(rows):
        scale, middle, size = scaled[:rows], centre[:rows], amplitude[:rows]
        strides = [scale * float(length * m) for m in range(turns)]

        def offsets(count, running):
            e = (length - block - block * count) * 1.0 - float(BAND // 2)
            for b in range(block):
                start = (e + float(b) - middle) * scale
                total = None
                for m in range(turns):
                    t = start + strides[m] if m else start
                    value = jnp.exp2(-(t * t))
                    total = value if total is None else total + value
                part = shift(size * total, b * group, 1)
                block_sum = part if b == 0 else block_sum + part
            return block_sum if running is None else shift(running, block * group, 1) + block_sum

        if length == block:
            running = offsets(0, None)
        else:
            running = lax.fori_loop(
                0,
                length // block,
                lambda i, c: offsets(i.astype(jnp.float32), c),
                jnp.zeros_like(size),
            )
        running = shift(running, -(BAND // 2) * group, 1)
        if group > 1:
            wide = jnp.broadcast_to(running[:, None, :], (rows, group, group * length))
            wide = wide.reshape(rows * group, group * length)
            at = lax.broadcasted_iota(jnp.int32, wide.shape, 1)
            of = lax.broadcasted_iota(jnp.int32, wide.shape, 0)
            wide = jnp.where(at % group == of % group, wide, 0.0)
            at = lax.broadcasted_iota(jnp.int32, (group * length, length), 0)
            of = lax.broadcasted_iota(jnp.int32, (group * length, length), 1)
            pick = jnp.where(at // group == of, 1.0, 0.0)
            pieces = []
            for _ in range(PIECES):
                pieces.append(wide.astype(jnp.bfloat16))
                wide = wide - pieces[-1].astype(jnp.float32)
            pick = jnp.concatenate([pick.astype(jnp.bfloat16)] * PIECES, axis=0)
            running = jnp.dot(jnp.concatenate(pieces, axis=1), pick, preferred_element_type=jnp.float32)
        depth_ref[pl.ds(0, rows * group), :] = running

    if msg.rows > ROWS:
        some = kept_ref if direct else own_ref
        more = jnp.max(some[pl.ds(ROWS, msg.rows - ROWS), pl.ds(0, part)]) > 0.0

        @pl.when(more)
        def _():
            skewers(msg.rows)

        @pl.when(jnp.logical_not(more))
        def _():
            depth_ref[...] = jnp.zeros_like(depth_ref)
            skewers(ROWS)

    else:
        skewers(msg.rows)
    writes.append(pltpu.make_async_copy(depth_ref, depth_hbm, sems.at[nx]))
    writes[-1].start()
    for write in writes:
        write.wait()


def around(value, axis, amount):
    count = lax.axis_size(axis)
    return lax.ppermute(value, axis, [(i, (i + amount) % count) for i in range(count)])


def to_partner(value, axis, bits):
    return lax.ppermute(value, axis, [(i, i ^ bits) for i in range(lax.axis_size(axis))])


def crossed(value, bits):
    count = lax.axis_size("slab")
    every = [(s, q) for s in range(lax.axis_size("sect")) for q in range(count)]
    pairs = [(s * count + q, (s ^ 1) * count + (q ^ bits)) for s, q in every]
    return lax.ppermute(value, ("sect", "slab"), pairs)


def to_other(value, axis):
    count = lax.axis_size(axis)
    return lax.ppermute(value, axis, [(i, (i + 2 * (i % 2) - 1) % count) for i in range(count)])


def body(density, velocity, pressure, owners):
    sizes = nx, ny, nz = density.shape
    n_sect, n_slab = lax.axis_size("sect"), lax.axis_size("slab")
    lines = nz // STRIDE
    columns = ny * lines
    slots = 2 * columns // n_slab
    length = nx * n_slab
    group = max(1, LANES // length)
    geometry = shape_of_message(nx, n_slab, slots, group)
    gas = (
        density.reshape(nx * ny, nz),
        velocity.reshape(3 * nx * ny, nz),
        pressure.reshape(nx * ny, nz),
    )
    cells = nx * ny * nz
    half = n_slab // 2
    direct = half <= 4
    x_edge, y_edge, row = (FIELDS, ny, nz), (FIELDS + 1, nx, nz), (ROWS, nz)
    owners = jnp.transpose(owners, (1, 2, 0))
    shapes = [(a.shape, a.dtype) for a in (*gas, owners)]
    x_first, x_last, y_near, y_far, top, *gas, owners = call(
        functools.partial(edges_kernel, sizes),
        [x_edge, x_edge, y_edge, (FIELDS, nx, nz), row, *shapes],
        "edges",
        20 * cells,
        [pltpu.SemaphoreType.DMA((4,))],
        in_specs=[HBM] * 4,
    )(*(pltpu.with_memory_space_constraint(a, pltpu.HBM) for a in (*gas, owners)))
    parts = (2, 2 * FIELDS + 1, nx, nz)
    spread, edge, target = call(
        functools.partial(prepare_kernel, sizes, geometry),
        [(group * spread_rows(geometry), columns), parts, (ROWS, columns)],
        "prepare",
        PREPARE_COST * cells,
    )(*gas, owners)
    y_near = to_partner(y_near, "sect", 1)
    y_far, edge = call(join_kernel, [y_edge, parts], "join", cells)(y_far, top, y_near, edge)
    y_far = to_other(y_far, "sect")
    selected = [(n_slab * geometry.rows, LANES), (n_slab * geometry.rows, columns)]
    if geometry.extra:
        count = n_slab * geometry.extra_rows
        selected += [(count, LANES), (geometry.fold * count, columns)]
    edge, *selected = call(
        functools.partial(select_kernel, sizes, geometry, direct),
        [parts, *selected],
        "select",
        SELECT_COST * cells,
    )(spread, edge, target)
    far = [around(top, "sect", d) for d in range(2, n_sect - 1)] if n_sect > 4 else []
    x_low = around(x_last, "slab", 1)
    firsts = range(half) if direct else range(1)
    x_first, *packed = call(
        functools.partial(pack_kernel, sizes, geometry, len(far)),
        [x_edge] + [(half // len(firsts) * geometry.count, LANES)] * len(firsts),
        "pack",
        PACK_COST * cells,
        [pltpu.VMEM((spread_rows(geometry), columns), jnp.float32)],
    )(edge, y_near, y_far, top, x_first, *selected, *far)
    shapes = [a.shape for a in (x_low, x_first, packed[0])]
    x_low, x_first, first = call(hold_kernel, shapes, "hold", HOLD_COST * cells)(x_low, x_first, packed[0])
    x_high = around(x_first, "slab", -1)
    merge = functools.partial(
        call,
        out_shapes=[(half * (geometry.rows + geometry.extra_rows) + ROWS, LANES)] * 2,
        name="merge",
        flops=MERGE_COST * cells,
    )
    if direct:
        arrived = [crossed(m, 2 * d) for d, m in zip(firsts, [first, *packed[1:]])]
        turn = [2, 3, 1, 0] if half == 4 else list(firsts)
        other, own = merge(functools.partial(merge_kernel, geometry, turn))(*(arrived[d] for d in turn))
        other, own = crossed(other, 1), crossed(own, 0)
    else:
        alike = [[2 * i + odd for i in range(half)] for odd in range(2)]
        arrived = [
            lax.all_to_all(m, "slab", split_axis=0, concat_axis=0, axis_index_groups=alike, tiled=True) for m in packed
        ]
        other, own = merge(functools.partial(merge_kernel, geometry, firsts))(*arrived)
        other = to_partner(other, "slab", 1)
    change, state = call(
        functools.partial(change_kernel, sizes),
        [(FIELDS, nx * ny, nz)] * 2,
        "change",
        300_000 * cells,
    )(*gas, x_low, x_high, y_near, y_far)
    new_state, depth = call(
        functools.partial(final_kernel, sizes, geometry, direct),
        [(FIELDS, nx * ny, nz), (slots, length)],
        "final",
        100 * cells,
        [
            pltpu.VMEM((FIELDS, nx * ny, nz), jnp.float32),
            pltpu.VMEM((slots, length), jnp.float32),
            pltpu.VMEM((n_slab, geometry.rows, LANES), jnp.float32),
            pltpu.VMEM((n_slab, max(1, geometry.extra_rows), LANES), jnp.float32),
            pltpu.SemaphoreType.DMA((nx + 1,)),
        ],
        out_specs=[HBM, HBM],
    )(state, change, other, own, packed[0])
    return (new_state.reshape(FIELDS, nx, ny, nz), depth.reshape(1, 1, slots, length))


def solution(mesh):
    in_specs = (
        P("slab", "sect", None),
        P(None, "slab", "sect", None),
        P("slab", "sect", None),
        P("sect", None, None),
    )
    out_specs = (P(None, "slab", "sect", None), P("sect", "slab", None, None))
    return jax.shard_map(body, mesh=mesh, in_specs=in_specs, out_specs=out_specs, check_vma=False)
```

```python
import functools
import math
from typing import NamedTuple

import jax
import jax.numpy as jnp
from jax import lax
from jax.experimental import pallas as pl
from jax.experimental.pallas import tpu as pltpu
from jax.sharding import PartitionSpec as P

STRIDE = 32
BAND = 512

GAMMA = 5.0 / 3.0
COURANT = 0.15
TURBULENT = 0.25
NORMALISE = 0.5641895835477563

LANES = 128
ROWS = 8
FIELDS = 5
UNROLL = 64
PACK_COST = 30_000
PREPARE_COST = 300
SELECT_COST = 300
PIECES = 3
MERGE_COST = 30_000
HOLD_COST = 1

VMEM = pl.BlockSpec(memory_space=pltpu.VMEM)


HBM = pl.BlockSpec(memory_space=pltpu.HBM)


class Message(NamedTuple):
    owners: int
    slots: int
    group: int
    rows: int
    part: int
    main: int
    extra: int
    fold: int
    extra_rows: int
    count: int


def shape_of_message(nx, owners, slots, group):
    rows, part = slots // group, nx * group
    main = min(2 * FIELDS, LANES // part)
    extra = 2 * FIELDS - main
    fold = min(rows, LANES // (extra * part)) if extra else 1
    extra_rows = rows // fold if extra else 0
    count = 2 * rows + 2 * extra_rows + ROWS
    return Message(owners, slots, group, rows, part, main, extra, fold, extra_rows, count)


def call(kernel, out_shapes, name, flops, scratch=(), in_specs=None, out_specs=None):
    more = {} if in_specs is None else {"in_specs": in_specs}
    return pl.pallas_call(
        kernel,
        out_shape=[
            jax.ShapeDtypeStruct(*s) if isinstance(s[0], tuple) else jax.ShapeDtypeStruct(s, jnp.float32)
            for s in out_shapes
        ],
        out_specs=out_specs or [VMEM] * len(out_shapes),
        **more,
        scratch_shapes=list(scratch),
        compiler_params=pltpu.CompilerParams(vmem_limit_bytes=24 * 1024 * 1024),
        cost_estimate=pl.CostEstimate(flops=flops, bytes_accessed=1 << 20, transcendentals=0),
        name=name,
    )


def shift(array, amount, axis):
    size = array.shape[axis]
    amount = amount % size
    return array if amount == 0 else pltpu.roll(array, amount, axis)


def derived(cell):
    r, u, v, w, p = cell
    m = (r * u, r * v, r * w)
    energy = p * (1.0 / (GAMMA - 1.0)) + 0.5 * (m[0] * u + m[1] * v + m[2] * w)
    sound = jnp.sqrt(GAMMA * p / r)
    return (r, *m, energy), sound


def flux_parts(cell, state, sound, d):
    moving = cell[1 + d]
    flux = [state[1 + d]]
    for k in range(3):
        term = state[1 + k] * moving
        flux.append(term + cell[4] if k == d else term)
    flux.append((state[4] + cell[4]) * moving)
    return (*state, *flux, jnp.abs(moving) + sound)


def face(left, right):
    speed = jnp.maximum(left[10], right[10])
    return [
        (left[5 + k] + right[5 + k]) - speed * (right[k] - left[k]) for k in range(FIELDS)
    ]


def fields_of(r_ref, v_ref, p_ref, index):
    total = r_ref.shape[0]
    first = index.start if isinstance(index, pl.Slice) else index
    out = [r_ref[index]]
    for k in range(3):
        if isinstance(index, pl.Slice):
            out.append(v_ref[pl.ds(k * total + first, index.size, index.stride)])
        else:
            out.append(v_ref[k * total + index])
    out.append(p_ref[index])
    return out


def place_of(direct):
    me = lax.axis_index("slab")
    return (me // 2 if direct else 0), me % 2


def is_odd(axis, shape):
    return jnp.full(shape, lax.axis_index(axis) % 2) == 1


def sides(near, far, axis):
    odd = is_odd(axis, near[0].shape)
    low = [jnp.where(odd, n, f) for n, f in zip(near, far)]
    high = [jnp.where(odd, f, n) for n, f in zip(near, far)]
    return low, high


def edges_kernel(
    sizes, r_hbm, v_hbm, p_hbm, o_hbm, x_first, x_last, y_near, y_far, top_ref, r_ref, v_ref, p_ref, o_ref, sems
):
    nx, ny, nz = sizes
    pairs = [(r_hbm, r_ref), (v_hbm, v_ref), (p_hbm, p_ref), (o_hbm, o_ref)]
    loads = [pltpu.make_async_copy(source, target, sems.at[i]) for i, (source, target) in enumerate(pairs)]
    for load in loads:
        load.start()
    for load in loads:
        load.wait()
    for out, x in ((x_first, 0), (x_last, nx - 1)):
        for f, value in enumerate(fields_of(r_ref, v_ref, p_ref, pl.ds(x * ny, ny))):
            out[f] = value
    first, last = (fields_of(r_ref, v_ref, p_ref, pl.ds(y, nx, ny)) for y in (0, ny - 1))
    far, near = sides(last, first, "sect")
    for f in range(FIELDS):
        y_near[f] = near[f]
        y_far[f] = far[f]
    top = jnp.zeros((ROWS, nz), jnp.float32)
    for row in range(0, nx * ny, ROWS):
        r, u, v, w, p = fields_of(r_ref, v_ref, p_ref, pl.ds(row, ROWS))
        speed = jnp.maximum(jnp.maximum(jnp.abs(u), jnp.abs(v)), jnp.abs(w)) + jnp.sqrt(GAMMA * p / r)
        top = jnp.maximum(top, speed)
    y_near[FIELDS] = top
    top_ref[...] = top


def join_kernel(y_far, top_ref, near_ref, edge_ref, out_ref, edge_out):
    for f in range(FIELDS):
        out_ref[f] = y_far[f]
    out_ref[FIELDS] = jnp.maximum(top_ref[...], near_ref[FIELDS])
    edge_out[...] = edge_ref[...]


def spread_rows(msg):
    return LANES + msg.extra * msg.part


def prepare_kernel(sizes, msg, r_ref, v_ref, p_ref, owner_ref, spread, edge_ref, target_ref):
    nx, ny, nz = sizes
    lines = nz // STRIDE
    columns = ny * lines
    step = STRIDE // ROWS
    lane = lax.broadcasted_iota(jnp.int32, (nx, nz), 1)
    first = lane % STRIDE < step
    last = lane % STRIDE >= ny - step
    tiles, changes, parts = [], [], []
    for t in range(step):
        cell = None
        for s in range(ny // step):
            rows = fields_of(r_ref, v_ref, p_ref, pl.ds(step * s + t, nx, ny))
            rows = [shift(a, step * s, 1) for a in rows]
            if cell is None:
                cell = rows
            else:
                mine = (lane - step * s + 1) % STRIDE < 3
                cell = [jnp.where(mine, a, b) for a, b in zip(rows, cell)]
        state, sound = derived(cell)
        here = flux_parts(cell, state, sound, 2)
        after = face(here, [shift(a, -1, 1) for a in here])
        tiles.append(cell)
        changes.append([a - shift(a, 1, 1) for a in after])
        parts.append(flux_parts(cell, state, sound, 1))
    inner = [face(a, b) for a, b in zip(parts, parts[1:])]
    around_face = face([shift(a, step, 1) for a in parts[-1]], parts[0])
    low = [jnp.where(first, 0.0, a) for a in around_face]
    high = [jnp.where(last, 0.0, shift(a, -step, 1)) for a in around_face]
    faces = [low, *inner, high]
    dense = None
    for t in range(step):
        total = [c + (b - a) for c, a, b in zip(changes[t], faces[t], faces[t + 1])]
        values = [shift(a, t, 1) for a in [*tiles[t], *total]]
        dense = values if dense is None else [jnp.where(lane % step == t, a, b) for a, b in zip(values, dense)]
    group, width = msg.group, spread_rows(msg)
    spread[...] = jnp.zeros_like(spread)
    for f, value in enumerate(dense):
        for h in range(group):
            spread[pl.ds(h * width + f * nx * group + h, nx, group), :] = value
    for i, (a, b) in enumerate(zip(parts[0], parts[-1])):
        edge_ref[0, i] = a
        edge_ref[1, i] = shift(b, step - ny, 1)
    owner = jnp.concatenate([owner_ref[k] for k in range(lines)], axis=1).astype(jnp.float32)
    own = jnp.broadcast_to(owner, (columns, columns))
    own_t = own.T

    def place(dim):
        at = lax.broadcasted_iota(jnp.int32, (columns, columns), dim)
        return (at % ny) * lines + at // ny

    ahead = (own == own_t) & (place(0) < place(1))
    rank = jnp.sum(jnp.where(ahead, 1.0, 0.0), axis=0, keepdims=True)
    target_ref[...] = jnp.broadcast_to(owner * msg.slots + rank, target_ref.shape)


def lane_of(side, piece, place, group):
    return (side * PIECES + piece) * group + place


def product(selection, values):
    return lax.dot_general(
        selection.astype(jnp.bfloat16), values, (((1,), (1,)), ((), ())), preferred_element_type=jnp.float32
    )


def folded(msg, picked):
    every = msg.owners * msg.extra_rows
    return jnp.concatenate([picked[a * every : (a + 1) * every] for a in range(msg.fold)], axis=1)


def select_kernel(sizes, msg, direct, spread, edge_ref, target_ref, edge_out, *outs):
    _, ny, nz = sizes
    group, width, columns = msg.group, spread_rows(msg), ny * (nz // STRIDE)
    edge_out[...] = edge_ref[...]
    target = target_ref[0:1]
    z_me, y_me = place_of(direct)
    at = lax.broadcasted_iota(jnp.int32, (1, columns), 1) % ny
    edges = jnp.full((1, columns), -1.0)
    for side, y in enumerate((0, ny - 1)):
        for p in range(PIECES):
            for h in range(group):
                some = jnp.where(at == y, target - float(h), -1.0)
                edges = jnp.maximum(edges, shift(some, lane_of(side, p, h, group) - y, 1))

    def slot_of(rows, first):
        row = lax.broadcasted_iota(jnp.int32, (msg.owners * rows, columns), 0)
        block = row // rows
        own_of = 2 * ((block // 2) ^ z_me) + ((block % 2) ^ y_me)
        return (own_of * msg.slots + (first + row % rows) * group).astype(jnp.float32)

    def pick(rows, folds, first, count):
        slot = jnp.concatenate([slot_of(rows, a * rows) for a in range(folds)], axis=0)
        every = [jnp.where(slot == target - float(h), 1.0, 0.0) for h in range(group)]
        every = jnp.concatenate(every, axis=1).astype(jnp.bfloat16)
        value = jnp.concatenate([spread[pl.ds(h * width + first, count), :] for h in range(group)], axis=1)
        out = []
        for _ in range(PIECES):
            out.append(value.astype(jnp.bfloat16))
            value = value - out[-1].astype(jnp.float32)
        picked = product(jnp.concatenate([every] * PIECES, axis=1), jnp.concatenate(out, axis=1))
        return picked, jnp.where(slot == edges, 1.0, 0.0)

    outs[0][...], outs[1][...] = pick(msg.rows, 1, 0, LANES)
    if msg.extra:
        picked, outs[3][...] = pick(msg.extra_rows, msg.fold, LANES, msg.extra * msg.part)
        outs[2][...] = folded(msg, picked)


def pack_kernel(sizes, msg, n_far, edge_ref, y_near, y_far, top_ref, main_ref, main_edges, *rest):
    nx, ny, nz = sizes
    group = msg.group
    (extra_ref, extra_edges), rest = (rest[:2], rest[2:]) if msg.extra else ((None, None), rest)
    far, outs, spread = rest[:n_far], rest[n_far:-1], rest[-1]
    on = lax.broadcasted_iota(jnp.int32, (nx, nz), 1) % STRIDE == 0
    spread[pl.ds(0, LANES), :] = jnp.zeros((LANES, spread.shape[1]), jnp.float32)
    rows = [[None] * group for _ in range(FIELDS)]
    cells = sides([y_near[f] for f in range(FIELDS)], [y_far[f] for f in range(FIELDS)], "sect")
    for side, cell in enumerate(cells):
        beyond = flux_parts(cell, *derived(cell), 1)
        edge = [edge_ref[side, i] for i in range(len(beyond))]
        faces = face(edge, beyond) if side else [-a for a in face(beyond, edge)]
        for f, value in enumerate(faces):
            value = jnp.where(on, value, 0.0)
            for p in range(PIECES):
                piece = value.astype(jnp.bfloat16).astype(jnp.float32)
                value = value - piece
                for h in range(group):
                    moved = shift(piece, lane_of(side, p, h, group), 1)
                    rows[f][h] = moved if rows[f][h] is None else rows[f][h] + moved
    for f in range(FIELDS):
        for h in range(group):
            spread[pl.ds((FIELDS + f) * nx * group + h, nx, group), :] = rows[f][h]
    top = jnp.maximum(jnp.maximum(top_ref[...], y_near[FIELDS]), y_far[FIELDS])
    for ref in far:
        top = jnp.maximum(top, ref[...])
    top = jnp.broadcast_to(jnp.max(top, keepdims=True), top.shape)
    per = msg.count
    each = msg.owners // len(outs)
    picked = main_ref[...] + product(main_edges[...], spread[pl.ds(0, LANES), :].astype(jnp.bfloat16))
    for b in range(msg.owners):
        at = (b % each) // 2 * per + b % 2 * msg.rows
        outs[b // each][pl.ds(at, msg.rows), :] = picked[b * msg.rows : (b + 1) * msg.rows]
    if msg.extra:
        rows = msg.extra_rows
        values = spread[pl.ds(LANES, msg.extra * msg.part), :].astype(jnp.bfloat16)
        picked = extra_ref[...] + folded(msg, product(extra_edges[...], values))
        for b in range(msg.owners):
            at = (b % each) // 2 * per + 2 * msg.rows + b % 2 * rows
            outs[b // each][pl.ds(at, rows), :] = picked[b * rows : (b + 1) * rows]
    for out in outs:
        for d in range(each // 2):
            out[pl.ds((d + 1) * per - ROWS, ROWS), :] = top


def merge_kernel(msg, firsts, *refs):
    *refs, other_ref, own_ref = refs
    half, top = msg.owners // 2, None
    for first, ref in zip(firsts, refs):
        for d in range(ref.shape[0] // msg.count):
            at, to = d * msg.count, first + d
            for odd, out in ((0, own_ref), (1, other_ref)):
                out[pl.ds(to * msg.rows, msg.rows), :] = ref[pl.ds(at + odd * msg.rows, msg.rows), :]
                if msg.extra:
                    rows = msg.extra_rows
                    out[pl.ds(half * msg.rows + to * rows, rows), :] = ref[
                        pl.ds(at + 2 * msg.rows + odd * rows, rows), :
                    ]
            new = ref[pl.ds(at + msg.count - ROWS, ROWS), :]
            top = new if top is None else jnp.maximum(top, new)
    for out in (own_ref, other_ref):
        out[pl.ds(half * (msg.rows + msg.extra_rows), ROWS), :] = top


def hold_kernel(*refs):
    half = len(refs) // 2
    for ref, out in zip(refs[:half], refs[half:]):
        out[...] = ref[...]


def change_kernel(sizes, r_ref, v_ref, p_ref, x_low, x_high, y_near, y_far, out_ref, state_ref):
    nx, ny, nz = sizes
    every = range(FIELDS)
    y_low, y_high = sides([y_near[f] for f in every], [y_far[f] for f in every], "sect")
    row = lax.broadcasted_iota(jnp.int32, (ny, nz), 0)
    half = 0.5

    def layer(x):
        if x < 0:
            return [x_low[f] for f in range(FIELDS)]
        if x >= nx:
            return [x_high[f] for f in range(FIELDS)]
        return fields_of(r_ref, v_ref, p_ref, pl.ds(x * ny, ny))

    def prepared(x):
        cell = layer(x)
        state, sound = derived(cell)
        return cell, state, sound, flux_parts(cell, state, sound, 0)

    previous = prepared(-1)
    here = prepared(0)
    x_face = face(previous[3], here[3])
    for x in range(nx):
        following = prepared(x + 1)
        cell, state, sound, parts = here
        next_face = face(parts, following[3])
        total = [a - b for a, b in zip(next_face, x_face)]
        x_face = next_face
        low_cell = [y_low[f][x : x + 1] for f in range(FIELDS)]
        high_cell = [y_high[f][x : x + 1] for f in range(FIELDS)]
        low = flux_parts(low_cell, *derived(low_cell), 1)
        high = flux_parts(high_cell, *derived(high_cell), 1)
        parts = flux_parts(cell, state, sound, 1)
        plus = [jnp.where(row == ny - 1, h, shift(a, -1, 0)) for a, h in zip(parts, high)]
        after = face(parts, plus)
        edge = face(low, [a[0:1] for a in parts])
        before = [jnp.where(row == 0, e, shift(a, 1, 0)) for a, e in zip(after, edge)]
        total = [t + (a - b) for t, a, b in zip(total, after, before)]
        parts = flux_parts(cell, state, sound, 2)
        after = face(parts, [shift(a, -1, 1) for a in parts])
        total = [t + (a - shift(a, 1, 1)) for t, a in zip(total, after)]
        for f in range(FIELDS):
            out_ref[f, pl.ds(x * ny, ny), :] = half * total[f]
            state_ref[f, pl.ds(x * ny, ny), :] = state[f]
        here = following


def final_kernel(sizes, msg, direct, state_ref, change_ref, other_ref, own_ref, kept_ref, *rest):
    new_hbm, depth_hbm, new_ref, depth_ref, main_ref, extra_ref, sems = rest
    nx, ny, nz = sizes
    n_owner, group, part = msg.owners, msg.group, msg.part
    half, length = n_owner // 2, nx * n_owner
    at = pl.ds(half * (msg.rows + msg.extra_rows), ROWS)
    top = jnp.maximum(other_ref[at, :], own_ref[at, :])
    step = COURANT / top[0:1, 0:1]
    writes = []
    for x in range(nx):
        rows = pl.ds(x * ny, ny)
        for f in range(FIELDS):
            new_ref[f, rows, :] = state_ref[f, rows, :] - step * change_ref[f, rows, :]
        writes.append(pltpu.make_async_copy(new_ref.at[:, rows], new_hbm.at[:, rows], sems.at[x]))
        writes[-1].start()
    z_me, y_me = place_of(direct)

    def settle(source, at, extra_at, d, odd):
        owner = 2 * (d ^ z_me) + (odd ^ y_me)
        main_ref[owner] = source[pl.ds(at, msg.rows), :]
        if msg.extra:
            extra_ref[owner] = source[pl.ds(extra_at, msg.extra_rows), :]

    for d in range(half):
        extra_at = half * msg.rows + d * msg.extra_rows
        if direct and d == 0:
            settle(kept_ref, 0, 2 * msg.rows, 0, 0)
        else:
            settle(own_ref, d * msg.rows, extra_at, d, 0)
        settle(other_ref, d * msg.rows, extra_at, d, 1)
    line = []
    for f in range(msg.main):
        line.append(jnp.concatenate([main_ref[q, :, pl.ds(f * part, part)] for q in range(n_owner)], axis=1))
    for f in range(msg.extra):
        folds = []
        for a in range(msg.fold):
            at = pl.ds((a * msg.extra + f) * part, part)
            folds.append(jnp.concatenate([extra_ref[q, :, at] for q in range(n_owner)], axis=1))
        line.append(jnp.concatenate(folds, axis=0))
    cell, change = line[:FIELDS], line[FIELDS:]
    taken = cell[0] > 0.0
    cell[0] = jnp.where(taken, cell[0], 1.0)
    state, sound = derived(cell)
    parts = flux_parts(cell, state, sound, 0)
    after = face(parts, [shift(a, -group, 1) for a in parts])
    change = [c + (a - shift(a, group, 1)) for c, a in zip(change, after)]
    new = [s - (0.5 * step) * c for s, c in zip(state, change)]
    density = new[0]
    pressure = (GAMMA - 1.0) * (new[4] - 0.5 * (new[1] * new[1] + new[2] * new[2] + new[3] * new[3]) / density)
    broadening = TURBULENT + pressure / density
    inverse = 1.0 / (BAND / 64.0 * jnp.sqrt(broadening))
    amplitude = NORMALISE * (density * density) * jnp.exp(-0.7 * jnp.log(broadening)) * inverse
    amplitude = jnp.where(taken, amplitude, 0.0)
    scaled = inverse * math.sqrt(math.log2(math.e))
    centre = (BAND / 8.0) * (new[1] / density)
    turns = BAND // length
    block = min(length, UNROLL)

    def skewers(rows):
        scale, middle, size = scaled[:rows], centre[:rows], amplitude[:rows]
        strides = [scale * float(length * m) for m in range(turns)]

        def offsets(count, running):
            e = (length - block - block * count) * 1.0 - float(BAND // 2)
            for b in range(block):
                start = (e + float(b) - middle) * scale
                total = None
                for m in range(turns):
                    t = start + strides[m] if m else start
                    value = jnp.exp2(-(t * t))
                    total = value if total is None else total + value
                part = shift(size * total, b * group, 1)
                block_sum = part if b == 0 else block_sum + part
            return block_sum if running is None else shift(running, block * group, 1) + block_sum

        if length == block:
            running = offsets(0, None)
        else:
            running = lax.fori_loop(
                0,
                length // block,
                lambda i, c: offsets(i.astype(jnp.float32), c),
                jnp.zeros_like(size),
            )
        running = shift(running, -(BAND // 2) * group, 1)
        if group > 1:
            wide = jnp.broadcast_to(running[:, None, :], (rows, group, group * length))
            wide = wide.reshape(rows * group, group * length)
            at = lax.broadcasted_iota(jnp.int32, wide.shape, 1)
            of = lax.broadcasted_iota(jnp.int32, wide.shape, 0)
            wide = jnp.where(at % group == of % group, wide, 0.0)
            at = lax.broadcasted_iota(jnp.int32, (group * length, length), 0)
            of = lax.broadcasted_iota(jnp.int32, (group * length, length), 1)
            pick = jnp.where(at // group == of, 1.0, 0.0)
            pieces = []
            for _ in range(PIECES):
                pieces.append(wide.astype(jnp.bfloat16))
                wide = wide - pieces[-1].astype(jnp.float32)
            pick = jnp.concatenate([pick.astype(jnp.bfloat16)] * PIECES, axis=0)
            running = jnp.dot(jnp.concatenate(pieces, axis=1), pick, preferred_element_type=jnp.float32)
        depth_ref[pl.ds(0, rows * group), :] = running

    if msg.rows > ROWS:
        some = kept_ref if direct else own_ref
        more = jnp.max(some[pl.ds(ROWS, msg.rows - ROWS), pl.ds(0, part)]) > 0.0

        @pl.when(more)
        def _():
            skewers(msg.rows)

        @pl.when(jnp.logical_not(more))
        def _():
            depth_ref[...] = jnp.zeros_like(depth_ref)
            skewers(ROWS)

    else:
        skewers(msg.rows)
    writes.append(pltpu.make_async_copy(depth_ref, depth_hbm, sems.at[nx]))
    writes[-1].start()
    for write in writes:
        write.wait()


def around(value, axis, amount):
    count = lax.axis_size(axis)
    return lax.ppermute(value, axis, [(i, (i + amount) % count) for i in range(count)])


def to_partner(value, axis, bits):
    return lax.ppermute(value, axis, [(i, i ^ bits) for i in range(lax.axis_size(axis))])


def crossed(value, bits):
    count = lax.axis_size("slab")
    every = [(s, q) for s in range(lax.axis_size("sect")) for q in range(count)]
    pairs = [(s * count + q, (s ^ 1) * count + (q ^ bits)) for s, q in every]
    return lax.ppermute(value, ("sect", "slab"), pairs)


def to_other(value, axis):
    count = lax.axis_size(axis)
    return lax.ppermute(value, axis, [(i, (i + 2 * (i % 2) - 1) % count) for i in range(count)])


def body(density, velocity, pressure, owners):
    sizes = nx, ny, nz = density.shape
    n_sect, n_slab = lax.axis_size("sect"), lax.axis_size("slab")
    lines = nz // STRIDE
    columns = ny * lines
    slots = 2 * columns // n_slab
    length = nx * n_slab
    group = max(1, LANES // length)
    geometry = shape_of_message(nx, n_slab, slots, group)
    gas = (
        density.reshape(nx * ny, nz),
        velocity.reshape(3 * nx * ny, nz),
        pressure.reshape(nx * ny, nz),
    )
    cells = nx * ny * nz
    half = n_slab // 2
    direct = half <= 4
    x_edge, y_edge, row = (FIELDS, ny, nz), (FIELDS + 1, nx, nz), (ROWS, nz)
    owners = jnp.transpose(owners, (1, 2, 0))
    shapes = [(a.shape, a.dtype) for a in (*gas, owners)]
    x_first, x_last, y_near, y_far, top, *gas, owners = call(
        functools.partial(edges_kernel, sizes),
        [x_edge, x_edge, y_edge, (FIELDS, nx, nz), row, *shapes],
        "edges",
        20 * cells,
        [pltpu.SemaphoreType.DMA((4,))],
        in_specs=[HBM] * 4,
    )(*(pltpu.with_memory_space_constraint(a, pltpu.HBM) for a in (*gas, owners)))
    parts = (2, 2 * FIELDS + 1, nx, nz)
    spread, edge, target = call(
        functools.partial(prepare_kernel, sizes, geometry),
        [(group * spread_rows(geometry), columns), parts, (ROWS, columns)],
        "prepare",
        PREPARE_COST * cells,
    )(*gas, owners)
    y_near = to_partner(y_near, "sect", 1)
    y_far, edge = call(join_kernel, [y_edge, parts], "join", cells)(y_far, top, y_near, edge)
    y_far = to_other(y_far, "sect")
    selected = [(n_slab * geometry.rows, LANES), (n_slab * geometry.rows, columns)]
    if geometry.extra:
        count = n_slab * geometry.extra_rows
        selected += [(count, LANES), (geometry.fold * count, columns)]
    edge, *selected = call(
        functools.partial(select_kernel, sizes, geometry, direct),
        [parts, *selected],
        "select",
        SELECT_COST * cells,
    )(spread, edge, target)
    far = [around(top, "sect", d) for d in range(2, n_sect - 1)] if n_sect > 4 else []
    x_low = around(x_last, "slab", 1)
    firsts = range(half) if direct else range(1)
    packed = call(
        functools.partial(pack_kernel, sizes, geometry, len(far)),
        [(half // len(firsts) * geometry.count, LANES)] * len(firsts),
        "pack",
        PACK_COST * cells,
        [pltpu.VMEM((spread_rows(geometry), columns), jnp.float32)],
    )(edge, y_near, y_far, top, *selected, *far)
    shapes = [a.shape for a in (x_low, x_first, packed[0])]
    x_low, x_first, first = call(hold_kernel, shapes, "hold", HOLD_COST * cells)(x_low, x_first, packed[0])
    x_high = around(x_first, "slab", -1)
    merge = functools.partial(
        call,
        out_shapes=[(half * (geometry.rows + geometry.extra_rows) + ROWS, LANES)] * 2,
        name="merge",
        flops=MERGE_COST * cells,
    )
    if direct:
        arrived = [crossed(m, 2 * d) for d, m in zip(firsts, [first, *packed[1:]])]
        turn = [2, 3, 1, 0] if half == 4 else list(firsts)
        other, own = merge(functools.partial(merge_kernel, geometry, turn))(*(arrived[d] for d in turn))
        other, own = crossed(other, 1), crossed(own, 0)
    else:
        alike = [[2 * i + odd for i in range(half)] for odd in range(2)]
        arrived = [
            lax.all_to_all(m, "slab", split_axis=0, concat_axis=0, axis_index_groups=alike, tiled=True) for m in packed
        ]
        other, own = merge(functools.partial(merge_kernel, geometry, firsts))(*arrived)
        other = to_partner(other, "slab", 1)
    change, state = call(
        functools.partial(change_kernel, sizes),
        [(FIELDS, nx * ny, nz)] * 2,
        "change",
        300_000 * cells,
    )(*gas, x_low, x_high, y_near, y_far)
    new_state, depth = call(
        functools.partial(final_kernel, sizes, geometry, direct),
        [(FIELDS, nx * ny, nz), (slots, length)],
        "final",
        100 * cells,
        [
            pltpu.VMEM((FIELDS, nx * ny, nz), jnp.float32),
            pltpu.VMEM((slots, length), jnp.float32),
            pltpu.VMEM((n_slab, geometry.rows, LANES), jnp.float32),
            pltpu.VMEM((n_slab, max(1, geometry.extra_rows), LANES), jnp.float32),
            pltpu.SemaphoreType.DMA((nx + 1,)),
        ],
        out_specs=[HBM, HBM],
    )(state, change, other, own, packed[0])
    return (new_state.reshape(FIELDS, nx, ny, nz), depth.reshape(1, 1, slots, length))


def solution(mesh):
    in_specs = (
        P("slab", "sect", None),
        P(None, "slab", "sect", None),
        P("slab", "sect", None),
        P("sect", None, None),
    )
    out_specs = (P(None, "slab", "sect", None), P("sect", "slab", None, None))
    return jax.shard_map(body, mesh=mesh, in_specs=in_specs, out_specs=out_specs, check_vma=False)
```

```python
import functools
import math
from typing import NamedTuple

import jax
import jax.numpy as jnp
from jax import lax
from jax.experimental import pallas as pl
from jax.experimental.pallas import tpu as pltpu
from jax.sharding import PartitionSpec as P

STRIDE = 32
BAND = 512

GAMMA = 5.0 / 3.0
COURANT = 0.15
TURBULENT = 0.25
NORMALISE = 0.5641895835477563

LANES = 128
ROWS = 8
FIELDS = 5
UNROLL = 64
PACK_COST = 30_000
PREPARE_COST = 300
SELECT_COST = 300
PIECES = 3
MERGE_COST = 30_000
HOLD_COST = 1

VMEM = pl.BlockSpec(memory_space=pltpu.VMEM)


HBM = pl.BlockSpec(memory_space=pltpu.HBM)


class Message(NamedTuple):
    owners: int
    slots: int
    group: int
    rows: int
    part: int
    main: int
    extra: int
    fold: int
    extra_rows: int
    count: int


def shape_of_message(nx, owners, slots, group):
    rows, part = slots // group, nx * group
    main = min(2 * FIELDS, LANES // part)
    extra = 2 * FIELDS - main
    fold = min(rows, LANES // (extra * part)) if extra else 1
    extra_rows = rows // fold if extra else 0
    count = 2 * rows + 2 * extra_rows + ROWS
    return Message(owners, slots, group, rows, part, main, extra, fold, extra_rows, count)


def call(kernel, out_shapes, name, flops, scratch=(), in_specs=None, out_specs=None):
    more = {} if in_specs is None else {"in_specs": in_specs}
    return pl.pallas_call(
        kernel,
        out_shape=[
            jax.ShapeDtypeStruct(*s) if isinstance(s[0], tuple) else jax.ShapeDtypeStruct(s, jnp.float32)
            for s in out_shapes
        ],
        out_specs=out_specs or [VMEM] * len(out_shapes),
        **more,
        scratch_shapes=list(scratch),
        compiler_params=pltpu.CompilerParams(vmem_limit_bytes=24 * 1024 * 1024),
        cost_estimate=pl.CostEstimate(flops=flops, bytes_accessed=1 << 20, transcendentals=0),
        name=name,
    )


def shift(array, amount, axis):
    size = array.shape[axis]
    amount = amount % size
    return array if amount == 0 else pltpu.roll(array, amount, axis)


def derived(cell):
    r, u, v, w, p = cell
    m = (r * u, r * v, r * w)
    energy = p * (1.0 / (GAMMA - 1.0)) + 0.5 * (m[0] * u + m[1] * v + m[2] * w)
    sound = jnp.sqrt(GAMMA * p / r)
    return (r, *m, energy), sound


def flux_parts(cell, state, sound, d):
    moving = cell[1 + d]
    flux = [state[1 + d]]
    for k in range(3):
        term = state[1 + k] * moving
        flux.append(term + cell[4] if k == d else term)
    flux.append((state[4] + cell[4]) * moving)
    return (*state, *flux, jnp.abs(moving) + sound)


def face(left, right):
    speed = jnp.maximum(left[10], right[10])
    return [
        (left[5 + k] + right[5 + k]) - speed * (right[k] - left[k]) for k in range(FIELDS)
    ]


def fields_of(r_ref, v_ref, p_ref, index):
    total = r_ref.shape[0]
    first = index.start if isinstance(index, pl.Slice) else index
    out = [r_ref[index]]
    for k in range(3):
        if isinstance(index, pl.Slice):
            out.append(v_ref[pl.ds(k * total + first, index.size, index.stride)])
        else:
            out.append(v_ref[k * total + index])
    out.append(p_ref[index])
    return out


def place_of(direct):
    me = lax.axis_index("slab")
    return (me // 2 if direct else 0), me % 2


def is_odd(axis, shape):
    return jnp.full(shape, lax.axis_index(axis) % 2) == 1


def sides(near, far, axis):
    odd = is_odd(axis, near[0].shape)
    low = [jnp.where(odd, n, f) for n, f in zip(near, far)]
    high = [jnp.where(odd, f, n) for n, f in zip(near, far)]
    return low, high


def edges_kernel(
    sizes, r_hbm, v_hbm, p_hbm, o_hbm, x_first, x_last, y_near, y_far, top_ref, r_ref, v_ref, p_ref, o_ref, sems
):
    nx, ny, nz = sizes
    pairs = [(r_hbm, r_ref), (v_hbm, v_ref), (p_hbm, p_ref), (o_hbm, o_ref)]
    loads = [pltpu.make_async_copy(source, target, sems.at[i]) for i, (source, target) in enumerate(pairs)]
    for load in loads:
        load.start()
    for load in loads:
        load.wait()
    for out, x in ((x_first, 0), (x_last, nx - 1)):
        for f, value in enumerate(fields_of(r_ref, v_ref, p_ref, pl.ds(x * ny, ny))):
            out[f] = value
    first, last = (fields_of(r_ref, v_ref, p_ref, pl.ds(y, nx, ny)) for y in (0, ny - 1))
    far, near = sides(last, first, "sect")
    for f in range(FIELDS):
        y_near[f] = near[f]
        y_far[f] = far[f]
    top = jnp.zeros((ROWS, nz), jnp.float32)
    for row in range(0, nx * ny, ROWS):
        r, u, v, w, p = fields_of(r_ref, v_ref, p_ref, pl.ds(row, ROWS))
        speed = jnp.maximum(jnp.maximum(jnp.abs(u), jnp.abs(v)), jnp.abs(w)) + jnp.sqrt(GAMMA * p / r)
        top = jnp.maximum(top, speed)
    y_near[FIELDS] = top
    top_ref[...] = top


def join_kernel(y_far, top_ref, near_ref, target_ref, out_ref, target_out):
    for f in range(FIELDS):
        out_ref[f] = y_far[f]
    out_ref[FIELDS] = jnp.maximum(top_ref[...], near_ref[FIELDS])
    target_out[...] = target_ref[...]


def spread_rows(msg):
    return LANES + msg.extra * msg.part


def prepare_kernel(sizes, msg, r_ref, v_ref, p_ref, owner_ref, spread, edge_ref, target_ref):
    nx, ny, nz = sizes
    lines = nz // STRIDE
    columns = ny * lines
    step = STRIDE // ROWS
    lane = lax.broadcasted_iota(jnp.int32, (nx, nz), 1)
    first = lane % STRIDE < step
    last = lane % STRIDE >= ny - step
    tiles, changes, parts = [], [], []
    for t in range(step):
        cell = None
        for s in range(ny // step):
            rows = fields_of(r_ref, v_ref, p_ref, pl.ds(step * s + t, nx, ny))
            rows = [shift(a, step * s, 1) for a in rows]
            if cell is None:
                cell = rows
            else:
                mine = (lane - step * s + 1) % STRIDE < 3
                cell = [jnp.where(mine, a, b) for a, b in zip(rows, cell)]
        state, sound = derived(cell)
        here = flux_parts(cell, state, sound, 2)
        after = face(here, [shift(a, -1, 1) for a in here])
        tiles.append(cell)
        changes.append([a - shift(a, 1, 1) for a in after])
        parts.append(flux_parts(cell, state, sound, 1))
    inner = [face(a, b) for a, b in zip(parts, parts[1:])]
    around_face = face([shift(a, step, 1) for a in parts[-1]], parts[0])
    low = [jnp.where(first, 0.0, a) for a in around_face]
    high = [jnp.where(last, 0.0, shift(a, -step, 1)) for a in around_face]
    faces = [low, *inner, high]
    dense = None
    for t in range(step):
        total = [c + (b - a) for c, a, b in zip(changes[t], faces[t], faces[t + 1])]
        values = [shift(a, t, 1) for a in [*tiles[t], *total]]
        dense = values if dense is None else [jnp.where(lane % step == t, a, b) for a, b in zip(values, dense)]
    group, width = msg.group, spread_rows(msg)
    spread[...] = jnp.zeros_like(spread)
    for f, value in enumerate(dense):
        for h in range(group):
            spread[pl.ds(h * width + f * nx * group + h, nx, group), :] = value
    for i, (a, b) in enumerate(zip(parts[0], parts[-1])):
        edge_ref[0, i] = a
        edge_ref[1, i] = shift(b, step - ny, 1)
    owner = jnp.concatenate([owner_ref[k] for k in range(lines)], axis=1).astype(jnp.float32)
    own = jnp.broadcast_to(owner, (columns, columns))
    own_t = own.T

    def place(dim):
        at = lax.broadcasted_iota(jnp.int32, (columns, columns), dim)
        return (at % ny) * lines + at // ny

    ahead = (own == own_t) & (place(0) < place(1))
    rank = jnp.sum(jnp.where(ahead, 1.0, 0.0), axis=0, keepdims=True)
    target_ref[...] = jnp.broadcast_to(owner * msg.slots + rank, target_ref.shape)


def lane_of(side, piece, place, group):
    return (side * PIECES + piece) * group + place


def product(selection, values):
    return lax.dot_general(
        selection.astype(jnp.bfloat16), values, (((1,), (1,)), ((), ())), preferred_element_type=jnp.float32
    )


def folded(msg, picked):
    every = msg.owners * msg.extra_rows
    return jnp.concatenate([picked[a * every : (a + 1) * every] for a in range(msg.fold)], axis=1)


def select_kernel(sizes, msg, direct, spread, target_ref, *outs):
    _, ny, nz = sizes
    group, width, columns = msg.group, spread_rows(msg), ny * (nz // STRIDE)
    target = target_ref[0:1]
    z_me, y_me = place_of(direct)
    at = lax.broadcasted_iota(jnp.int32, (1, columns), 1) % ny
    edges = jnp.full((1, columns), -1.0)
    for side, y in enumerate((0, ny - 1)):
        for p in range(PIECES):
            for h in range(group):
                some = jnp.where(at == y, target - float(h), -1.0)
                edges = jnp.maximum(edges, shift(some, lane_of(side, p, h, group) - y, 1))

    def slot_of(rows, first):
        row = lax.broadcasted_iota(jnp.int32, (msg.owners * rows, columns), 0)
        block = row // rows
        own_of = 2 * ((block // 2) ^ z_me) + ((block % 2) ^ y_me)
        return (own_of * msg.slots + (first + row % rows) * group).astype(jnp.float32)

    def pick(rows, folds, first, count):
        slot = jnp.concatenate([slot_of(rows, a * rows) for a in range(folds)], axis=0)
        every = [jnp.where(slot == target - float(h), 1.0, 0.0) for h in range(group)]
        every = jnp.concatenate(every, axis=1).astype(jnp.bfloat16)
        value = jnp.concatenate([spread[pl.ds(h * width + first, count), :] for h in range(group)], axis=1)
        out = []
        for _ in range(PIECES):
            out.append(value.astype(jnp.bfloat16))
            value = value - out[-1].astype(jnp.float32)
        picked = product(jnp.concatenate([every] * PIECES, axis=1), jnp.concatenate(out, axis=1))
        return picked, jnp.where(slot == edges, 1.0, 0.0)

    outs[0][...], outs[1][...] = pick(msg.rows, 1, 0, LANES)
    if msg.extra:
        picked, outs[3][...] = pick(msg.extra_rows, msg.fold, LANES, msg.extra * msg.part)
        outs[2][...] = folded(msg, picked)


def pack_kernel(sizes, msg, n_far, edge_ref, y_near, y_far, top_ref, main_ref, main_edges, *rest):
    nx, ny, nz = sizes
    group = msg.group
    (extra_ref, extra_edges), rest = (rest[:2], rest[2:]) if msg.extra else ((None, None), rest)
    far, outs, spread = rest[:n_far], rest[n_far:-1], rest[-1]
    on = lax.broadcasted_iota(jnp.int32, (nx, nz), 1) % STRIDE == 0
    spread[pl.ds(0, LANES), :] = jnp.zeros((LANES, spread.shape[1]), jnp.float32)
    rows = [[None] * group for _ in range(FIELDS)]
    cells = sides([y_near[f] for f in range(FIELDS)], [y_far[f] for f in range(FIELDS)], "sect")
    for side, cell in enumerate(cells):
        beyond = flux_parts(cell, *derived(cell), 1)
        edge = [edge_ref[side, i] for i in range(len(beyond))]
        faces = face(edge, beyond) if side else [-a for a in face(beyond, edge)]
        for f, value in enumerate(faces):
            value = jnp.where(on, value, 0.0)
            for p in range(PIECES):
                piece = value.astype(jnp.bfloat16).astype(jnp.float32)
                value = value - piece
                for h in range(group):
                    moved = shift(piece, lane_of(side, p, h, group), 1)
                    rows[f][h] = moved if rows[f][h] is None else rows[f][h] + moved
    for f in range(FIELDS):
        for h in range(group):
            spread[pl.ds((FIELDS + f) * nx * group + h, nx, group), :] = rows[f][h]
    top = jnp.maximum(jnp.maximum(top_ref[...], y_near[FIELDS]), y_far[FIELDS])
    for ref in far:
        top = jnp.maximum(top, ref[...])
    top = jnp.broadcast_to(jnp.max(top, keepdims=True), top.shape)
    per = msg.count
    each = msg.owners // len(outs)
    picked = main_ref[...] + product(main_edges[...], spread[pl.ds(0, LANES), :].astype(jnp.bfloat16))
    for b in range(msg.owners):
        at = (b % each) // 2 * per + b % 2 * msg.rows
        outs[b // each][pl.ds(at, msg.rows), :] = picked[b * msg.rows : (b + 1) * msg.rows]
    if msg.extra:
        rows = msg.extra_rows
        values = spread[pl.ds(LANES, msg.extra * msg.part), :].astype(jnp.bfloat16)
        picked = extra_ref[...] + folded(msg, product(extra_edges[...], values))
        for b in range(msg.owners):
            at = (b % each) // 2 * per + 2 * msg.rows + b % 2 * rows
            outs[b // each][pl.ds(at, rows), :] = picked[b * rows : (b + 1) * rows]
    for out in outs:
        for d in range(each // 2):
            out[pl.ds((d + 1) * per - ROWS, ROWS), :] = top


def merge_kernel(msg, firsts, *refs):
    *refs, other_ref, own_ref = refs
    half, top = msg.owners // 2, None
    for first, ref in zip(firsts, refs):
        for d in range(ref.shape[0] // msg.count):
            at, to = d * msg.count, first + d
            for odd, out in ((0, own_ref), (1, other_ref)):
                out[pl.ds(to * msg.rows, msg.rows), :] = ref[pl.ds(at + odd * msg.rows, msg.rows), :]
                if msg.extra:
                    rows = msg.extra_rows
                    out[pl.ds(half * msg.rows + to * rows, rows), :] = ref[
                        pl.ds(at + 2 * msg.rows + odd * rows, rows), :
                    ]
            new = ref[pl.ds(at + msg.count - ROWS, ROWS), :]
            top = new if top is None else jnp.maximum(top, new)
    for out in (own_ref, other_ref):
        out[pl.ds(half * (msg.rows + msg.extra_rows), ROWS), :] = top


def hold_kernel(*refs):
    half = len(refs) // 2
    for ref, out in zip(refs[:half], refs[half:]):
        out[...] = ref[...]


def change_kernel(sizes, r_ref, v_ref, p_ref, x_low, x_high, y_near, y_far, out_ref, state_ref):
    nx, ny, nz = sizes
    every = range(FIELDS)
    y_low, y_high = sides([y_near[f] for f in every], [y_far[f] for f in every], "sect")
    row = lax.broadcasted_iota(jnp.int32, (ny, nz), 0)
    half = 0.5

    def layer(x):
        if x < 0:
            return [x_low[f] for f in range(FIELDS)]
        if x >= nx:
            return [x_high[f] for f in range(FIELDS)]
        return fields_of(r_ref, v_ref, p_ref, pl.ds(x * ny, ny))

    def prepared(x):
        cell = layer(x)
        state, sound = derived(cell)
        return cell, state, sound, flux_parts(cell, state, sound, 0)

    previous = prepared(-1)
    here = prepared(0)
    x_face = face(previous[3], here[3])
    for x in range(nx):
        following = prepared(x + 1)
        cell, state, sound, parts = here
        next_face = face(parts, following[3])
        total = [a - b for a, b in zip(next_face, x_face)]
        x_face = next_face
        low_cell = [y_low[f][x : x + 1] for f in range(FIELDS)]
        high_cell = [y_high[f][x : x + 1] for f in range(FIELDS)]
        low = flux_parts(low_cell, *derived(low_cell), 1)
        high = flux_parts(high_cell, *derived(high_cell), 1)
        parts = flux_parts(cell, state, sound, 1)
        plus = [jnp.where(row == ny - 1, h, shift(a, -1, 0)) for a, h in zip(parts, high)]
        after = face(parts, plus)
        edge = face(low, [a[0:1] for a in parts])
        before = [jnp.where(row == 0, e, shift(a, 1, 0)) for a, e in zip(after, edge)]
        total = [t + (a - b) for t, a, b in zip(total, after, before)]
        parts = flux_parts(cell, state, sound, 2)
        after = face(parts, [shift(a, -1, 1) for a in parts])
        total = [t + (a - shift(a, 1, 1)) for t, a in zip(total, after)]
        for f in range(FIELDS):
            out_ref[f, pl.ds(x * ny, ny), :] = half * total[f]
            state_ref[f, pl.ds(x * ny, ny), :] = state[f]
        here = following


def final_kernel(sizes, msg, direct, state_ref, change_ref, other_ref, own_ref, kept_ref, *rest):
    new_hbm, depth_hbm, new_ref, depth_ref, main_ref, extra_ref, sems = rest
    nx, ny, nz = sizes
    n_owner, group, part = msg.owners, msg.group, msg.part
    half, length = n_owner // 2, nx * n_owner
    at = pl.ds(half * (msg.rows + msg.extra_rows), ROWS)
    top = jnp.maximum(other_ref[at, :], own_ref[at, :])
    step = COURANT / top[0:1, 0:1]
    writes = []
    for x in range(nx):
        rows = pl.ds(x * ny, ny)
        for f in range(FIELDS):
            new_ref[f, rows, :] = state_ref[f, rows, :] - step * change_ref[f, rows, :]
        writes.append(pltpu.make_async_copy(new_ref.at[:, rows], new_hbm.at[:, rows], sems.at[x]))
        writes[-1].start()
    z_me, y_me = place_of(direct)

    def settle(source, at, extra_at, d, odd):
        owner = 2 * (d ^ z_me) + (odd ^ y_me)
        main_ref[owner] = source[pl.ds(at, msg.rows), :]
        if msg.extra:
            extra_ref[owner] = source[pl.ds(extra_at, msg.extra_rows), :]

    for d in range(half):
        extra_at = half * msg.rows + d * msg.extra_rows
        if direct and d == 0:
            settle(kept_ref, 0, 2 * msg.rows, 0, 0)
        else:
            settle(own_ref, d * msg.rows, extra_at, d, 0)
        settle(other_ref, d * msg.rows, extra_at, d, 1)
    line = []
    for f in range(msg.main):
        line.append(jnp.concatenate([main_ref[q, :, pl.ds(f * part, part)] for q in range(n_owner)], axis=1))
    for f in range(msg.extra):
        folds = []
        for a in range(msg.fold):
            at = pl.ds((a * msg.extra + f) * part, part)
            folds.append(jnp.concatenate([extra_ref[q, :, at] for q in range(n_owner)], axis=1))
        line.append(jnp.concatenate(folds, axis=0))
    cell, change = line[:FIELDS], line[FIELDS:]
    taken = cell[0] > 0.0
    cell[0] = jnp.where(taken, cell[0], 1.0)
    state, sound = derived(cell)
    parts = flux_parts(cell, state, sound, 0)
    after = face(parts, [shift(a, -group, 1) for a in parts])
    change = [c + (a - shift(a, group, 1)) for c, a in zip(change, after)]
    new = [s - (0.5 * step) * c for s, c in zip(state, change)]
    density = new[0]
    pressure = (GAMMA - 1.0) * (new[4] - 0.5 * (new[1] * new[1] + new[2] * new[2] + new[3] * new[3]) / density)
    broadening = TURBULENT + pressure / density
    inverse = 1.0 / (BAND / 64.0 * jnp.sqrt(broadening))
    amplitude = NORMALISE * (density * density) * jnp.exp(-0.7 * jnp.log(broadening)) * inverse
    amplitude = jnp.where(taken, amplitude, 0.0)
    scaled = inverse * math.sqrt(math.log2(math.e))
    centre = (BAND / 8.0) * (new[1] / density)
    turns = BAND // length
    block = min(length, UNROLL)

    def skewers(rows):
        scale, middle, size = scaled[:rows], centre[:rows], amplitude[:rows]
        strides = [scale * float(length * m) for m in range(turns)]

        def offsets(count, running):
            e = (length - block - block * count) * 1.0 - float(BAND // 2)
            for b in range(block):
                start = (e + float(b) - middle) * scale
                total = None
                for m in range(turns):
                    t = start + strides[m] if m else start
                    value = jnp.exp2(-(t * t))
                    total = value if total is None else total + value
                part = shift(size * total, b * group, 1)
                block_sum = part if b == 0 else block_sum + part
            return block_sum if running is None else shift(running, block * group, 1) + block_sum

        if length == block:
            running = offsets(0, None)
        else:
            running = lax.fori_loop(
                0,
                length // block,
                lambda i, c: offsets(i.astype(jnp.float32), c),
                jnp.zeros_like(size),
            )
        running = shift(running, -(BAND // 2) * group, 1)
        if group > 1:
            wide = jnp.broadcast_to(running[:, None, :], (rows, group, group * length))
            wide = wide.reshape(rows * group, group * length)
            at = lax.broadcasted_iota(jnp.int32, wide.shape, 1)
            of = lax.broadcasted_iota(jnp.int32, wide.shape, 0)
            wide = jnp.where(at % group == of % group, wide, 0.0)
            at = lax.broadcasted_iota(jnp.int32, (group * length, length), 0)
            of = lax.broadcasted_iota(jnp.int32, (group * length, length), 1)
            pick = jnp.where(at // group == of, 1.0, 0.0)
            pieces = []
            for _ in range(PIECES):
                pieces.append(wide.astype(jnp.bfloat16))
                wide = wide - pieces[-1].astype(jnp.float32)
            pick = jnp.concatenate([pick.astype(jnp.bfloat16)] * PIECES, axis=0)
            running = jnp.dot(jnp.concatenate(pieces, axis=1), pick, preferred_element_type=jnp.float32)
        depth_ref[pl.ds(0, rows * group), :] = running

    if msg.rows > ROWS:
        some = kept_ref if direct else own_ref
        more = jnp.max(some[pl.ds(ROWS, msg.rows - ROWS), pl.ds(0, part)]) > 0.0

        @pl.when(more)
        def _():
            skewers(msg.rows)

        @pl.when(jnp.logical_not(more))
        def _():
            depth_ref[...] = jnp.zeros_like(depth_ref)
            skewers(ROWS)

    else:
        skewers(msg.rows)
    writes.append(pltpu.make_async_copy(depth_ref, depth_hbm, sems.at[nx]))
    writes[-1].start()
    for write in writes:
        write.wait()


def around(value, axis, amount):
    count = lax.axis_size(axis)
    return lax.ppermute(value, axis, [(i, (i + amount) % count) for i in range(count)])


def to_partner(value, axis, bits):
    return lax.ppermute(value, axis, [(i, i ^ bits) for i in range(lax.axis_size(axis))])


def crossed(value, bits):
    count = lax.axis_size("slab")
    every = [(s, q) for s in range(lax.axis_size("sect")) for q in range(count)]
    pairs = [(s * count + q, (s ^ 1) * count + (q ^ bits)) for s, q in every]
    return lax.ppermute(value, ("sect", "slab"), pairs)


def to_other(value, axis):
    count = lax.axis_size(axis)
    return lax.ppermute(value, axis, [(i, (i + 2 * (i % 2) - 1) % count) for i in range(count)])


def body(density, velocity, pressure, owners):
    sizes = nx, ny, nz = density.shape
    n_sect, n_slab = lax.axis_size("sect"), lax.axis_size("slab")
    lines = nz // STRIDE
    columns = ny * lines
    slots = 2 * columns // n_slab
    length = nx * n_slab
    group = max(1, LANES // length)
    geometry = shape_of_message(nx, n_slab, slots, group)
    gas = (
        density.reshape(nx * ny, nz),
        velocity.reshape(3 * nx * ny, nz),
        pressure.reshape(nx * ny, nz),
    )
    cells = nx * ny * nz
    half = n_slab // 2
    direct = half <= 4
    x_edge, y_edge, row = (FIELDS, ny, nz), (FIELDS + 1, nx, nz), (ROWS, nz)
    owners = jnp.transpose(owners, (1, 2, 0))
    shapes = [(a.shape, a.dtype) for a in (*gas, owners)]
    x_first, x_last, y_near, y_far, top, *gas, owners = call(
        functools.partial(edges_kernel, sizes),
        [x_edge, x_edge, y_edge, (FIELDS, nx, nz), row, *shapes],
        "edges",
        20 * cells,
        [pltpu.SemaphoreType.DMA((4,))],
        in_specs=[HBM] * 4,
    )(*(pltpu.with_memory_space_constraint(a, pltpu.HBM) for a in (*gas, owners)))
    parts = (2, 2 * FIELDS + 1, nx, nz)
    spread, edge, target = call(
        functools.partial(prepare_kernel, sizes, geometry),
        [(group * spread_rows(geometry), columns), parts, (ROWS, columns)],
        "prepare",
        PREPARE_COST * cells,
    )(*gas, owners)
    y_near = to_partner(y_near, "sect", 1)
    y_far, target = call(join_kernel, [y_edge, (ROWS, columns)], "join", cells)(y_far, top, y_near, target)
    y_far = to_other(y_far, "sect")
    selected = [(n_slab * geometry.rows, LANES), (n_slab * geometry.rows, columns)]
    if geometry.extra:
        count = n_slab * geometry.extra_rows
        selected += [(count, LANES), (geometry.fold * count, columns)]
    selected = call(
        functools.partial(select_kernel, sizes, geometry, direct),
        selected,
        "select",
        SELECT_COST * cells,
    )(spread, target)
    far = [around(top, "sect", d) for d in range(2, n_sect - 1)] if n_sect > 4 else []
    x_low = around(x_last, "slab", 1)
    firsts = range(half) if direct else range(1)
    packed = call(
        functools.partial(pack_kernel, sizes, geometry, len(far)),
        [(half // len(firsts) * geometry.count, LANES)] * len(firsts),
        "pack",
        PACK_COST * cells,
        [pltpu.VMEM((spread_rows(geometry), columns), jnp.float32)],
    )(edge, y_near, y_far, top, *selected, *far)
    shapes = [a.shape for a in (x_low, x_first, packed[0])]
    x_low, x_first, first = call(hold_kernel, shapes, "hold", HOLD_COST * cells)(x_low, x_first, packed[0])
    x_high = around(x_first, "slab", -1)
    merge = functools.partial(
        call,
        out_shapes=[(half * (geometry.rows + geometry.extra_rows) + ROWS, LANES)] * 2,
        name="merge",
        flops=MERGE_COST * cells,
    )
    if direct:
        arrived = [crossed(m, 2 * d) for d, m in zip(firsts, [first, *packed[1:]])]
        turn = [2, 3, 1, 0] if half == 4 else list(firsts)
        other, own = merge(functools.partial(merge_kernel, geometry, turn))(*(arrived[d] for d in turn))
        other, own = crossed(other, 1), crossed(own, 0)
    else:
        alike = [[2 * i + odd for i in range(half)] for odd in range(2)]
        arrived = [
            lax.all_to_all(m, "slab", split_axis=0, concat_axis=0, axis_index_groups=alike, tiled=True) for m in packed
        ]
        other, own = merge(functools.partial(merge_kernel, geometry, firsts))(*arrived)
        other = to_partner(other, "slab", 1)
    change, state = call(
        functools.partial(change_kernel, sizes),
        [(FIELDS, nx * ny, nz)] * 2,
        "change",
        300_000 * cells,
    )(*gas, x_low, x_high, y_near, y_far)
    new_state, depth = call(
        functools.partial(final_kernel, sizes, geometry, direct),
        [(FIELDS, nx * ny, nz), (slots, length)],
        "final",
        100 * cells,
        [
            pltpu.VMEM((FIELDS, nx * ny, nz), jnp.float32),
            pltpu.VMEM((slots, length), jnp.float32),
            pltpu.VMEM((n_slab, geometry.rows, LANES), jnp.float32),
            pltpu.VMEM((n_slab, max(1, geometry.extra_rows), LANES), jnp.float32),
            pltpu.SemaphoreType.DMA((nx + 1,)),
        ],
        out_specs=[HBM, HBM],
    )(state, change, other, own, packed[0])
    return (new_state.reshape(FIELDS, nx, ny, nz), depth.reshape(1, 1, slots, length))


def solution(mesh):
    in_specs = (
        P("slab", "sect", None),
        P(None, "slab", "sect", None),
        P("slab", "sect", None),
        P("sect", None, None),
    )
    out_specs = (P(None, "slab", "sect", None), P("sect", "slab", None, None))
    return jax.shard_map(body, mesh=mesh, in_specs=in_specs, out_specs=out_specs, check_vma=False)
```
